256 devices in a mesh: lat: 16 (over y, x_hi, core), lon: 16 (over x_lo, z).
Axes of the slice: x: 4 (x_hi: 2, x_lo: 2; x = x_hi * 2 + x_lo), y: 4, z: 8, core: 2. Of those that a mesh axis runs over, the one named last changes fastest.
Arguments:
- adjoint_in: float32 [384, 768, 288], P('lat', 'lon'), may hold values from -6 to 6
- winds: float32 [384, 768, 144], P('lat', 'lon'), may hold values from -0.35 to 0.35
- vert_mix: float32 [72, 72], replicated
- level_weights: float32 [288], replicated, may hold values from 0.02 to 0.3
- snd_weights: bfloat16 [16, 16, 256, 16, 288], P('lat', 'lon'), may hold values from -6 to 6
- snd_columns: int32 [16, 16, 256, 16], P('lat', 'lon'), may hold values from 0 to 1151
- snd_counts: int32 [16, 16, 256], P('lat', 'lon'), may hold values from 8 to 16, as said below
- basis: float32 [384, 768, 256], P('lat', 'lon')
- owner: int32 [256], replicated, may hold values from 0 to 255, each once
Outputs:
- adjoint_out: float32 [384, 768, 288], P('lat', 'lon')
- grad_owned: float32 [256, 1, 4], P(('lat', 'lon'))
The draws below stay inside these ranges and needn't reach their ends.
Inputs may be any that keep to these rules, and one draw needn't show every extreme that they name: `snd_counts`: some destination device receives exactly 16 live slots from every device.
All inputs are finite; a program needn't handle non-finite values.
Results may differ from the reference program's by a relative error of at most 0.0003.
Values may be sent and summed in bfloat16 or wider, within the bound.
A program may use at most 128 MiB of HBM per device.

```python
import math
import jax
import jax.numpy as jnp
from jax import lax

TR = 4
LEV = 72
NB = 256
CLAT = 24
CLON = 48
CAP = 16
NLAT = 384
NLON = 768
BLK = 1
N_LAT = 16
N_LON = 16
DEVICES = 256


def draw_vert_mix(key, part):
    key = jax.random.fold_in(key, 2)
    spread = jax.random.uniform(key, (LEV, LEV), jnp.float32, 0.0, 0.9 / LEV)
    return spread + 0.55 * jnp.eye(LEV, dtype=jnp.float32)


def draw_snd_counts(key, part):
    key = jax.random.fold_in(key, 1)
    lat_blocks = NLAT // CLAT
    lon_blocks = NLON // CLON
    devices = lat_blocks * lon_blocks
    key_busy, key_count, key_full = jax.random.split(key, 3)
    busy = jax.random.randint(key_busy, (devices,), 0, 4) == 0
    lowest = jnp.where(busy, CAP, CAP // 2).astype(jnp.int32)
    counts = jax.random.randint(key_count, (lat_blocks, lon_blocks, devices), lowest[None, None, :], CAP + 1)
    full_dest = jax.random.randint(key_full, (), 0, devices)
    counts = jnp.where(jnp.arange(devices)[None, None, :] == full_dest, CAP, counts)
    return counts.astype(jnp.int32)


def draw_basis(key, part):
    key = jax.random.fold_in(key, 3)
    lon_blocks = NLON // CLON
    devices = NLAT // CLAT * lon_blocks
    key_back, key_home = jax.random.split(key)
    region = jnp.arange(NLAT)[:, None] // CLAT * lon_blocks + jnp.arange(NLON)[None, :] // CLON
    home = jnp.arange(NB) % devices
    inside = (region[:, :, None] == home[None, None, :]).astype(jnp.float32)
    background = 0.3 * jax.random.normal(key_back, (NLAT, NLON, NB), jnp.float32)
    regional = 4.0 * jax.random.normal(key_home, (NLAT, NLON, NB), jnp.float32)
    return background + inside * regional


def set_ends(result, stream_key, smallest, high):
    extent = result.shape
    spot = [jax.random.randint(jax.random.fold_in(stream_key, axis), (), 0, extent[axis]) for axis in range(len(extent))]
    result = result.at[tuple(spot)].set(smallest)
    longest = extent.index(max(extent))
    spot[longest] = (spot[longest] + 1) % extent[longest]
    return result.at[tuple(spot)].set(high)


def level_of(rng, extent, shards, least, high):
    loudness = 1.0
    for dim, parts in shards:
        steps = jax.random.uniform(jax.random.fold_in(jax.random.fold_in(rng, 6), dim), (parts,), jnp.float32, least / len(shards), high / len(shards))
        loudness = loudness * jnp.repeat(jnp.exp(steps), extent[dim] // parts).reshape((-1,) + (1,) * (len(extent) - 1 - dim))
    return loudness


def scatter_about(rng, extent, deviation, most, cuts=(), held_as=jnp.bfloat16):
    values = jax.random.normal(rng, extent, jnp.float32) * deviation
    if len(cuts) > 0:
        values = level_of(rng, extent, cuts, -0.22, 0.18) * values
    return jnp.clip(values, min=-most, max=most).astype(held_as)


def setup_inputs(seed: int = 0) -> dict:
    key_of = jax.random.split(jax.random.key(seed), 10)
    return {
        "adjoint_in": scatter_about(key_of[0], (NLAT, NLON, TR * LEV), 1.0, 6.0, ((0, 16), (1, 16)), jnp.float32),
        "winds": jnp.clip(jax.random.uniform(key_of[1], (NLAT, NLON, 2 * LEV), jnp.float32, -0.35, 0.35) * level_of(key_of[1], (NLAT, NLON, 2 * LEV), ((0, 16), (1, 16)), -0.4, 0.0), -0.35, 0.35),
        "vert_mix": draw_vert_mix(jax.random.fold_in(key_of[9], 71), 0),
        "level_weights": jnp.clip(jnp.exp(jax.random.uniform(key_of[3], (TR * LEV,), jnp.float32, math.log(0.02), math.log(0.3))), 0.02, 0.3),
        "snd_weights": scatter_about(key_of[4], (N_LAT, N_LON, DEVICES, CAP, TR * LEV), 1.0, 6.0, ((0, 16), (1, 16))),
        "snd_columns": set_ends(jax.random.randint(key_of[5], (N_LAT, N_LON, DEVICES, CAP), 0, CLAT * CLON), jax.random.fold_in(key_of[5], 1), 0, (CLAT * CLON) - 1).astype(jnp.int32),
        "snd_counts": draw_snd_counts(jax.random.fold_in(key_of[9], 71), 0),
        "basis": draw_basis(jax.random.fold_in(key_of[9], 71), 0),
        "owner": jax.random.permutation(key_of[8], DEVICES).astype(jnp.int32),
    }


diffusion = 0.05

def combine(center, east, west, north, south, winds, vert_mix):
    lat_rows, lon_cols, channels = center.shape
    levels = vert_mix.shape[0]
    tracers = channels // levels
    zonal_wind = winds[..., :levels][:, :, None, :]
    merid_wind = winds[..., levels:][:, :, None, :]

    def to_levels(value):
        return value.reshape(lat_rows, lon_cols, tracers, levels)
    middle = to_levels(center)
    advected = middle + (jnp.maximum(zonal_wind, 0.0) + diffusion) * (to_levels(east) - middle)
    advected = advected + (jnp.maximum(-zonal_wind, 0.0) + diffusion) * (to_levels(west) - middle)
    advected = advected + (jnp.maximum(merid_wind, 0.0) + diffusion) * (to_levels(north) - middle)
    advected = advected + (jnp.maximum(-merid_wind, 0.0) + diffusion) * (to_levels(south) - middle)
    vertical = jnp.einsum('abtl,lm->abtm', advected, vert_mix, precision=lax.Precision.HIGHEST)
    return vertical.reshape(lat_rows, lon_cols, channels)

def transport(field, winds, vert_mix):
    east = jnp.roll(field, -1, axis=1)
    west = jnp.roll(field, 1, axis=1)
    north = jnp.concatenate([field[1:], field[-1:]], axis=0)
    south = jnp.concatenate([field[:1], field[:-1]], axis=0)
    return combine(field, east, west, north, south, winds, vert_mix)

def reference(adjoint_in, winds, vert_mix, level_weights, snd_weights, snd_columns, snd_counts, basis, owner):
    lat_blocks = NLAT // CLAT
    lon_blocks = NLON // CLON
    devices = lat_blocks * lon_blocks
    channels = adjoint_in.shape[2]
    levels = vert_mix.shape[0]
    tracers = channels // levels
    dest = jnp.arange(devices, dtype=jnp.int32)
    dest_lat = dest // lon_blocks
    dest_lon = dest % lon_blocks
    slot_ids = jnp.arange(CAP, dtype=jnp.int32)

    def absorb(total, source):
        weights, columns, counts = source
        lat_index = dest_lat[:, None] * CLAT + columns // CLON
        lon_index = dest_lon[:, None] * CLON + columns % CLON
        flat_index = (lat_index * NLON + lon_index).astype(jnp.int32)
        live = slot_ids[None, :] < counts[:, None]
        values = jnp.where(live[..., None], weights.astype(jnp.float32), jnp.float32(0.0))
        total = total.at[flat_index.reshape(-1)].add(values.reshape(-1, channels))
        return (total, None)
    sources = (snd_weights.reshape(devices, devices, CAP, channels), snd_columns.reshape(devices, devices, CAP), snd_counts.reshape(devices, devices))
    injected, _ = lax.scan(absorb, jnp.zeros((NLAT * NLON, channels), jnp.float32), sources)
    state = adjoint_in + injected.reshape(NLAT, NLON, channels)
    state = transport(state, winds, vert_mix)
    state = transport(state, winds, vert_mix)
    sens = lax.optimization_barrier(jnp.sum(state.reshape(NLAT * NLON, tracers, levels) * level_weights.reshape(tracers, levels), axis=2))
    grad = jnp.dot(basis.reshape(NLAT * NLON, NB).T, sens, precision=lax.Precision.HIGHEST)
    grad = grad / jnp.sqrt(jnp.float32(NLAT * NLON))
    grad_owned = jnp.zeros((devices, BLK, tracers), jnp.float32).at[owner].set(grad.reshape(devices, BLK, tracers))
    return (state, grad_owned)
```

```python
import functools
import math

import jax
import jax.numpy as jnp
from jax import lax
from jax.experimental import pallas as pl
from jax.experimental.pallas import tpu as pltpu
from jax.sharding import PartitionSpec as P

diffusion = 0.05
MESH = pl.DeviceIdType.MESH
CELLS = 1152
CHUNK = 384
LAG = 3


def padded(array, sides, width):
    for axis, dim in sides:
        peers, length = (lax.axis_size(axis), array.shape[dim])
        up = [(i, (i + 1) % peers) for i in range(peers)]
        down = [(j, i) for i, j in up]
        last = lax.slice_in_dim(array, length - width, length, axis=dim)
        leading = lax.slice_in_dim(array, 0, width, axis=dim)
        before = lax.ppermute(last, axis, up)
        after = lax.ppermute(leading, axis, down)
        array = jnp.concatenate([before, array, after], axis=dim)
    return array


def combine(center, east, west, north, south, winds, vert_mix):
    lat_rows, lon_cols, channels = center.shape
    levels = vert_mix.shape[0]
    tracers = channels // levels
    zonal_wind = winds[..., :levels][:, :, None, :]
    merid_wind = winds[..., levels:][:, :, None, :]

    def to_levels(value):
        return value.reshape(lat_rows, lon_cols, tracers, levels)

    middle = to_levels(center)
    advected = middle + (jnp.maximum(zonal_wind, 0.0) + diffusion) * (to_levels(east) - middle)
    advected = advected + (jnp.maximum(-zonal_wind, 0.0) + diffusion) * (to_levels(west) - middle)
    advected = advected + (jnp.maximum(merid_wind, 0.0) + diffusion) * (to_levels(north) - middle)
    advected = advected + (jnp.maximum(-merid_wind, 0.0) + diffusion) * (to_levels(south) - middle)
    vertical = jnp.einsum("abtl,lm->abtm", advected, vert_mix, precision=lax.Precision.HIGHEST)
    return vertical.reshape(lat_rows, lon_cols, channels)


def advance(extended, winds, vert_mix):
    return combine(
        extended[1:-1, 1:-1],
        extended[1:-1, 2:],
        extended[1:-1, :-2],
        extended[2:, 1:-1],
        extended[:-2, 1:-1],
        winds,
        vert_mix,
    )


def fix_poles(extended, depth):
    position = lax.axis_index("lat")
    last_band = lax.axis_size("lat") - 1
    inner = extended.shape[0] - 2 * depth
    low_edge = extended[depth : depth + 1]
    high_edge = extended[depth + inner - 1 : depth + inner]
    low_part = jnp.where(position == 0, low_edge, extended[:depth])
    high_part = jnp.where(position == last_band, high_edge, extended[depth + inner :])
    return jnp.concatenate([low_part, extended[depth : depth + inner], high_part], axis=0)


def offsets(i):
    j = i - 31
    a_far, b_far = 1 + j // 15, 1 + j % 15
    lat_off = jnp.where(i < 16, i, jnp.where(i < 31, 0, a_far))
    lon_off = jnp.where(i < 16, 0, jnp.where(i < 31, i - 15, b_far))
    return lat_off, lon_off


def target(a, b, lat_off, lon_off):
    y, x_hi, core = a // 4, (a // 2) % 2, a % 2
    x_lo, z = b // 8, b % 8
    zi = lon_off // 2
    dz = jnp.where(zi % 2 == 1, (zi + 1) // 2, (8 - zi // 2) % 8)
    y = (y + lat_off // 4) % 4
    x_hi = (x_hi + (lat_off // 2) % 2) % 2
    core = (core + lat_off % 2) % 2
    z = (z + dz) % 8
    x_lo = (x_lo + lon_off % 2) % 2
    return (y * 2 + x_hi) * 2 + core, x_lo * 8 + z


def exchange_kernel(
    w, r, k, adj, out, recv, recr, reck, acc, stage, rhs, adj_v, pair_sem, ssem, rsem, lsem
):
    a = lax.axis_index("lat")
    b = lax.axis_index("lon")
    me = a * 16 + b
    bar = pltpu.get_barrier_semaphore()

    def greet(i, _):
        pl.semaphore_signal(bar, inc=1, device_id=((a + i) % 16, b), device_id_type=MESH)
        pl.semaphore_signal(bar, inc=1, device_id=(a, (b + i) % 16), device_id_type=MESH)
        return 0

    lax.fori_loop(1, 16, greet, 0)
    load = pltpu.make_async_copy(adj, adj_v, lsem.at[0])
    load.start()
    pltpu.make_async_copy(w.at[me, :, 0:256], recv.at[0], rsem.at[0, 0]).start()
    pltpu.make_async_copy(r.at[me], recr.at[0], rsem.at[1, 0]).start()
    pltpu.make_async_copy(k.at[me], reck.at[0], rsem.at[2, 0]).start()
    acc[...] = jnp.zeros_like(acc)
    pl.semaphore_wait(bar, 30)

    def ready(i, _):
        pl.semaphore_signal(pair_sem, inc=1, device_id=(a, (b + i) % 16), device_id_type=MESH)
        return 0

    lax.fori_loop(1, 16, ready, 0)

    def send(i, _):
        ta, tb = target(a, b, *offsets(i))
        d = ta * 16 + tb
        g = i // 16
        for n, (src, dst) in enumerate(
            ((w.at[d, :, 0:256], recv.at[i]), (r.at[d], recr.at[i]), (k.at[d], reck.at[i]))
        ):
            pltpu.make_async_remote_copy(
                src_ref=src,
                dst_ref=dst,
                send_sem=ssem.at[n],
                recv_sem=rsem.at[n, g],
                device_id=(ta, tb),
                device_id_type=MESH,
            ).start()
        return 0

    lax.fori_loop(1, 31, send, 0)
    pl.semaphore_wait(pair_sem, 15)

    rows = lax.broadcasted_iota(jnp.int32, (256, 64), 0)
    cols = lax.broadcasted_iota(jnp.int32, (256, 64), 1)
    spread = ((rows // 16 == cols // 4) & (rows % 4 == cols % 4)).astype(jnp.bfloat16)
    rows = lax.broadcasted_iota(jnp.int32, (256, 128), 0)
    lanes = lax.broadcasted_iota(jnp.int32, (256, 128), 1)
    keep = ((rows // 4) % 4 == lanes // 32).astype(jnp.float32)

    def absorb(g):
        first = g * 16
        for n, buf in enumerate((recv, recr, reck)):
            part = buf.at[pl.ds(first, 16)]
            pltpu.make_async_copy(part, part, rsem.at[n, g]).wait()
        rhs[:, 0:256] = recv[pl.ds(first, 16)].reshape(256, 256)
        for m in range(16):
            stage[4 * m : 4 * m + 4, :] = recr[first + m].astype(jnp.float32)
        packed = stage[...].astype(jnp.bfloat16)
        wide = jnp.dot(spread, packed, preferred_element_type=jnp.float32) * keep
        rhs[:, 256:384] = wide.astype(jnp.bfloat16)
        low = reck[first]
        high = reck[first + 8]
        for m in range(1, 8):
            low = low + reck[first + m]
            high = high + reck[first + 8 + m]
        where = jnp.concatenate([low, high], axis=1)
        for c in range(CELLS // CHUNK):
            ids = lax.broadcasted_iota(jnp.int32, (CHUNK, 256), 0) + c * CHUNK
            table = jnp.where(ids == where, 1.0, 0.0).astype(jnp.bfloat16)
            span = slice(c * CHUNK, (c + 1) * CHUNK)
            acc[span, :] += jnp.dot(table, rhs[...], preferred_element_type=jnp.float32)

    def turn(c, _):
        @pl.when(c < 15)
        def _():
            lax.fori_loop(31 + c * 15, 46 + c * 15, send, 0)

        @pl.when(c >= LAG)
        def _():
            absorb(c - LAG)

        return 0

    lax.fori_loop(0, 16 + LAG, turn, 0)
    load.wait()
    out[:, 0:256] = adj_v[:, 0:256] + acc[:, 0:256]
    tail = acc[:, 256:288] + acc[:, 288:320] + acc[:, 320:352] + acc[:, 352:384]
    out[:, 256:288] = adj_v[:, 256:288] + tail
    for n, buf in enumerate((recv, recr, reck)):
        part = buf.at[pl.ds(1, 255)]
        pltpu.make_async_copy(part, part, ssem.at[n]).wait()


def exchange(adjoint, weights, columns, counts):
    channels = adjoint.shape[-1]
    w = weights[0, 0]
    live = lax.broadcasted_iota(jnp.int32, (256, 16), 1) < counts[0, 0][:, None]
    where = jnp.where(live, columns[0, 0], -1)
    r = w[:, :, 256:].reshape(256, 4, 4, 32).transpose(0, 2, 1, 3).reshape(256, 4, 128)
    a, b = lax.axis_index("lat"), lax.axis_index("lon")
    dest = lax.broadcasted_iota(jnp.int32, (256, 128), 0)
    lane = lax.broadcasted_iota(jnp.int32, (256, 128), 1)
    ta, tb = dest // 16, dest % 16
    y = (ta // 4 - a // 4 + 4) % 4
    x_hi = ((ta // 2) % 2 + (a // 2) % 2) % 2
    core = (ta % 2 + a % 2) % 2
    lat_off = (y * 2 + x_hi) * 2 + core
    dz = (tb % 8 - b % 8 + 8) % 8
    zi = jnp.where(dz == 0, 0, jnp.where(dz <= 4, 2 * dz - 1, 2 * (8 - dz)))
    lon_off = zi * 2 + (tb // 8 + b // 8) % 2
    step = jnp.where(
        lon_off == 0,
        lat_off,
        jnp.where(lat_off == 0, 15 + lon_off, 31 + (lat_off - 1) * 15 + lon_off - 1),
    )
    spot = jnp.where(step % 8 == lane // 16, jnp.tile(where, (1, 8)), 0)
    k = spot.reshape(256, 1, 128)
    return pl.pallas_call(
        exchange_kernel,
        out_shape=jax.ShapeDtypeStruct((CELLS, channels), jnp.float32),
        in_specs=[pl.BlockSpec(memory_space=pl.ANY)] * 4,
        out_specs=pl.BlockSpec(memory_space=pltpu.VMEM),
        scratch_shapes=[
            pltpu.VMEM((256, 16, 256), jnp.bfloat16),
            pltpu.VMEM((256, 4, 128), jnp.bfloat16),
            pltpu.VMEM((256, 1, 128), jnp.int32),
            pltpu.VMEM((CELLS, 384), jnp.float32),
            pltpu.VMEM((64, 128), jnp.float32),
            pltpu.VMEM((256, 384), jnp.bfloat16),
            pltpu.VMEM((CELLS, channels), jnp.float32),
            pltpu.SemaphoreType.REGULAR,
            pltpu.SemaphoreType.DMA((3,)),
            pltpu.SemaphoreType.DMA((3, 16)),
            pltpu.SemaphoreType.DMA((1,)),
        ],
        compiler_params=pltpu.CompilerParams(
            collective_id=0, has_side_effects=True, vmem_limit_bytes=40 << 20
        ),
        name="exchange",
    )(w, r, k, adjoint.reshape(CELLS, channels))


def body(
    adjoint_in, winds, vert_mix, level_weights, snd_weights, snd_columns, snd_counts, basis, owner
):
    lat_cells, lon_cells, channels = adjoint_in.shape
    levels = vert_mix.shape[0]
    tracers = channels // levels
    devices = lax.axis_size("lat") * lax.axis_size("lon")
    cells = lat_cells * lon_cells
    state = exchange(adjoint_in, snd_weights, snd_columns, snd_counts)
    state = state.reshape(lat_cells, lon_cells, channels)

    def rim_step(current):
        extended = padded(current, (("lat", 0), ("lon", 1)), 1)
        return advance(fix_poles(extended, 1), winds, vert_mix)

    state = rim_step(rim_step(state))
    sens = jnp.sum(
        state.reshape(cells, tracers, levels) * level_weights.reshape(tracers, levels), axis=2
    )
    patterns = basis.shape[2]
    partial_grad = lax.dot_general(
        basis.reshape(cells, patterns),
        sens,
        (((0,), (0,)), ((), ())),
        precision=lax.Precision.HIGHEST,
        preferred_element_type=jnp.float32,
    )
    block_size = patterns // devices
    select = (owner[:, None] == lax.broadcasted_iota(jnp.int32, (1, devices), 1)).astype(
        jnp.float32
    )
    ordered = jnp.einsum(
        "bd,bjt->djt",
        select,
        partial_grad.reshape(devices, block_size, tracers),
        precision=lax.Precision.HIGHEST,
    )
    owned = lax.psum_scatter(ordered, ("lat", "lon"), scatter_dimension=0, tiled=True)
    owned = owned / jnp.sqrt(jnp.float32(cells * devices))
    return (state, owned)


def solution(mesh):
    return jax.shard_map(
        body,
        mesh=mesh,
        in_specs=(
            P("lat", "lon", None),
            P("lat", "lon", None),
            P(),
            P(),
            P("lat", "lon", None, None, None),
            P("lat", "lon", None, None),
            P("lat", "lon", None),
            P("lat", "lon", None),
            P(),
        ),
        out_specs=(P("lat", "lon", None), P(("lat", "lon"), None, None)),
        check_vma=False,
    )
```

```python
import jax
import jax.numpy as jnp
from jax import lax
from jax.experimental import pallas as pl
from jax.experimental.pallas import tpu as pltpu
from jax.sharding import PartitionSpec as P

diffusion = 0.05
MESH = pl.DeviceIdType.MESH
BF16 = jnp.bfloat16
F32 = jnp.float32
DEVICES = 256
SIDE = 16
SLOTS = 16
CLAT, CLON = 24, 48
CELLS = CLAT * CLON
CHAN = 288
WIDE = 384
LEV = 72
TRACERS = 4
CHUNK = 384
EAGER = 91
LAG = 2
ROWS = 4


def offsets(i):
    j = i - 31
    lat_off = jnp.where(i < 16, i, jnp.where(i < 31, 0, 1 + j // 15))
    lon_off = jnp.where(i < 16, 0, jnp.where(i < 31, i - 15, 1 + j % 15))
    return lat_off, lon_off


def target(a, b, lat_off, lon_off):
    y, x_hi, core = a // 4, (a // 2) % 2, a % 2
    x_lo, z = b // 8, b % 8
    zi = lon_off // 2
    dz = jnp.where(zi % 2 == 1, (zi + 1) // 2, (8 - zi // 2) % 8)
    y = (y + lat_off // 4) % 4
    x_hi = (x_hi + (lat_off // 2) % 2) % 2
    core = (core + lat_off % 2) % 2
    z = (z + dz) % 8
    x_lo = (x_lo + lon_off % 2) % 2
    return (y * 2 + x_hi) * 2 + core, x_lo * 8 + z


def step_of(a, b, dest):
    ta, tb = dest // 16, dest % 16
    y = (ta // 4 - a // 4 + 4) % 4
    x_hi = ((ta // 2) % 2 + (a // 2) % 2) % 2
    core = (ta % 2 + a % 2) % 2
    lat_off = (y * 2 + x_hi) * 2 + core
    dz = (tb % 8 - b % 8 + 8) % 8
    zi = jnp.where(dz == 0, 0, jnp.where(dz <= 4, 2 * dz - 1, 2 * (8 - dz)))
    lon_off = zi * 2 + (tb // 8 + b // 8) % 2
    far = 31 + (lat_off - 1) * 15 + lon_off - 1
    return jnp.where(lon_off == 0, lat_off, jnp.where(lat_off == 0, 15 + lon_off, far))


def iota(shape, dim):
    return lax.broadcasted_iota(jnp.int32, shape, dim)


def split(value):
    high = value.astype(BF16)
    return high, (value - high.astype(F32)).astype(BF16)


def dot(x, y):
    return jnp.dot(x, y, preferred_element_type=F32)


def window_kernel(
    adj, winds, mix, lweights, w, columns, counts, basis, owner,
    out, grad,
    w_v, f0, f1, fr, wbuf, rbuf, kbuf, recv, recr, reck, acc, stage, rhs,
    adj_v, winds_v, coef, basis_v, base_hi, base_lo, mat, mat_hi, mat_lo,
    cur, nxt, col_out, col_in, mh, ml, sens, part, part_in, total, total_in,
    pair_sem, ssem, rsem, lsem, hs_sem, hr_sem, gs_sem, gr_sem,
):
    a = lax.axis_index("lat")
    b = lax.axis_index("lon")
    me = a * SIDE + b
    bar = pltpu.get_barrier_semaphore()

    def greet(i, _):
        pl.semaphore_signal(bar, inc=1, device_id=((a + i) % SIDE, b), device_id_type=MESH)
        pl.semaphore_signal(bar, inc=1, device_id=(a, (b + i) % SIDE), device_id_type=MESH)
        return 0

    lax.fori_loop(1, SIDE, greet, 0)
    loads = [
        pltpu.make_async_copy(w.at[pl.ds(4 * q, 4)], w_v.at[pl.ds(4 * q, 4)], lsem.at[q])
        for q in range(4)
    ]
    loads.append(pltpu.make_async_copy(adj, adj_v, lsem.at[4]))
    loads.append(pltpu.make_async_copy(winds, winds_v, lsem.at[5]))
    loads.append(pltpu.make_async_copy(basis, basis_v, lsem.at[6]))
    for load in loads:
        load.start()

    slot = iota((SLOTS, DEVICES), 0)
    where = jnp.where(slot < counts[...], columns[...], -1)
    step = step_of(a, b, iota((1, DEVICES), 1))
    placed = jnp.where(iota((128, DEVICES), 0) // SLOTS == step % 8, jnp.concatenate([where] * 8, axis=0), 0)
    for h in range(2):
        kbuf[pl.ds(128 * h, 128), 0, :] = placed[:, 128 * h : 128 * h + 128].T

    for q in range(4):
        loads[q].wait()

        def turn_slot(s, _):
            for h in range(2):
                for c, dst in ((0, f0), (1, f1)):
                    block = w_v[s, 128 * c : 128 * c + 128, 128 * h : 128 * h + 128]
                    dst[pl.ds(2048 * h + s, 128, stride=SLOTS), :] = block.astype(F32).T
            return 0

        lax.fori_loop(4 * q, 4 * q + 4, turn_slot, 0)

    def turn_rest(r, _):
        for h in range(2):
            pieces = [w_v[4 * g + r, 256:288, 128 * h : 128 * h + 128] for g in range(4)]
            block = jnp.concatenate([p.astype(F32) for p in pieces], axis=0)
            fr[pl.ds(512 * h + r, 128, stride=4), :] = block.T
        return 0

    lax.fori_loop(0, 4, turn_rest, 0)

    def pack(d, _):
        n = 8 * d
        rows = pl.ds(pl.multiple_of(SLOTS * n, 128), 128)
        wbuf[pl.ds(n, 8), :, 0:128] = f0[rows, :].astype(BF16).reshape(8, SLOTS, 128)
        wbuf[pl.ds(n, 8), :, 128:256] = f1[rows, :].astype(BF16).reshape(8, SLOTS, 128)
        four = fr[pl.ds(pl.multiple_of(4 * n, 32), 32), :]
        for m in range(8):
            rbuf[n + m] = four[4 * m : 4 * m + 4, :].astype(BF16)
        return 0

    lax.fori_loop(0, DEVICES // 8, pack, 0)

    pl.semaphore_wait(bar, 2 * (SIDE - 1))

    def ready(i, _):
        pl.semaphore_signal(pair_sem, inc=1, device_id=(a, (b + i) % SIDE), device_id_type=MESH)
        return 0

    lax.fori_loop(1, SIDE, ready, 0)

    own = [
        pltpu.make_async_copy(wbuf.at[me], recv.at[0], rsem.at[0, 0]),
        pltpu.make_async_copy(rbuf.at[me], recr.at[0], rsem.at[1, 0]),
        pltpu.make_async_copy(kbuf.at[me], reck.at[0], rsem.at[2, 0]),
    ]
    for copy in own:
        copy.start()

    def send(i, _):
        ta, tb = target(a, b, *offsets(i))
        d = ta * SIDE + tb
        for n, (src, dst) in enumerate(((wbuf, recv), (rbuf, recr), (kbuf, reck))):
            pltpu.make_async_remote_copy(
                src_ref=src.at[d],
                dst_ref=dst.at[i],
                send_sem=ssem.at[n],
                recv_sem=rsem.at[n, i // 16],
                device_id=(ta, tb),
                device_id_type=MESH,
            ).start()
        return 0

    lax.fori_loop(1, 31, send, 0)
    pl.semaphore_wait(pair_sem, SIDE - 1)
    lax.fori_loop(31, EAGER, send, 0)

    mat[...] = jnp.zeros_like(mat)
    for t in range(TRACERS):
        mat[LEV * t : LEV * t + LEV, LEV * t : LEV * t + LEV] = mix[...]
    gain = jnp.sum(mat[:, 0:CHAN] * lweights[...], axis=1, keepdims=True)
    extra = iota((CHAN, WIDE - CHAN), 0) // LEV == iota((CHAN, WIDE - CHAN), 1)
    mat[:, CHAN:WIDE] = jnp.where(extra, gain, 0.0)
    mat_hi[...], mat_lo[...] = split(mat[...])

    loads[6].wait()
    pick = jnp.where(iota((DEVICES, DEVICES), 0) == owner[...], 1.0, 0.0).astype(BF16)
    for c in range(CELLS // 128):
        for piece, dst in zip(split(basis_v[128 * c : 128 * c + 128, :]), (base_hi, base_lo)):
            turned = lax.dot_general(pick, piece, (((1,), (1,)), ((), ())), preferred_element_type=F32)
            dst[:, 128 * c : 128 * c + 128] = turned.astype(BF16)

    loads[4].wait()
    loads[5].wait()
    acc[:, 0:CHAN] = adj_v[...]
    acc[:, CHAN:WIDE] = jnp.zeros((CELLS, WIDE - CHAN), F32)

    def coefficients(r):
        span = pl.ds(pl.multiple_of(r * CLON, CLON), CLON)
        both = winds_v[span, :]
        u = jnp.concatenate([both[:, 0:LEV]] * TRACERS, axis=1)
        v = jnp.concatenate([both[:, LEV : 2 * LEV]] * TRACERS, axis=1)
        east = jnp.maximum(u, 0.0) + diffusion
        west = jnp.maximum(-u, 0.0) + diffusion
        north = jnp.maximum(v, 0.0) + diffusion
        south = jnp.maximum(-v, 0.0) + diffusion
        coef[0, span, :] = 1.0 - ((east + west) + (north + south))
        coef[1, span, :] = east
        coef[2, span, :] = west
        coef[3, span, :] = north
        coef[4, span, :] = south

    rows = iota((DEVICES, 64), 0)
    lanes = iota((DEVICES, 64), 1)
    spread = jnp.where((rows // 16 == lanes // 4) & (rows % 4 == lanes % 4), 1.0, 0.0).astype(BF16)
    rows = iota((DEVICES, 128), 0)
    lanes = iota((DEVICES, 128), 1)
    keep = jnp.where((rows // 4) % 4 == lanes // 32, 1.0, 0.0)

    def absorb(g):
        first = g * 16
        for n, buf in enumerate((recv, recr, reck)):
            piece = buf.at[pl.ds(first, 16)]
            pltpu.make_async_copy(piece, piece, rsem.at[n, g]).wait()
        rhs[:, 0:256] = recv[pl.ds(first, 16)].reshape(256, 256)
        for m in range(16):
            stage[4 * m : 4 * m + 4, :] = recr[first + m].astype(F32)
        rhs[:, 256:384] = (dot(spread, stage[...].astype(BF16)) * keep).astype(BF16)
        low = reck[first]
        high = reck[first + 8]
        for m in range(1, 8):
            low = low + reck[first + m]
            high = high + reck[first + 8 + m]
        spot = jnp.concatenate([low, high], axis=1)
        for c in range(CELLS // CHUNK):
            table = jnp.where(iota((CHUNK, 256), 0) + c * CHUNK == spot, 1.0, 0.0).astype(BF16)
            acc[c * CHUNK : (c + 1) * CHUNK, :] += dot(table, rhs[...])

    chunks = (DEVICES - EAGER) // 15

    def turn(c, _):
        @pl.when(c < chunks)
        def _():
            lax.fori_loop(EAGER + c * 15, EAGER + 15 + c * 15, send, 0)

        @pl.when(c < 12)
        def _():
            coefficients(2 * c)
            coefficients(2 * c + 1)

        @pl.when(c >= LAG)
        def _():
            absorb(c - LAG)

        return 0

    lax.fori_loop(0, 16 + LAG, turn, 0)

    def first_state(r, _):
        span = pl.ds(pl.multiple_of(r * CLON, CLON), CLON)
        row = acc[span, :]
        cur[r + 1, 8:56, 0:256] = row[:, 0:256]
        cur[r + 1, 8:56, 256:288] = (row[:, 256:288] + row[:, 288:320]) + (row[:, 320:352] + row[:, 352:384])
        return 0

    lax.fori_loop(0, CLAT, first_state, 0)

    def copy_to(src, dst, send_sem, recv_sem, ta, tb):
        return pltpu.make_async_remote_copy(
            src_ref=src, dst_ref=dst, send_sem=send_sem, recv_sem=recv_sem, device_id=(ta, tb), device_id_type=MESH
        )

    def halo(buf, e):
        north = copy_to(buf.at[CLAT, 8:56, :], buf.at[0, 8:56, :], hs_sem.at[e, 0], hr_sem.at[e, 0], (a + 1) % SIDE, b)
        south = copy_to(buf.at[1, 8:56, :], buf.at[CLAT + 1, 8:56, :], hs_sem.at[e, 1], hr_sem.at[e, 1], (a + SIDE - 1) % SIDE, b)
        east = copy_to(col_out.at[e, 0], col_in.at[e, 0], hs_sem.at[e, 2], hr_sem.at[e, 2], a, (b + 1) % SIDE)
        west = copy_to(col_out.at[e, 1], col_in.at[e, 1], hs_sem.at[e, 3], hr_sem.at[e, 3], a, (b + SIDE - 1) % SIDE)

        @pl.when(a < SIDE - 1)
        def _():
            north.start()

        @pl.when(a > 0)
        def _():
            south.start()

        col_out[e, 0] = buf[1 : CLAT + 1, 55, :]
        east.start()
        col_out[e, 1] = buf[1 : CLAT + 1, 8, :]
        west.start()

        @pl.when(a > 0)
        def _():
            north.wait_recv()

        @pl.when(a == 0)
        def _():
            buf[0, 8:56, :] = buf[1, 8:56, :]

        @pl.when(a < SIDE - 1)
        def _():
            south.wait_recv()

        @pl.when(a == SIDE - 1)
        def _():
            buf[CLAT + 1, 8:56, :] = buf[CLAT, 8:56, :]

        east.wait_recv()
        buf[1 : CLAT + 1, 7, :] = col_in[e, 0]
        west.wait_recv()
        buf[1 : CLAT + 1, 56, :] = col_in[e, 1]
        return north, south, east, west

    def finish(copies):
        north, south, east, west = copies

        @pl.when(a < SIDE - 1)
        def _():
            north.wait_send()

        @pl.when(a > 0)
        def _():
            south.wait_send()

        east.wait_send()
        west.wait_send()

    def advect(buf, c):
        for k in range(ROWS):
            r = c * ROWS + k
            span = pl.ds(pl.multiple_of(r * CLON, CLON), CLON)
            m = coef[0, span, :] * buf[r + 1, 8:56, 0:CHAN]
            m = m + coef[1, span, :] * buf[r + 1, 9:57, 0:CHAN]
            m = m + coef[2, span, :] * buf[r + 1, 7:55, 0:CHAN]
            m = m + coef[3, span, :] * buf[r + 2, 8:56, 0:CHAN]
            m = m + coef[4, span, :] * buf[r, 8:56, 0:CHAN]
            mh[k * CLON : (k + 1) * CLON, :], ml[k * CLON : (k + 1) * CLON, :] = split(m)

    def step_one(c, _):
        advect(cur, c)
        res = dot(mh[...], mat_hi[:, 0:CHAN]) + dot(ml[...], mat_hi[:, 0:CHAN]) + dot(mh[...], mat_lo[:, 0:CHAN])
        nxt[pl.ds(c * ROWS + 1, ROWS), 8:56, 0:CHAN] = res.reshape(ROWS, CLON, CHAN)
        return 0

    def step_two(c, _):
        advect(nxt, c)
        res = dot(mh[...], mat_hi[...]) + dot(ml[...], mat_hi[...]) + dot(mh[...], mat_lo[...])
        out[pl.ds(c * ROWS, ROWS), :, :] = res[:, 0:CHAN].reshape(ROWS, CLON, CHAN)
        sens[pl.ds(pl.multiple_of(c * ROWS * CLON, ROWS * CLON), ROWS * CLON), :] = res[:, 256:WIDE]
        return 0

    one = halo(cur, 0)
    lax.fori_loop(0, CLAT // ROWS, step_one, 0)
    two = halo(nxt, 1)
    lax.fori_loop(0, CLAT // ROWS, step_two, 0)

    sens_hi, sens_lo = split(sens[...])
    part[...] = dot(base_hi[...], sens_hi) + dot(base_lo[...], sens_hi) + dot(base_hi[...], sens_lo)

    def give_lat(i, _):
        ta = (a + i) % SIDE
        src = part.at[pl.ds(pl.multiple_of(ta * SIDE, SIDE), SIDE)]
        copy_to(src, part_in.at[i], gs_sem.at[0], gr_sem.at[0], ta, b).start()
        return 0

    lax.fori_loop(1, SIDE, give_lat, 0)
    got = part[pl.ds(pl.multiple_of(a * SIDE, SIDE), SIDE), :]
    waiting = part_in.at[pl.ds(1, SIDE - 1)]
    pltpu.make_async_copy(waiting, waiting, gr_sem.at[0]).wait()
    for i in range(1, SIDE):
        got = got + part_in[i]
    total[...] = got

    def give_lon(i, _):
        tb = (b + i) % SIDE
        src = total.at[pl.ds(pl.multiple_of(tb // 8 * 8, 8), 8)]
        copy_to(src, total_in.at[i], gs_sem.at[1], gr_sem.at[1], a, tb).start()
        return 0

    lax.fori_loop(1, SIDE, give_lon, 0)
    mine = total[pl.ds(pl.multiple_of(b // 8 * 8, 8), 8), :]
    landed = total_in.at[pl.ds(1, SIDE - 1)]
    pltpu.make_async_copy(landed, landed, gr_sem.at[1]).wait()
    for i in range(1, SIDE):
        mine = mine + total_in[i]
    row = jnp.sum(jnp.where(iota((8, 128), 0) == b % 8, mine, 0.0), axis=0, keepdims=True)
    scale = 1.0 / jnp.sqrt(jnp.full((1, TRACERS), CELLS * DEVICES, F32))
    grad[...] = row[:, 32 : 32 + TRACERS] * scale

    finish(one)
    finish(two)
    pltpu.make_async_copy(waiting, waiting, gs_sem.at[0]).wait()
    pltpu.make_async_copy(landed, landed, gs_sem.at[1]).wait()
    for n, buf in enumerate((recv, recr, reck)):
        piece = buf.at[pl.ds(1, DEVICES - 1)]
        pltpu.make_async_copy(piece, piece, ssem.at[n]).wait()


def body(
    adjoint_in, winds, vert_mix, level_weights, snd_weights, snd_columns, snd_counts, basis, owner
):
    anywhere = pl.BlockSpec(memory_space=pl.ANY)
    vmem = pl.BlockSpec(memory_space=pltpu.VMEM)
    state, grad = pl.pallas_call(
        window_kernel,
        out_shape=(
            jax.ShapeDtypeStruct((CLAT, CLON, CHAN), F32),
            jax.ShapeDtypeStruct((1, TRACERS), F32),
        ),
        in_specs=[anywhere, anywhere, vmem, vmem, anywhere, vmem, vmem, anywhere, vmem],
        out_specs=(vmem, vmem),
        scratch_shapes=[
            pltpu.VMEM((SLOTS, CHAN, DEVICES), BF16),
            pltpu.VMEM((DEVICES * SLOTS, 128), F32),
            pltpu.VMEM((DEVICES * SLOTS, 128), F32),
            pltpu.VMEM((DEVICES * 4, 128), F32),
            pltpu.VMEM((DEVICES, SLOTS, 256), BF16),
            pltpu.VMEM((DEVICES, 4, 128), BF16),
            pltpu.VMEM((DEVICES, 1, 128), jnp.int32),
            pltpu.VMEM((DEVICES, SLOTS, 256), BF16),
            pltpu.VMEM((DEVICES, 4, 128), BF16),
            pltpu.VMEM((DEVICES, 1, 128), jnp.int32),
            pltpu.VMEM((CELLS, WIDE), F32),
            pltpu.VMEM((64, 128), F32),
            pltpu.VMEM((256, WIDE), BF16),
            pltpu.VMEM((CELLS, CHAN), F32),
            pltpu.VMEM((CELLS, 2 * LEV), F32),
            pltpu.VMEM((5, CELLS, CHAN), F32),
            pltpu.VMEM((CELLS, DEVICES), F32),
            pltpu.VMEM((DEVICES, CELLS), BF16),
            pltpu.VMEM((DEVICES, CELLS), BF16),
            pltpu.VMEM((CHAN, WIDE), F32),
            pltpu.VMEM((CHAN, WIDE), BF16),
            pltpu.VMEM((CHAN, WIDE), BF16),
            pltpu.VMEM((CLAT + 2, 64, WIDE), F32),
            pltpu.VMEM((CLAT + 2, 64, WIDE), F32),
            pltpu.VMEM((2, 2, CLAT, WIDE), F32),
            pltpu.VMEM((2, 2, CLAT, WIDE), F32),
            pltpu.VMEM((ROWS * CLON, CHAN), BF16),
            pltpu.VMEM((ROWS * CLON, CHAN), BF16),
            pltpu.VMEM((CELLS, 128), F32),
            pltpu.VMEM((DEVICES, 128), F32),
            pltpu.VMEM((SIDE, SIDE, 128), F32),
            pltpu.VMEM((SIDE, 128), F32),
            pltpu.VMEM((SIDE, 8, 128), F32),
            pltpu.SemaphoreType.REGULAR,
            pltpu.SemaphoreType.DMA((3,)),
            pltpu.SemaphoreType.DMA((3, 16)),
            pltpu.SemaphoreType.DMA((7,)),
            pltpu.SemaphoreType.DMA((2, 4)),
            pltpu.SemaphoreType.DMA((2, 4)),
            pltpu.SemaphoreType.DMA((2,)),
            pltpu.SemaphoreType.DMA((2,)),
        ],
        compiler_params=pltpu.CompilerParams(
            collective_id=0, has_side_effects=True, vmem_limit_bytes=56 << 20
        ),
        name="window",
    )(
        adjoint_in.reshape(CELLS, CHAN),
        winds.reshape(CELLS, 2 * LEV),
        vert_mix,
        level_weights.reshape(1, CHAN),
        jnp.transpose(snd_weights[0, 0], (1, 2, 0)),
        jnp.transpose(snd_columns[0, 0], (1, 0)),
        snd_counts[0],
        basis.reshape(CELLS, DEVICES),
        owner.reshape(1, DEVICES),
    )
    return state, grad.reshape(1, 1, TRACERS)


def solution(mesh):
    return jax.shard_map(
        body,
        mesh=mesh,
        in_specs=(
            P("lat", "lon", None),
            P("lat", "lon", None),
            P(),
            P(),
            P("lat", "lon", None, None, None),
            P("lat", "lon", None, None),
            P("lat", "lon", None),
            P("lat", "lon", None),
            P(),
        ),
        out_specs=(P("lat", "lon", None), P(("lat", "lon"), None, None)),
        check_vma=False,
    )
```

```python
import jax
import jax.numpy as jnp
from jax import lax
from jax.experimental import pallas as pl
from jax.experimental.pallas import tpu as pltpu
from jax.sharding import PartitionSpec as P

diffusion = 0.05
MESH = pl.DeviceIdType.MESH
BF16 = jnp.bfloat16
F32 = jnp.float32
DEVICES = 256
SIDE = 16
SLOTS = 16
CLAT, CLON = 24, 48
CELLS = CLAT * CLON
CHAN = 288
WIDE = 384
LEV = 72
TRACERS = 4
BAND = 8
LAG = 2
ROWS = 11
RIM = 2 * CLAT + 2 * CLON


def flip(index, by):
    return sum(((index // k) % 2 + (by // k) % 2) % 2 * k for k in (8, 4, 2, 1))


def along(b, lon_off):
    p, f, e = lon_off // 4, (lon_off // 2) % 2, lon_off % 2
    dz = jnp.where(e == 0, p, jnp.where(p == 0, 4, 8 - p))
    return (b // 8 + f) % 2 * 8 + (b % 8 + dz) % 8


def iota(shape, dim):
    return lax.broadcasted_iota(jnp.int32, shape, dim)


def split(value):
    high = value.astype(BF16)
    return high, (value - high.astype(F32)).astype(BF16)


def dot(x, y):
    return jnp.dot(x, y, preferred_element_type=F32)


def window_kernel(
    adj, winds, mix, lweights, w, columns, counts, basis, owner,
    out, grad,
    w_v, f0, f1, fr, wbuf, rbuf, kbuf, kin, kmid, recv, recr, reck, stage, rhs,
    adj_v, winds_v, coef, coef_rim, basis_v, base_hi, base_lo, mat, mat_hi, mat_lo,
    cur, nxt, col_out, col_in, mh, ml, rim, out_v, sens, gsend, gin, grow, gfin,
    pair_sem, ssem, rsem, lsem, ks_sem, kr_sem, hs_sem, hr_sem, gs_sem, gr_sem, out_sem,
):
    a = lax.axis_index("lat")
    b = lax.axis_index("lon")
    me = a * SIDE + b
    bar = pltpu.get_barrier_semaphore()

    def greet(i, _):
        pl.semaphore_signal(bar, inc=1, device_id=((a + i) % SIDE, b), device_id_type=MESH)
        pl.semaphore_signal(bar, inc=1, device_id=(a, (b + i) % SIDE), device_id_type=MESH)
        return 0

    lax.fori_loop(1, SIDE, greet, 0)
    loads = [
        pltpu.make_async_copy(w.at[pl.ds(4 * q, 4)], w_v.at[pl.ds(4 * q, 4)], lsem.at[q])
        for q in range(4)
    ]
    loads.append(pltpu.make_async_copy(adj, adj_v, lsem.at[4]))
    loads.append(pltpu.make_async_copy(winds, winds_v, lsem.at[5]))
    loads.append(pltpu.make_async_copy(basis, basis_v, lsem.at[6]))
    for load in loads:
        load.start()

    def copy_to(src, dst, send_sem, recv_sem, ta, tb):
        return pltpu.make_async_remote_copy(
            src_ref=src, dst_ref=dst, send_sem=send_sem, recv_sem=recv_sem, device_id=(ta, tb), device_id_type=MESH
        )

    slot = iota((SLOTS, DEVICES), 0)
    where = jnp.where(slot < counts[...], columns[...], -1)
    place = flip(a, iota((1, DEVICES), 1) // SIDE) % 8
    placed = jnp.where(iota((128, DEVICES), 0) // SLOTS == place, jnp.concatenate([where] * 8, axis=0), 0)
    for h in range(2):
        kbuf[128 * h : 128 * h + 128, :] = placed[:, 128 * h : 128 * h + 128].T

    def prepare(h, first):
        lanes = pl.ds(pl.multiple_of(128 * h, 128), 128)

        def turn_slot(s, _):
            for c, dst in ((0, f0), (1, f1)):
                block = w_v[s, 128 * c : 128 * c + 128, lanes]
                dst[pl.ds(s, 128, stride=SLOTS), :] = block.astype(F32).T
            return 0

        for q in range(4):
            if first:
                loads[q].wait()
            lax.fori_loop(4 * q, 4 * q + 4, turn_slot, 0)

        def turn_rest(r, _):
            pieces = [w_v[4 * g + r, 256:288, lanes] for g in range(4)]
            block = jnp.concatenate([p.astype(F32) for p in pieces], axis=0)
            fr[pl.ds(r, 128, stride=4), :] = block.T
            return 0

        lax.fori_loop(0, 4, turn_rest, 0)

        def pack(i, _):
            n = 128 * h + 8 * i
            rows = pl.ds(pl.multiple_of(128 * i, 128), 128)
            wbuf[pl.ds(n, 8), :, 0:128] = f0[rows, :].astype(BF16).reshape(8, SLOTS, 128)
            wbuf[pl.ds(n, 8), :, 128:256] = f1[rows, :].astype(BF16).reshape(8, SLOTS, 128)
            four = fr[pl.ds(pl.multiple_of(32 * i, 32), 32), :]
            for m in range(8):
                rbuf[n + m] = four[4 * m : 4 * m + 4, :].astype(BF16)
            return 0

        lax.fori_loop(0, 16, pack, 0)

    def send(lat_off, lon_off):
        ta, tb = flip(a, lat_off), along(b, lon_off)
        d = ta * SIDE + tb
        i = lon_off * SIDE + lat_off
        for n, (src, dst) in enumerate(((wbuf, recv), (rbuf, recr))):
            copy_to(src.at[d], dst.at[i], ssem.at[n], rsem.at[n, lon_off], ta, tb).start()

    def send_lat(lat_off, _):
        send(lat_off, 0)
        return 0

    def send_lon(lon_off, _):
        send(0, lon_off)
        return 0

    prepare(a // 8, True)
    pl.semaphore_wait(bar, 2 * (SIDE - 1))

    def ready(i, _):
        pl.semaphore_signal(pair_sem, inc=1, device_id=(a, (b + i) % SIDE), device_id_type=MESH)
        return 0

    lax.fori_loop(1, SIDE, ready, 0)

    def send_columns(lat_off, _):
        ta = flip(a, lat_off)
        src = kbuf.at[pl.ds(pl.multiple_of(ta * SIDE, SIDE), SIDE)]
        copy_to(src, kin.at[lat_off], ks_sem.at[0], kr_sem.at[0], ta, b).start()
        return 0

    lax.fori_loop(1, SIDE, send_columns, 0)
    lax.fori_loop(1, SIDE, send_lon, 0)
    lax.fori_loop(1, 8, send_lat, 0)
    prepare(1 - a // 8, False)
    lax.fori_loop(8, SIDE, send_lat, 0)
    own = [
        pltpu.make_async_copy(wbuf.at[me], recv.at[0], rsem.at[0, 0]),
        pltpu.make_async_copy(rbuf.at[me], recr.at[0], rsem.at[1, 0]),
    ]
    for copy in own:
        copy.start()

    def pair_of(t):
        return jnp.where(t < 6, t + 2, 7 - t)

    def send_pair(t):
        first = 2 * pair_of(t)

        def both(lat_off, _):
            @pl.when(first > 0)
            def _():
                send(lat_off, first)

            send(lat_off, first + 1)
            return 0

        lax.fori_loop(1, SIDE, both, 0)

    pl.semaphore_wait(pair_sem, SIDE - 1)
    send_pair(0)

    landed = kin.at[pl.ds(1, SIDE - 1)]
    pltpu.make_async_copy(landed, landed, kr_sem.at[0]).wait()
    low = kbuf[pl.ds(pl.multiple_of(a * SIDE, SIDE), SIDE), :]
    high = kin[8]
    for i in range(1, 8):
        low = low + kin[i]
        high = high + kin[8 + i]
    kmid[:, 0, 0:128] = low
    kmid[:, 0, 128:256] = high
    reck[0] = kmid[b]

    def send_rows(lon_off, _):
        tb = along(b, lon_off)
        copy_to(kmid.at[tb], reck.at[lon_off], ks_sem.at[1], kr_sem.at[1], a, tb).start()
        return 0

    lax.fori_loop(1, SIDE, send_rows, 0)
    send_pair(1)

    mat[...] = jnp.zeros_like(mat)
    for t in range(TRACERS):
        mat[LEV * t : LEV * t + LEV, LEV * t : LEV * t + LEV] = mix[...]
    gain = jnp.sum(mat[:, 0:CHAN] * lweights[...].reshape(1, CHAN), axis=1, keepdims=True)
    lane = iota((CHAN, WIDE - CHAN), 1)
    extra = (iota((CHAN, WIDE - CHAN), 0) // LEV == lane % TRACERS) & (lane < TRACERS * SIDE)
    mat[:, CHAN:WIDE] = jnp.where(extra, gain, 0.0)
    mat_hi[...], mat_lo[...] = split(mat[...])

    loads[6].wait()
    pick = jnp.where(iota((DEVICES, DEVICES), 0) == owner[...], 1.0, 0.0).astype(BF16)
    for c in range(CELLS // 128):
        for piece, dst in zip(split(basis_v[128 * c : 128 * c + 128, :]), (base_hi, base_lo)):
            turned = lax.dot_general(pick, piece, (((1,), (1,)), ((), ())), preferred_element_type=F32)
            dst[:, 128 * c : 128 * c + 128] = turned.astype(BF16)

    loads[4].wait()
    loads[5].wait()

    def begin(r, _):
        cur[r + 1, 8:56, 0:CHAN] = adj_v[r]
        cur[r + 1, 8:56, CHAN:WIDE] = jnp.zeros((CLON, WIDE - CHAN), F32)
        return 0

    lax.fori_loop(0, CLAT, begin, 0)

    def coefficients(r):
        both = winds_v[r]
        u = jnp.concatenate([both[:, 0:LEV]] * TRACERS, axis=1)
        v = jnp.concatenate([both[:, LEV : 2 * LEV]] * TRACERS, axis=1)
        east = jnp.maximum(u, 0.0) + diffusion
        west = jnp.maximum(-u, 0.0) + diffusion
        north = jnp.maximum(v, 0.0) + diffusion
        south = jnp.maximum(-v, 0.0) + diffusion
        coef[0, r] = 1.0 - ((east + west) + (north + south))
        coef[1, r] = east
        coef[2, r] = west
        coef[3, r] = north
        coef[4, r] = south

    rows = iota((DEVICES, 64), 0)
    lanes = iota((DEVICES, 64), 1)
    spread = jnp.where((rows // 16 == lanes // 4) & (rows % 4 == lanes % 4), 1.0, 0.0).astype(BF16)
    rows = iota((DEVICES, 128), 0)
    lanes = iota((DEVICES, 128), 1)
    keep = jnp.where((rows // 4) % 4 == lanes // 32, 1.0, 0.0)
    rows = iota((128, 128), 0)
    lanes = iota((128, 128), 1)
    fold = jnp.where(rows % 32 == lanes, 1.0, 0.0).astype(BF16)

    def absorb(g):
        first = g * SIDE
        for n, buf in enumerate((recv, recr)):
            piece = buf.at[pl.ds(first, SIDE)]
            pltpu.make_async_copy(piece, piece, rsem.at[n, g]).wait()
        rhs[:, 0:256] = recv[pl.ds(first, SIDE)].reshape(256, 256)
        for m in range(SIDE):
            stage[4 * m : 4 * m + 4, :] = recr[first + m].astype(F32)
        wide = (dot(spread, stage[...].astype(BF16)) * keep).astype(BF16)
        rhs[:, 256:384] = dot(wide, fold).astype(BF16)
        spot = reck[g]
        for c in range(CLAT // BAND):
            ids = iota((BAND * CLON, 256), 0) + c * BAND * CLON
            table = jnp.where(ids == spot, 1.0, 0.0).astype(BF16)
            cur[c * BAND + 1 : (c + 1) * BAND + 1, 8:56, :] += dot(table, rhs[...]).reshape(BAND, CLON, WIDE)

    coming = reck.at[pl.ds(1, SIDE - 1)]
    pltpu.make_async_copy(coming, coming, kr_sem.at[1]).wait()

    def turn(t, _):
        @pl.when(t < 8)
        def _():
            send_pair(t)

        @pl.when(t < 8)
        def _():
            for i in range(4):
                coefficients(4 * (t - 2) + i)

        first = 2 * pair_of(t - LAG)
        absorb(first)
        absorb(first + 1)
        return 0

    lax.fori_loop(LAG, 8, turn, 0)
    for k in range(5):
        coef_rim[k, 0:CLAT, :] = coef[k, :, 0, :]
        coef_rim[k, CLAT : 2 * CLAT, :] = coef[k, :, CLON - 1, :]

    def last_turns(t, _):
        first = 2 * pair_of(t)
        absorb(first)
        absorb(first + 1)
        return 0

    lax.fori_loop(8 - LAG, 8, last_turns, 0)

    def halo(buf, e):
        north = copy_to(buf.at[CLAT, 8:56, :], buf.at[0, 8:56, :], hs_sem.at[e, 0], hr_sem.at[e, 0], (a + 1) % SIDE, b)
        south = copy_to(buf.at[1, 8:56, :], buf.at[CLAT + 1, 8:56, :], hs_sem.at[e, 1], hr_sem.at[e, 1], (a + SIDE - 1) % SIDE, b)
        east = copy_to(col_out.at[e, 0], col_in.at[e, 0], hs_sem.at[e, 2], hr_sem.at[e, 2], a, (b + 1) % SIDE)
        west = copy_to(col_out.at[e, 1], col_in.at[e, 1], hs_sem.at[e, 3], hr_sem.at[e, 3], a, (b + SIDE - 1) % SIDE)

        @pl.when(a < SIDE - 1)
        def _():
            north.start()

        @pl.when(a > 0)
        def _():
            south.start()

        east.start()
        west.start()
        return north, south, east, west

    def arrive(buf, e, copies):
        north, south, east, west = copies

        @pl.when(a > 0)
        def _():
            north.wait_recv()

        @pl.when(a == 0)
        def _():
            buf[0, 8:56, :] = buf[1, 8:56, :]

        @pl.when(a < SIDE - 1)
        def _():
            south.wait_recv()

        @pl.when(a == SIDE - 1)
        def _():
            buf[CLAT + 1, 8:56, :] = buf[CLAT, 8:56, :]

        east.wait_recv()
        west.wait_recv()

    def finish(copies):
        north, south, east, west = copies

        @pl.when(a < SIDE - 1)
        def _():
            north.wait_send()

        @pl.when(a > 0)
        def _():
            south.wait_send()

        east.wait_send()
        west.wait_send()

    def blend(weights, values):
        m = weights[0] * values[0]
        for k in range(1, 5):
            m = m + weights[k] * values[k]
        return m

    def mixed(high, low, width):
        return dot(high, mat_hi[:, 0:width]) + dot(low, mat_hi[:, 0:width]) + dot(high, mat_lo[:, 0:width])

    def inner(buf, c, width):
        for k in range(ROWS):
            r = 1 + c * ROWS + k
            m = blend(
                [coef[n, r] for n in range(5)],
                [buf[r + 1, 8:56, 0:CHAN], buf[r + 1, 9:57, 0:CHAN], buf[r + 1, 7:55, 0:CHAN],
                 buf[r + 2, 8:56, 0:CHAN], buf[r, 8:56, 0:CHAN]],
            )
            mh[k * CLON : (k + 1) * CLON, :], ml[k * CLON : (k + 1) * CLON, :] = split(m)
        return mixed(mh[...], ml[...], width)

    def outer(buf, e, width):
        west = col_in[e, 0, :, 0:CHAN]
        east = col_in[e, 1, :, 0:CHAN]
        for n, (x, x_west, x_east) in enumerate(((8, west, None), (55, None, east))):
            span = slice(n * CLAT, (n + 1) * CLAT)
            x_west = buf[1 : CLAT + 1, x - 1, 0:CHAN] if x_west is None else x_west
            x_east = buf[1 : CLAT + 1, x + 1, 0:CHAN] if x_east is None else x_east
            rim[span, :] = blend(
                [coef_rim[k, span, :] for k in range(5)],
                [buf[1 : CLAT + 1, x, 0:CHAN], x_east, x_west, buf[2 : CLAT + 2, x, 0:CHAN], buf[0:CLAT, x, 0:CHAN]],
            )
        for n, r in enumerate((0, CLAT - 1)):
            buf[r + 1, 7:8, 0:CHAN] = west[r : r + 1, :]
            buf[r + 1, 56:57, 0:CHAN] = east[r : r + 1, :]
            m = blend(
                [coef[k, r] for k in range(5)],
                [buf[r + 1, 8:56, 0:CHAN], buf[r + 1, 9:57, 0:CHAN], buf[r + 1, 7:55, 0:CHAN],
                 buf[r + 2, 8:56, 0:CHAN], buf[r, 8:56, 0:CHAN]],
            )
            rim[2 * CLAT + n * CLON : 2 * CLAT + (n + 1) * CLON, :] = m
        return mixed(*split(rim[...]), width)

    col_out[0, 0, :, 0:CHAN] = cur[1 : CLAT + 1, 55, 0:CHAN]
    col_out[0, 1, :, 0:CHAN] = cur[1 : CLAT + 1, 8, 0:CHAN]
    one = halo(cur, 0)

    def inner_one(c, _):
        res = inner(cur, c, CHAN).reshape(ROWS, CLON, CHAN)
        nxt[pl.ds(c * ROWS + 2, ROWS), 8:56, 0:CHAN] = res
        return 0

    lax.fori_loop(0, 2, inner_one, 0)
    arrive(cur, 0, one)
    res = outer(cur, 0, CHAN)
    nxt[1 : CLAT + 1, 8, 0:CHAN] = res[0:CLAT]
    nxt[1 : CLAT + 1, 55, 0:CHAN] = res[CLAT : 2 * CLAT]
    nxt[1, 8:56, 0:CHAN] = res[2 * CLAT : 2 * CLAT + CLON]
    nxt[CLAT, 8:56, 0:CHAN] = res[2 * CLAT + CLON : RIM]
    col_out[1, 0, :, 0:CHAN] = res[CLAT : 2 * CLAT]
    col_out[1, 1, :, 0:CHAN] = res[0:CLAT]
    two = halo(nxt, 1)

    def inner_two(c, _):
        res = inner(nxt, c, WIDE)
        out_v[pl.ds(c * ROWS + 1, ROWS)] = res[:, 0:CHAN].reshape(ROWS, CLON, CHAN)
        sens[pl.ds(c * ROWS + 1, ROWS)] = res[:, 256:WIDE].reshape(ROWS, CLON, 128)
        return 0

    lax.fori_loop(0, 2, inner_two, 0)
    arrive(nxt, 1, two)
    res = outer(nxt, 1, WIDE)
    for dst, lanes in ((out_v, slice(0, CHAN)), (sens, slice(256, WIDE))):
        dst[:, 0, :] = res[0:CLAT, lanes]
        dst[:, CLON - 1, :] = res[CLAT : 2 * CLAT, lanes]
        dst[0] = res[2 * CLAT : 2 * CLAT + CLON, lanes]
        dst[CLAT - 1] = res[2 * CLAT + CLON : RIM, lanes]
    leave = pltpu.make_async_copy(out_v, out, out_sem.at[0])
    leave.start()

    sens_hi, sens_lo = split(sens[...].reshape(CELLS, 128))
    part = dot(base_hi[...], sens_hi) + dot(base_lo[...], sens_hi) + dot(base_hi[...], sens_lo)
    rows = iota((DEVICES, 128), 0)
    lanes = iota((DEVICES, 128), 1)
    part = jnp.where((lanes // TRACERS == rows % SIDE + 8) & (lanes >= 32), part, 0.0)
    gsend[:, 0, :] = jnp.sum(part.reshape(SIDE, SIDE, 128), axis=1)

    def give_lat(i, _):
        ta = (a + i) % SIDE
        copy_to(gsend.at[ta], gin.at[i], gs_sem.at[0], gr_sem.at[0], ta, b).start()
        return 0

    lax.fori_loop(1, SIDE, give_lat, 0)
    got = gsend[a]
    lat_in = gin.at[pl.ds(1, SIDE - 1)]
    pltpu.make_async_copy(lat_in, lat_in, gr_sem.at[0]).wait()
    for i in range(1, SIDE):
        got = got + gin[i]
    grow[...] = got

    def give_lon(i, _):
        copy_to(grow, gfin.at[i], gs_sem.at[1], gr_sem.at[1], a, (b + i) % SIDE).start()
        return 0

    lax.fori_loop(1, SIDE, give_lon, 0)
    lon_in = gfin.at[pl.ds(1, SIDE - 1)]
    pltpu.make_async_copy(lon_in, lon_in, gr_sem.at[1]).wait()
    for i in range(1, SIDE):
        got = got + gfin[i]
    lanes = iota((1, 128), 1)
    owned = jnp.zeros((1, TRACERS), F32)
    for t in range(TRACERS):
        value = jnp.sum(jnp.where(lanes == 32 + TRACERS * b + t, got, 0.0), axis=1, keepdims=True)
        owned = jnp.where(iota((1, TRACERS), 1) == t, value, owned)
    grad[...] = owned * (1.0 / jnp.sqrt(jnp.full((1, TRACERS), CELLS * DEVICES, F32)))

    finish(one)
    finish(two)
    leave.wait()
    for piece, sem in ((landed, ks_sem.at[0]), (coming, ks_sem.at[1]), (lat_in, gs_sem.at[0]), (lon_in, gs_sem.at[1])):
        pltpu.make_async_copy(piece, piece, sem).wait()
    for n, buf in enumerate((recv, recr)):
        piece = buf.at[pl.ds(1, DEVICES - 1)]
        pltpu.make_async_copy(piece, piece, ssem.at[n]).wait()


def body(
    adjoint_in, winds, vert_mix, level_weights, snd_weights, snd_columns, snd_counts, basis, owner
):
    anywhere = pl.BlockSpec(memory_space=pl.ANY)
    vmem = pl.BlockSpec(memory_space=pltpu.VMEM)
    state, grad = pl.pallas_call(
        window_kernel,
        out_shape=(
            jax.ShapeDtypeStruct((CLAT, CLON, CHAN), F32),
            jax.ShapeDtypeStruct((1, TRACERS), F32),
        ),
        in_specs=[anywhere, anywhere, vmem, vmem, anywhere, vmem, vmem, anywhere, vmem],
        out_specs=(anywhere, vmem),
        scratch_shapes=[
            pltpu.VMEM((SLOTS, CHAN, DEVICES), BF16),
            pltpu.VMEM((128 * SLOTS, 128), F32),
            pltpu.VMEM((128 * SLOTS, 128), F32),
            pltpu.VMEM((128 * 4, 128), F32),
            pltpu.VMEM((DEVICES, SLOTS, 256), BF16),
            pltpu.VMEM((DEVICES, 4, 128), BF16),
            pltpu.VMEM((DEVICES, 128), jnp.int32),
            pltpu.VMEM((SIDE, SIDE, 128), jnp.int32),
            pltpu.VMEM((SIDE, 1, 256), jnp.int32),
            pltpu.VMEM((DEVICES, SLOTS, 256), BF16),
            pltpu.VMEM((DEVICES, 4, 128), BF16),
            pltpu.VMEM((SIDE, 1, 256), jnp.int32),
            pltpu.VMEM((64, 128), F32),
            pltpu.VMEM((256, WIDE), BF16),
            pltpu.VMEM((CLAT, CLON, CHAN), F32),
            pltpu.VMEM((CLAT, CLON, 2 * LEV), F32),
            pltpu.VMEM((5, CLAT, CLON, CHAN), F32),
            pltpu.VMEM((5, 2 * CLAT, CHAN), F32),
            pltpu.VMEM((CELLS, DEVICES), F32),
            pltpu.VMEM((DEVICES, CELLS), BF16),
            pltpu.VMEM((DEVICES, CELLS), BF16),
            pltpu.VMEM((CHAN, WIDE), F32),
            pltpu.VMEM((CHAN, WIDE), BF16),
            pltpu.VMEM((CHAN, WIDE), BF16),
            pltpu.VMEM((CLAT + 2, 64, WIDE), F32),
            pltpu.VMEM((CLAT + 2, 64, WIDE), F32),
            pltpu.VMEM((2, 2, CLAT, WIDE), F32),
            pltpu.VMEM((2, 2, CLAT, WIDE), F32),
            pltpu.VMEM((ROWS * CLON, CHAN), BF16),
            pltpu.VMEM((ROWS * CLON, CHAN), BF16),
            pltpu.VMEM((RIM, CHAN), F32),
            pltpu.VMEM((CLAT, CLON, CHAN), F32),
            pltpu.VMEM((CLAT, CLON, 128), F32),
            pltpu.VMEM((SIDE, 1, 128), F32),
            pltpu.VMEM((SIDE, 1, 128), F32),
            pltpu.VMEM((1, 128), F32),
            pltpu.VMEM((SIDE, 1, 128), F32),
            pltpu.SemaphoreType.REGULAR,
            pltpu.SemaphoreType.DMA((2,)),
            pltpu.SemaphoreType.DMA((2, SIDE)),
            pltpu.SemaphoreType.DMA((7,)),
            pltpu.SemaphoreType.DMA((2,)),
            pltpu.SemaphoreType.DMA((2,)),
            pltpu.SemaphoreType.DMA((2, 4)),
            pltpu.SemaphoreType.DMA((2, 4)),
            pltpu.SemaphoreType.DMA((2,)),
            pltpu.SemaphoreType.DMA((2,)),
            pltpu.SemaphoreType.DMA((1,)),
        ],
        compiler_params=pltpu.CompilerParams(
            collective_id=0, has_side_effects=True, vmem_limit_bytes=56 << 20
        ),
        name="window",
    )(
        adjoint_in,
        winds,
        vert_mix,
        level_weights,
        jnp.transpose(snd_weights[0, 0], (1, 2, 0)),
        jnp.transpose(snd_columns[0, 0], (1, 0)),
        snd_counts[0],
        basis.reshape(CELLS, DEVICES),
        owner.reshape(1, DEVICES),
    )
    return state, grad.reshape(1, 1, TRACERS)


def solution(mesh):
    return jax.shard_map(
        body,
        mesh=mesh,
        in_specs=(
            P("lat", "lon", None),
            P("lat", "lon", None),
            P(),
            P(),
            P("lat", "lon", None, None, None),
            P("lat", "lon", None, None),
            P("lat", "lon", None),
            P("lat", "lon", None),
            P(),
        ),
        out_specs=(P("lat", "lon", None), P(("lat", "lon"), None, None)),
        check_vma=False,
    )
```

```python
import jax
import jax.numpy as jnp
from jax import lax
from jax.experimental import pallas as pl
from jax.experimental.pallas import tpu as pltpu
from jax.sharding import PartitionSpec as P

diffusion = 0.05
MESH = pl.DeviceIdType.MESH
BF16 = jnp.bfloat16
F32 = jnp.float32
DEVICES = 256
SIDE = 16
SLOTS = 16
CLAT, CLON = 24, 48
CELLS = CLAT * CLON
CHAN = 288
WIDE = 384
LEV = 72
TRACERS = 4
BAND = 8
LAG = 2
ROWS = 11
RIM = 2 * CLAT + 2 * CLON


def flip(index, by):
    return sum(((index // k) % 2 + (by // k) % 2) % 2 * k for k in (8, 4, 2, 1))


def along(b, lon_off):
    p, f, e = lon_off // 4, (lon_off // 2) % 2, lon_off % 2
    dz = jnp.where(p == 0, 4 * f, jnp.where(e == 0, p, 8 - p))
    f = jnp.where(p == 0, e, f)
    return (b // 8 + f) % 2 * 8 + (b % 8 + dz) % 8


def iota(shape, dim):
    return lax.broadcasted_iota(jnp.int32, shape, dim)


def split(value):
    high = value.astype(BF16)
    return high, (value - high.astype(F32)).astype(BF16)


def dot(x, y):
    return jnp.dot(x, y, preferred_element_type=F32)


def window_kernel(
    adj, winds, mix, lweights, w, columns, counts, basis, owner,
    out, grad,
    w_v, f0, f1, fr, wbuf, rbuf, kbuf, kin, kmid, recv, recr, reck, stage, rhs,
    adj_v, winds_v, coef, coef_rim, basis_v, base_hi, base_lo, mat, mat_hi, mat_lo,
    cur, nxt, col_out, col_in, row_in, mh, ml, rim, out_v, sens, gsend, gin, grow, gfin,
    pair_sem, ssem, rsem, lsem, ks_sem, kr_sem, hs_sem, hr_sem, gs_sem, gr_sem, out_sem,
):
    a = lax.axis_index("lat")
    b = lax.axis_index("lon")
    me = a * SIDE + b
    bar = pltpu.get_barrier_semaphore()

    def greet(i, _):
        pl.semaphore_signal(bar, inc=1, device_id=((a + i) % SIDE, b), device_id_type=MESH)
        pl.semaphore_signal(bar, inc=1, device_id=(a, (b + i) % SIDE), device_id_type=MESH)
        return 0

    halves = [a // 8, 1 - a // 8]
    loads = []
    for n, h in enumerate(halves):
        lanes = pl.ds(pl.multiple_of(128 * h, 128), 128)
        for q in range(2):
            eight = pl.ds(8 * q, 8)
            loads.append(pltpu.make_async_copy(w.at[eight, :, lanes], w_v.at[n, eight], lsem.at[2 * n + q]))
    for load in loads:
        load.start()
    lax.fori_loop(1, SIDE, greet, 0)
    loads.append(pltpu.make_async_copy(adj, adj_v, lsem.at[4]))
    loads.append(pltpu.make_async_copy(winds, winds_v, lsem.at[5]))
    loads.append(pltpu.make_async_copy(basis, basis_v, lsem.at[6]))
    for load in loads[4:]:
        load.start()

    def copy_to(src, dst, send_sem, recv_sem, ta, tb):
        return pltpu.make_async_remote_copy(
            src_ref=src, dst_ref=dst, send_sem=send_sem, recv_sem=recv_sem, device_id=(ta, tb), device_id_type=MESH
        )

    slot = iota((SLOTS, DEVICES), 0)
    where = jnp.where(slot < counts[...], columns[...], -1)
    place = flip(a, iota((1, DEVICES), 1) // SIDE) % 8
    placed = jnp.where(iota((128, DEVICES), 0) // SLOTS == place, jnp.concatenate([where] * 8, axis=0), 0)
    for h in range(2):
        kbuf[128 * h : 128 * h + 128, :] = placed[:, 128 * h : 128 * h + 128].T

    def prepare(n):
        h = halves[n]
        for q in range(2):
            loads[2 * n + q].wait()
            for s in range(8 * q, 8 * q + 8):
                for c, dst in ((0, f0), (1, f1)):
                    block = w_v[n, s, 128 * c : 128 * c + 128, :]
                    dst[pl.ds(s, 128, stride=SLOTS), :] = block.astype(F32).T
        for r in range(4):
            pieces = [w_v[n, 4 * g + r, 256:288, :] for g in range(4)]
            block = jnp.concatenate([p.astype(F32) for p in pieces], axis=0)
            fr[pl.ds(r, 128, stride=4), :] = block.T

        def pack(i, _):
            first = 128 * h + 8 * i
            rows = pl.ds(pl.multiple_of(128 * i, 128), 128)
            wbuf[pl.ds(first, 8), :, 0:128] = f0[rows, :].astype(BF16).reshape(8, SLOTS, 128)
            wbuf[pl.ds(first, 8), :, 128:256] = f1[rows, :].astype(BF16).reshape(8, SLOTS, 128)
            four = fr[pl.ds(pl.multiple_of(32 * i, 32), 32), :]
            rbuf[pl.ds(first, 8)] = four.reshape(8, 4, 128).astype(BF16)
            return 0

        lax.fori_loop(0, 16, pack, 0, unroll=4)

    def send(lat_off, lon_off):
        ta, tb = flip(a, lat_off), along(b, lon_off)
        d = ta * SIDE + tb
        i = lon_off * SIDE + lat_off
        for n, (src, dst) in enumerate(((wbuf, recv), (rbuf, recr))):
            copy_to(src.at[d], dst.at[i], ssem.at[n], rsem.at[n, lon_off], ta, tb).start()

    def send_lat(lat_off, _):
        send(lat_off, 0)
        return 0

    def send_lon(lon_off, _):
        send(0, lon_off)
        return 0

    prepare(0)
    pl.semaphore_wait(bar, 2 * (SIDE - 1))

    def ready(i, _):
        pl.semaphore_signal(pair_sem, inc=1, device_id=(a, (b + i) % SIDE), device_id_type=MESH)
        return 0

    lax.fori_loop(1, SIDE, ready, 0)

    def send_columns(lat_off, _):
        ta = flip(a, lat_off)
        src = kbuf.at[pl.ds(pl.multiple_of(ta * SIDE, SIDE), SIDE)]
        copy_to(src, kin.at[lat_off], ks_sem.at[0], kr_sem.at[0], ta, b).start()
        return 0

    lax.fori_loop(1, SIDE, send_columns, 0)
    lax.fori_loop(1, SIDE, send_lon, 0)
    lax.fori_loop(1, 8, send_lat, 0)
    prepare(1)
    lax.fori_loop(8, SIDE, send_lat, 0)
    own = [
        pltpu.make_async_copy(wbuf.at[me], recv.at[0], rsem.at[0, 0]),
        pltpu.make_async_copy(rbuf.at[me], recr.at[0], rsem.at[1, 0]),
    ]
    for copy in own:
        copy.start()

    def pair_of(t):
        near = 2 * (3 - (t - 1) // 2) + (t - 1) % 2
        return jnp.where(t == 0, 1, jnp.where(t == 7, 0, near))

    def send_pair(t):
        first = 2 * pair_of(t)

        def both(i, _):
            lat_off = SIDE - i

            @pl.when(first > 0)
            def _():
                send(lat_off, first)

            send(lat_off, first + 1)
            return 0

        lax.fori_loop(1, SIDE, both, 0)

    pl.semaphore_wait(pair_sem, SIDE - 1)
    send_pair(0)

    landed = kin.at[pl.ds(1, SIDE - 1)]
    pltpu.make_async_copy(landed, landed, kr_sem.at[0]).wait()
    low = kbuf[pl.ds(pl.multiple_of(a * SIDE, SIDE), SIDE), :]
    high = kin[8]
    for i in range(1, 8):
        low = low + kin[i]
        high = high + kin[8 + i]
    kmid[:, 0, 0:128] = low
    kmid[:, 0, 128:256] = high
    reck[0] = kmid[b]

    def send_rows(lon_off, _):
        tb = along(b, lon_off)
        copy_to(kmid.at[tb], reck.at[lon_off], ks_sem.at[1], kr_sem.at[1], a, tb).start()
        return 0

    lax.fori_loop(1, SIDE, send_rows, 0)
    send_pair(1)

    mat[...] = jnp.zeros_like(mat)
    for t in range(TRACERS):
        mat[LEV * t : LEV * t + LEV, LEV * t : LEV * t + LEV] = mix[...]
    gain = jnp.sum(mat[:, 0:CHAN] * lweights[...].reshape(1, CHAN), axis=1, keepdims=True)
    lane = iota((CHAN, WIDE - CHAN), 1)
    extra = (iota((CHAN, WIDE - CHAN), 0) // LEV == lane % TRACERS) & (lane < TRACERS * SIDE)
    mat[:, CHAN:WIDE] = jnp.where(extra, gain, 0.0)
    mat_hi[...], mat_lo[...] = split(mat[...])

    loads[6].wait()
    pick = jnp.where(iota((DEVICES, DEVICES), 0) == owner[...], 1.0, 0.0).astype(BF16)
    for c in range(CELLS // 128):
        for piece, dst in zip(split(basis_v[128 * c : 128 * c + 128, :]), (base_hi, base_lo)):
            turned = lax.dot_general(pick, piece, (((1,), (1,)), ((), ())), preferred_element_type=F32)
            dst[:, 128 * c : 128 * c + 128] = turned.astype(BF16)

    loads[4].wait()
    loads[5].wait()

    def clear(r, _):
        cur[r] = jnp.zeros((64, WIDE), F32)
        nxt[r] = jnp.zeros((64, WIDE), F32)
        return 0

    lax.fori_loop(0, CLAT + 2, clear, 0)

    def begin(r, _):
        cur[r + 1, 8:56, 0:CHAN] = adj_v[r]
        return 0

    lax.fori_loop(0, CLAT, begin, 0)

    def coefficients(r):
        both = winds_v[r]
        u = jnp.concatenate([both[:, 0:LEV]] * TRACERS, axis=1)
        v = jnp.concatenate([both[:, LEV : 2 * LEV]] * TRACERS, axis=1)
        east = jnp.maximum(u, 0.0) + diffusion
        west = jnp.maximum(-u, 0.0) + diffusion
        north = jnp.maximum(v, 0.0) + diffusion
        south = jnp.maximum(-v, 0.0) + diffusion
        coef[0, r] = 1.0 - ((east + west) + (north + south))
        coef[1, r] = east
        coef[2, r] = west
        coef[3, r] = north
        coef[4, r] = south

    rows = iota((DEVICES, 64), 0)
    lanes = iota((DEVICES, 64), 1)
    spread = jnp.where((rows // 16 == lanes // 4) & (rows % 4 == lanes % 4), 1.0, 0.0).astype(BF16)
    rows = iota((DEVICES, 128), 0)
    lanes = iota((DEVICES, 128), 1)
    keep = jnp.where((rows // 4) % 4 == lanes // 32, 1.0, 0.0)
    rows = iota((128, 128), 0)
    lanes = iota((128, 128), 1)
    fold = jnp.where(rows % 32 == lanes, 1.0, 0.0).astype(BF16)

    def absorb(g):
        first = g * SIDE
        for n, buf in enumerate((recv, recr)):
            piece = buf.at[pl.ds(first, SIDE)]
            pltpu.make_async_copy(piece, piece, rsem.at[n, g]).wait()
        rhs[:, 0:256] = recv[pl.ds(first, SIDE)].reshape(256, 256)
        for m in range(SIDE):
            stage[4 * m : 4 * m + 4, :] = recr[first + m].astype(F32)
        wide = (dot(spread, stage[...].astype(BF16)) * keep).astype(BF16)
        rhs[:, 256:384] = dot(wide, fold).astype(BF16)
        spot = reck[g]
        for c in range(CLAT // BAND):
            ids = iota((BAND * CLON, 256), 0) + c * BAND * CLON
            table = jnp.where(ids == spot, 1.0, 0.0).astype(BF16)
            cur[c * BAND + 1 : (c + 1) * BAND + 1, 8:56, :] += dot(table, rhs[...]).reshape(BAND, CLON, WIDE)

    coming = reck.at[pl.ds(1, SIDE - 1)]
    pltpu.make_async_copy(coming, coming, kr_sem.at[1]).wait()

    def turn(t, _):
        @pl.when(t < 8)
        def _():
            send_pair(t)

        @pl.when(t < 8)
        def _():
            for i in range(4):
                coefficients(4 * (t - 2) + i)

        first = 2 * pair_of(t - LAG)
        absorb(first)
        absorb(first + 1)
        return 0

    lax.fori_loop(LAG, 8, turn, 0)
    for k in range(5):
        coef_rim[k, 0:CLAT, :] = coef[k, :, 0, :]
        coef_rim[k, CLAT : 2 * CLAT, :] = coef[k, :, CLON - 1, :]

    absorb(0)
    last = 2 * pair_of(6)

    def last_turns(g, _):
        absorb(jnp.where(g == 2, 1, last + g))
        return 0

    lax.fori_loop(0, 3, last_turns, 0)

    def halo(buf, e):
        north = copy_to(buf.at[CLAT, 8:56, :], row_in.at[e, 0], hs_sem.at[e, 0], hr_sem.at[e, 0], (a + 1) % SIDE, b)
        south = copy_to(buf.at[1, 8:56, :], row_in.at[e, 1], hs_sem.at[e, 1], hr_sem.at[e, 1], (a + SIDE - 1) % SIDE, b)
        east = copy_to(col_out.at[e, 0], col_in.at[e, 0], hs_sem.at[e, 2], hr_sem.at[e, 2], a, (b + 1) % SIDE)
        west = copy_to(col_out.at[e, 1], col_in.at[e, 1], hs_sem.at[e, 3], hr_sem.at[e, 3], a, (b + SIDE - 1) % SIDE)

        @pl.when(a < SIDE - 1)
        def _():
            north.start()

        @pl.when(a > 0)
        def _():
            south.start()

        east.start()
        west.start()
        return north, south, east, west

    def arrive(buf, e, copies):
        north, south, east, west = copies

        @pl.when(a > 0)
        def _():
            north.wait_recv()

        @pl.when(a == 0)
        def _():
            row_in[e, 0] = buf[1, 8:56, :]

        @pl.when(a < SIDE - 1)
        def _():
            south.wait_recv()

        @pl.when(a == SIDE - 1)
        def _():
            row_in[e, 1] = buf[CLAT, 8:56, :]

        east.wait_recv()
        west.wait_recv()

    def finish(copies):
        north, south, east, west = copies

        @pl.when(a < SIDE - 1)
        def _():
            north.wait_send()

        @pl.when(a > 0)
        def _():
            south.wait_send()

        east.wait_send()
        west.wait_send()

    def blend(weights, values):
        m = weights[0] * values[0]
        for k in range(1, 5):
            m = m + weights[k] * values[k]
        return m

    def mixed(high, low, width):
        return dot(high, mat_hi[:, 0:width]) + dot(low, mat_hi[:, 0:width]) + dot(high, mat_lo[:, 0:width])

    def inner(buf, c, width):
        for k in range(ROWS):
            r = 1 + c * ROWS + k
            m = blend(
                [coef[n, r] for n in range(5)],
                [buf[r + 1, 8:56, 0:CHAN], buf[r + 1, 9:57, 0:CHAN], buf[r + 1, 7:55, 0:CHAN],
                 buf[r + 2, 8:56, 0:CHAN], buf[r, 8:56, 0:CHAN]],
            )
            mh[k * CLON : (k + 1) * CLON, :], ml[k * CLON : (k + 1) * CLON, :] = split(m)
        return mixed(mh[...], ml[...], width)

    def rim_inside(buf):
        for n, x in enumerate((8, 55)):
            span = slice(n * CLAT, (n + 1) * CLAT)
            rim[span, :] = blend(
                [coef_rim[k, span, :] for k in range(5)],
                [buf[1 : CLAT + 1, x, 0:CHAN], buf[1 : CLAT + 1, x + 1, 0:CHAN], buf[1 : CLAT + 1, x - 1, 0:CHAN],
                 buf[2 : CLAT + 2, x, 0:CHAN], buf[0:CLAT, x, 0:CHAN]],
            )
        for n, r in enumerate((0, CLAT - 1)):
            rim[2 * CLAT + n * CLON : 2 * CLAT + (n + 1) * CLON, :] = blend(
                [coef[k, r] for k in range(5)],
                [buf[r + 1, 8:56, 0:CHAN], buf[r + 1, 9:57, 0:CHAN], buf[r + 1, 7:55, 0:CHAN],
                 buf[r + 2, 8:56, 0:CHAN], buf[r, 8:56, 0:CHAN]],
            )

    def rim_beyond(e, width):
        rim[0:CLAT, :] += coef_rim[2, 0:CLAT, :] * col_in[e, 0, :, 0:CHAN]
        rim[CLAT : 2 * CLAT, :] += coef_rim[1, CLAT : 2 * CLAT, :] * col_in[e, 1, :, 0:CHAN]
        for n, r, k in ((0, 0, 4), (1, CLAT - 1, 3)):
            rim[2 * CLAT + n * CLON : 2 * CLAT + (n + 1) * CLON, :] += coef[k, r] * row_in[e, n, :, 0:CHAN]
            for i, x in ((r, 0), (CLAT + r, CLON - 1)):
                rim[i : i + 1, :] += coef_rim[k, i : i + 1, :] * row_in[e, n, x : x + 1, 0:CHAN]
        return mixed(*split(rim[...]), width)

    col_out[0, 0, :, 0:CHAN] = cur[1 : CLAT + 1, 55, 0:CHAN]
    col_out[0, 1, :, 0:CHAN] = cur[1 : CLAT + 1, 8, 0:CHAN]
    one = halo(cur, 0)

    def inner_one(c, _):
        res = inner(cur, c, CHAN).reshape(ROWS, CLON, CHAN)
        nxt[pl.ds(c * ROWS + 2, ROWS), 8:56, 0:CHAN] = res
        return 0

    lax.fori_loop(0, 2, inner_one, 0)
    rim_inside(cur)
    arrive(cur, 0, one)
    res = rim_beyond(0, CHAN)
    nxt[1, 8:56, 0:CHAN] = res[2 * CLAT : 2 * CLAT + CLON]
    nxt[CLAT, 8:56, 0:CHAN] = res[2 * CLAT + CLON : RIM]
    nxt[1 : CLAT + 1, 8, 0:CHAN] = res[0:CLAT]
    nxt[1 : CLAT + 1, 55, 0:CHAN] = res[CLAT : 2 * CLAT]
    col_out[1, 0, :, 0:CHAN] = res[CLAT : 2 * CLAT]
    col_out[1, 1, :, 0:CHAN] = res[0:CLAT]
    two = halo(nxt, 1)

    def inner_two(c, _):
        res = inner(nxt, c, WIDE)
        out_v[pl.ds(c * ROWS + 1, ROWS)] = res[:, 0:CHAN].reshape(ROWS, CLON, CHAN)
        sens[pl.ds(c * ROWS + 1, ROWS)] = res[:, 256:WIDE].reshape(ROWS, CLON, 128)
        return 0

    lax.fori_loop(0, 2, inner_two, 0)
    rim_inside(nxt)
    arrive(nxt, 1, two)
    res = rim_beyond(1, WIDE)
    for dst, lanes in ((sens, slice(256, WIDE)), (out_v, slice(0, CHAN))):
        dst[0] = res[2 * CLAT : 2 * CLAT + CLON, lanes]
        dst[CLAT - 1] = res[2 * CLAT + CLON : RIM, lanes]
        dst[:, 0, :] = res[0:CLAT, lanes]
        dst[:, CLON - 1, :] = res[CLAT : 2 * CLAT, lanes]
    leave = pltpu.make_async_copy(out_v, out, out_sem.at[0])
    leave.start()

    sens_hi, sens_lo = split(sens[...].reshape(CELLS, 128))
    part = dot(base_hi[...], sens_hi) + dot(base_lo[...], sens_hi) + dot(base_hi[...], sens_lo)
    rows = iota((DEVICES, 128), 0)
    lanes = iota((DEVICES, 128), 1)
    part = jnp.where((lanes // TRACERS == rows % SIDE + 8) & (lanes >= 32), part, 0.0)
    gsend[:, 0, :] = jnp.sum(part.reshape(SIDE, SIDE, 128), axis=1)

    def give_lat(i, _):
        ta = (a + i) % SIDE
        copy_to(gsend.at[ta], gin.at[i], gs_sem.at[0], gr_sem.at[0], ta, b).start()
        return 0

    lax.fori_loop(1, SIDE, give_lat, 0)
    got = gsend[a]
    lat_in = gin.at[pl.ds(1, SIDE - 1)]
    pltpu.make_async_copy(lat_in, lat_in, gr_sem.at[0]).wait()
    for i in range(1, SIDE):
        got = got + gin[i]
    grow[...] = got

    def give_lon(i, _):
        copy_to(grow, gfin.at[i], gs_sem.at[1], gr_sem.at[1], a, (b + i) % SIDE).start()
        return 0

    lax.fori_loop(1, SIDE, give_lon, 0)
    lon_in = gfin.at[pl.ds(1, SIDE - 1)]
    pltpu.make_async_copy(lon_in, lon_in, gr_sem.at[1]).wait()
    for i in range(1, SIDE):
        got = got + gfin[i]
    lanes = iota((1, 128), 1)
    owned = jnp.zeros((1, TRACERS), F32)
    for t in range(TRACERS):
        value = jnp.sum(jnp.where(lanes == 32 + TRACERS * b + t, got, 0.0), axis=1, keepdims=True)
        owned = jnp.where(iota((1, TRACERS), 1) == t, value, owned)
    grad[...] = owned * (1.0 / jnp.sqrt(jnp.full((1, TRACERS), CELLS * DEVICES, F32)))

    finish(one)
    finish(two)
    leave.wait()
    for piece, sem in ((landed, ks_sem.at[0]), (coming, ks_sem.at[1]), (lat_in, gs_sem.at[0]), (lon_in, gs_sem.at[1])):
        pltpu.make_async_copy(piece, piece, sem).wait()
    for n, buf in enumerate((recv, recr)):
        piece = buf.at[pl.ds(1, DEVICES - 1)]
        pltpu.make_async_copy(piece, piece, ssem.at[n]).wait()


def deliver_kernel(state, grad, state_out, grad_out, held, sems):
    parts = 4
    rows = CLAT // parts
    spans = [pl.ds(i * rows, rows) for i in range(parts)]
    reads = [pltpu.make_async_copy(state.at[p], held.at[p], sems.at[0, i]) for i, p in enumerate(spans)]
    writes = [pltpu.make_async_copy(held.at[p], state_out.at[p], sems.at[1, i]) for i, p in enumerate(spans)]
    for read in reads:
        read.start()
    grad_out[...] = grad[...].reshape(1, 1, TRACERS)
    for read, write in zip(reads, writes):
        read.wait()
        write.start()
    for write in writes:
        write.wait()


def body(
    adjoint_in, winds, vert_mix, level_weights, snd_weights, snd_columns, snd_counts, basis, owner
):
    anywhere = pl.BlockSpec(memory_space=pl.ANY)
    vmem = pl.BlockSpec(memory_space=pltpu.VMEM)
    state, grad = pl.pallas_call(
        window_kernel,
        out_shape=(
            jax.ShapeDtypeStruct((CLAT, CLON, CHAN), F32),
            jax.ShapeDtypeStruct((1, TRACERS), F32),
        ),
        in_specs=[anywhere, anywhere, vmem, vmem, anywhere, vmem, vmem, anywhere, vmem],
        out_specs=(anywhere, vmem),
        scratch_shapes=[
            pltpu.VMEM((2, SLOTS, CHAN, 128), BF16),
            pltpu.VMEM((128 * SLOTS, 128), F32),
            pltpu.VMEM((128 * SLOTS, 128), F32),
            pltpu.VMEM((128 * 4, 128), F32),
            pltpu.VMEM((DEVICES, SLOTS, 256), BF16),
            pltpu.VMEM((DEVICES, 4, 128), BF16),
            pltpu.VMEM((DEVICES, 128), jnp.int32),
            pltpu.VMEM((SIDE, SIDE, 128), jnp.int32),
            pltpu.VMEM((SIDE, 1, 256), jnp.int32),
            pltpu.VMEM((DEVICES, SLOTS, 256), BF16),
            pltpu.VMEM((DEVICES, 4, 128), BF16),
            pltpu.VMEM((SIDE, 1, 256), jnp.int32),
            pltpu.VMEM((64, 128), F32),
            pltpu.VMEM((256, WIDE), BF16),
            pltpu.VMEM((CLAT, CLON, CHAN), F32),
            pltpu.VMEM((CLAT, CLON, 2 * LEV), F32),
            pltpu.VMEM((5, CLAT, CLON, CHAN), F32),
            pltpu.VMEM((5, 2 * CLAT, CHAN), F32),
            pltpu.VMEM((CELLS, DEVICES), F32),
            pltpu.VMEM((DEVICES, CELLS), BF16),
            pltpu.VMEM((DEVICES, CELLS), BF16),
            pltpu.VMEM((CHAN, WIDE), F32),
            pltpu.VMEM((CHAN, WIDE), BF16),
            pltpu.VMEM((CHAN, WIDE), BF16),
            pltpu.VMEM((CLAT + 2, 64, WIDE), F32),
            pltpu.VMEM((CLAT + 2, 64, WIDE), F32),
            pltpu.VMEM((2, 2, CLAT, WIDE), F32),
            pltpu.VMEM((2, 2, CLAT, WIDE), F32),
            pltpu.VMEM((2, 2, CLON, WIDE), F32),
            pltpu.VMEM((ROWS * CLON, CHAN), BF16),
            pltpu.VMEM((ROWS * CLON, CHAN), BF16),
            pltpu.VMEM((RIM, CHAN), F32),
            pltpu.VMEM((CLAT, CLON, CHAN), F32),
            pltpu.VMEM((CLAT, CLON, 128), F32),
            pltpu.VMEM((SIDE, 1, 128), F32),
            pltpu.VMEM((SIDE, 1, 128), F32),
            pltpu.VMEM((1, 128), F32),
            pltpu.VMEM((SIDE, 1, 128), F32),
            pltpu.SemaphoreType.REGULAR,
            pltpu.SemaphoreType.DMA((2,)),
            pltpu.SemaphoreType.DMA((2, SIDE)),
            pltpu.SemaphoreType.DMA((7,)),
            pltpu.SemaphoreType.DMA((2,)),
            pltpu.SemaphoreType.DMA((2,)),
            pltpu.SemaphoreType.DMA((2, 4)),
            pltpu.SemaphoreType.DMA((2, 4)),
            pltpu.SemaphoreType.DMA((2,)),
            pltpu.SemaphoreType.DMA((2,)),
            pltpu.SemaphoreType.DMA((1,)),
        ],
        compiler_params=pltpu.CompilerParams(
            collective_id=0, has_side_effects=True, vmem_limit_bytes=56 << 20
        ),
        name="window",
    )(
        adjoint_in,
        winds,
        vert_mix,
        level_weights,
        jnp.transpose(snd_weights[0, 0], (1, 2, 0)),
        jnp.transpose(snd_columns[0, 0], (1, 0)),
        snd_counts[0],
        basis.reshape(CELLS, DEVICES),
        owner.reshape(1, DEVICES),
    )
    return pl.pallas_call(
        deliver_kernel,
        out_shape=(
            jax.ShapeDtypeStruct((CLAT, CLON, CHAN), F32),
            jax.ShapeDtypeStruct((1, 1, TRACERS), F32),
        ),
        in_specs=[anywhere, vmem],
        out_specs=(anywhere, vmem),
        scratch_shapes=[pltpu.VMEM((CLAT, CLON, CHAN), F32), pltpu.SemaphoreType.DMA((2, 4))],
        compiler_params=pltpu.CompilerParams(vmem_limit_bytes=56 << 20),
        name="deliver",
    )(state, grad)


def solution(mesh):
    return jax.shard_map(
        body,
        mesh=mesh,
        in_specs=(
            P("lat", "lon", None),
            P("lat", "lon", None),
            P(),
            P(),
            P("lat", "lon", None, None, None),
            P("lat", "lon", None, None),
            P("lat", "lon", None),
            P("lat", "lon", None),
            P(),
        ),
        out_specs=(P("lat", "lon", None), P(("lat", "lon"), None, None)),
        check_vma=False,
    )
```

```python
import jax
import jax.numpy as jnp
from jax import lax
from jax.experimental import pallas as pl
from jax.experimental.pallas import tpu as pltpu
from jax.sharding import PartitionSpec as P

diffusion = 0.05
MESH = pl.DeviceIdType.MESH
BF16 = jnp.bfloat16
F32 = jnp.float32
DEVICES = 256
SIDE = 16
SLOTS = 16
CLAT, CLON = 24, 48
CELLS = CLAT * CLON
CHAN = 288
WIDE = 384
LEV = 72
TRACERS = 4
BAND = 8
LAG = 2
ROWS = 11
RIM = 2 * CLAT + 2 * CLON


def flip(index, by):
    return sum(((index // k) % 2 + (by // k) % 2) % 2 * k for k in (8, 4, 2, 1))


def along(b, lon_off):
    p, f, e = lon_off // 4, (lon_off // 2) % 2, lon_off % 2
    dz = jnp.where(p == 0, 4 * f, jnp.where(e == 0, p, 8 - p))
    f = jnp.where(p == 0, e, f)
    return (b // 8 + f) % 2 * 8 + (b % 8 + dz) % 8


def iota(shape, dim):
    return lax.broadcasted_iota(jnp.int32, shape, dim)


def split(value):
    high = value.astype(BF16)
    return high, (value - high.astype(F32)).astype(BF16)


def dot(x, y):
    return jnp.dot(x, y, preferred_element_type=F32)


def window_kernel(
    adj, winds, mix, lweights, w, columns, counts, basis, owner,
    out, grad,
    w_v, f0, f1, fr, wbuf, rbuf, kbuf, kin, kmid, recv, recr, reck, stage, rhs,
    adj_v, winds_v, coef, coef_rim, basis_v, base_hi, base_lo, mat, mat_hi, mat_lo,
    cur, nxt, col_out, col_in, row_in, mh, ml, rim, ring, ring_coef, ring_hi, ring_lo, out_v, sens, gsend, gin, grow, gfin,
    winds_col, basis_col, near_winds_col, near_basis_col, near_winds_row, near_basis_row,
    pair_sem, ns_sem, nr_sem, ssem, rsem, lsem, ks_sem, kr_sem, hs_sem, hr_sem, gs_sem, gr_sem, out_sem,
):
    a = lax.axis_index("lat")
    b = lax.axis_index("lon")
    me = a * SIDE + b
    bar = pltpu.get_barrier_semaphore()

    def greet(i, _):
        pl.semaphore_signal(bar, inc=1, device_id=((a + i) % SIDE, b), device_id_type=MESH)
        pl.semaphore_signal(bar, inc=1, device_id=(a, (b + i) % SIDE), device_id_type=MESH)
        return 0

    halves = [a // 8, 1 - a // 8]
    loads = []
    for n, h in enumerate(halves):
        lanes = pl.ds(pl.multiple_of(128 * h, 128), 128)
        for q in range(2):
            eight = pl.ds(8 * q, 8)
            loads.append(pltpu.make_async_copy(w.at[eight, :, lanes], w_v.at[n, eight], lsem.at[2 * n + q]))
    for load in loads:
        load.start()
    lax.fori_loop(1, SIDE, greet, 0)
    loads.append(pltpu.make_async_copy(adj, adj_v, lsem.at[4]))
    loads.append(pltpu.make_async_copy(winds, winds_v, lsem.at[5]))
    loads.append(pltpu.make_async_copy(basis, basis_v, lsem.at[6]))
    for load in loads[4:]:
        load.start()

    def copy_to(src, dst, send_sem, recv_sem, ta, tb):
        return pltpu.make_async_remote_copy(
            src_ref=src, dst_ref=dst, send_sem=send_sem, recv_sem=recv_sem, device_id=(ta, tb), device_id_type=MESH
        )

    slot = iota((SLOTS, DEVICES), 0)
    where = jnp.where(slot < counts[...], columns[...], -1)
    place = flip(a, iota((1, DEVICES), 1) // SIDE) % 8
    placed = jnp.where(iota((128, DEVICES), 0) // SLOTS == place, jnp.concatenate([where] * 8, axis=0), 0)
    for h in range(2):
        kbuf[128 * h : 128 * h + 128, :] = placed[:, 128 * h : 128 * h + 128].T

    def prepare(n):
        h = halves[n]
        for q in range(2):
            loads[2 * n + q].wait()
            for s in range(8 * q, 8 * q + 8):
                for c, dst in ((0, f0), (1, f1)):
                    block = w_v[n, s, 128 * c : 128 * c + 128, :]
                    dst[pl.ds(s, 128, stride=SLOTS), :] = block.astype(F32).T
        for r in range(4):
            pieces = [w_v[n, 4 * g + r, 256:288, :] for g in range(4)]
            block = jnp.concatenate([p.astype(F32) for p in pieces], axis=0)
            fr[pl.ds(r, 128, stride=4), :] = block.T

        def pack(i, _):
            first = 128 * h + 8 * i
            rows = pl.ds(pl.multiple_of(128 * i, 128), 128)
            wbuf[pl.ds(first, 8), :, 0:128] = f0[rows, :].astype(BF16).reshape(8, SLOTS, 128)
            wbuf[pl.ds(first, 8), :, 128:256] = f1[rows, :].astype(BF16).reshape(8, SLOTS, 128)
            four = fr[pl.ds(pl.multiple_of(32 * i, 32), 32), :]
            rbuf[pl.ds(first, 8)] = four.reshape(8, 4, 128).astype(BF16)
            return 0

        lax.fori_loop(0, 16, pack, 0, unroll=4)

    def send(lat_off, lon_off):
        ta, tb = flip(a, lat_off), along(b, lon_off)
        d = ta * SIDE + tb
        i = lon_off * SIDE + lat_off
        for n, (src, dst) in enumerate(((wbuf, recv), (rbuf, recr))):
            copy_to(src.at[d], dst.at[i], ssem.at[n], rsem.at[n, lon_off], ta, tb).start()

    def send_lat(lat_off, _):
        send(lat_off, 0)
        return 0

    def send_lon(lon_off, _):
        send(0, lon_off)
        return 0

    prepare(0)
    pl.semaphore_wait(bar, 2 * (SIDE - 1))

    def ready(i, _):
        pl.semaphore_signal(pair_sem, inc=1, device_id=(a, (b + i) % SIDE), device_id_type=MESH)
        return 0

    lax.fori_loop(1, SIDE, ready, 0)

    def send_columns(lat_off, _):
        ta = flip(a, lat_off)
        src = kbuf.at[pl.ds(pl.multiple_of(ta * SIDE, SIDE), SIDE)]
        copy_to(src, kin.at[lat_off], ks_sem.at[0], kr_sem.at[0], ta, b).start()
        return 0

    lax.fori_loop(1, SIDE, send_columns, 0)
    lax.fori_loop(1, SIDE, send_lon, 0)
    lax.fori_loop(1, 8, send_lat, 0)
    prepare(1)
    lax.fori_loop(8, SIDE, send_lat, 0)
    own = [
        pltpu.make_async_copy(wbuf.at[me], recv.at[0], rsem.at[0, 0]),
        pltpu.make_async_copy(rbuf.at[me], recr.at[0], rsem.at[1, 0]),
    ]
    for copy in own:
        copy.start()

    def pair_of(t):
        near = 2 * (3 - (t - 1) // 2) + (t - 1) % 2
        return jnp.where(t == 0, 1, jnp.where(t == 7, 0, near))

    def send_pair(t):
        first = 2 * pair_of(t)

        def both(i, _):
            lat_off = SIDE - i

            @pl.when(first > 0)
            def _():
                send(lat_off, first)

            send(lat_off, first + 1)
            return 0

        lax.fori_loop(1, SIDE, both, 0)

    pl.semaphore_wait(pair_sem, SIDE - 1)
    send_pair(0)

    landed = kin.at[pl.ds(1, SIDE - 1)]
    pltpu.make_async_copy(landed, landed, kr_sem.at[0]).wait()
    low = kbuf[pl.ds(pl.multiple_of(a * SIDE, SIDE), SIDE), :]
    high = kin[8]
    for i in range(1, 8):
        low = low + kin[i]
        high = high + kin[8 + i]
    kmid[:, 0, 0:128] = low
    kmid[:, 0, 128:256] = high
    reck[0] = kmid[b]

    def send_rows(lon_off, _):
        tb = along(b, lon_off)
        copy_to(kmid.at[tb], reck.at[lon_off], ks_sem.at[1], kr_sem.at[1], a, tb).start()
        return 0

    lax.fori_loop(1, SIDE, send_rows, 0)
    send_pair(1)

    mat[...] = jnp.zeros_like(mat)
    for t in range(TRACERS):
        mat[LEV * t : LEV * t + LEV, LEV * t : LEV * t + LEV] = mix[...]
    gain = jnp.sum(mat[:, 0:CHAN] * lweights[...].reshape(1, CHAN), axis=1, keepdims=True)
    lane = iota((CHAN, WIDE - CHAN), 1)
    extra = (iota((CHAN, WIDE - CHAN), 0) // LEV == lane % TRACERS) & (lane < TRACERS * SIDE)
    mat[:, CHAN:WIDE] = jnp.where(extra, gain, 0.0)
    mat_hi[...], mat_lo[...] = split(mat[...])

    loads[6].wait()
    pick = jnp.where(iota((DEVICES, DEVICES), 0) == owner[...], 1.0, 0.0).astype(BF16)

    def by_owner(piece):
        turned = lax.dot_general(pick, piece, (((1,), (1,)), ((), ())), preferred_element_type=F32)
        return turned.astype(BF16)

    for c in range(CLAT // BAND):
        high, low = split(basis_v[BAND * c : BAND * c + BAND].reshape(BAND * CLON, DEVICES))
        base_hi[:, BAND * CLON * c : BAND * CLON * (c + 1)] = by_owner(high)
        base_lo[:, BAND * CLON * c : BAND * CLON * (c + 1)] = by_owner(low)

    loads[4].wait()
    loads[5].wait()

    for n, x in enumerate((CLON - 1, 0)):
        winds_col[n] = winds_v[:, x, 0:LEV]
        basis_col[n] = basis_v[:, x, :]
    lon_near = []
    lat_near = []
    for n, (r, tb, ta) in enumerate((
        (CLAT - 1, (b + 1) % SIDE, (a + 1) % SIDE),
        (0, (b + SIDE - 1) % SIDE, (a + SIDE - 1) % SIDE),
    )):
        for k, (col, row, col_in_, row_in_) in enumerate((
            (winds_col, winds_v, near_winds_col, near_winds_row),
            (basis_col, basis_v, near_basis_col, near_basis_row),
        )):
            lon_near.append(copy_to(col.at[n], col_in_.at[n], ns_sem.at[k, n], nr_sem.at[k, n], a, tb))
            lat_near.append((n, copy_to(row.at[r], row_in_.at[n], ns_sem.at[k, 2 + n], nr_sem.at[k, 2 + n], ta, b)))
    for copy in lon_near:
        copy.start()
    first_band, last_band = a == 0, a == SIDE - 1
    for n, copy in lat_near:
        @pl.when(jnp.logical_not(last_band if n == 0 else first_band))
        def _():
            copy.start()

    for n, none in ((0, first_band), (1, last_band)):
        @pl.when(none)
        def _():
            near_winds_row[n] = jnp.zeros((CLON, 2 * LEV), F32)
            near_basis_row[n] = jnp.zeros((CLON, DEVICES), F32)
            row_in[0, n] = jnp.zeros((CLON, WIDE), F32)
            row_in[1, n] = jnp.zeros((CLON, WIDE), F32)

    def clear(r, _):
        cur[r] = jnp.zeros((64, WIDE), F32)
        nxt[r] = jnp.zeros((64, WIDE), F32)
        return 0

    lax.fori_loop(0, CLAT + 2, clear, 0)

    def begin(r, _):
        cur[r + 1, 8:56, 0:CHAN] = adj_v[r]
        return 0

    lax.fori_loop(0, CLAT, begin, 0)

    def coefficients(r):
        both = winds_v[r]
        u = jnp.concatenate([both[:, 0:LEV]] * TRACERS, axis=1)
        v = jnp.concatenate([both[:, LEV : 2 * LEV]] * TRACERS, axis=1)
        east = jnp.maximum(u, 0.0) + diffusion
        west = jnp.maximum(-u, 0.0) + diffusion
        north = jnp.maximum(v, 0.0) + diffusion
        south = jnp.maximum(-v, 0.0) + diffusion
        coef[0, r] = 1.0 - ((east + west) + (north + south))
        coef[1, r] = east
        coef[2, r] = west
        coef[3, r] = north
        coef[4, r] = south

    rows = iota((DEVICES, 64), 0)
    lanes = iota((DEVICES, 64), 1)
    spread = jnp.where((rows // 16 == lanes // 4) & (rows % 4 == lanes % 4), 1.0, 0.0).astype(BF16)
    rows = iota((DEVICES, 128), 0)
    lanes = iota((DEVICES, 128), 1)
    keep = jnp.where((rows // 4) % 4 == lanes // 32, 1.0, 0.0)
    rows = iota((128, 128), 0)
    lanes = iota((128, 128), 1)
    fold = jnp.where(rows % 32 == lanes, 1.0, 0.0).astype(BF16)

    def absorb(g):
        first = g * SIDE
        for n, buf in enumerate((recv, recr)):
            piece = buf.at[pl.ds(first, SIDE)]
            pltpu.make_async_copy(piece, piece, rsem.at[n, g]).wait()
        rhs[:, 0:256] = recv[pl.ds(first, SIDE)].reshape(256, 256)
        for m in range(SIDE):
            stage[4 * m : 4 * m + 4, :] = recr[first + m].astype(F32)
        wide = (dot(spread, stage[...].astype(BF16)) * keep).astype(BF16)
        rhs[:, 256:384] = dot(wide, fold).astype(BF16)
        spot = reck[g]
        for c in range(CLAT // BAND):
            ids = iota((BAND * CLON, 256), 0) + c * BAND * CLON
            table = jnp.where(ids == spot, 1.0, 0.0).astype(BF16)
            cur[c * BAND + 1 : (c + 1) * BAND + 1, 8:56, :] += dot(table, rhs[...]).reshape(BAND, CLON, WIDE)

    coming = reck.at[pl.ds(1, SIDE - 1)]
    pltpu.make_async_copy(coming, coming, kr_sem.at[1]).wait()

    def turn(t, _):
        @pl.when(t < 8)
        def _():
            send_pair(t)

        @pl.when(t < 8)
        def _():
            for i in range(4):
                coefficients(4 * (t - 2) + i)

        first = 2 * pair_of(t - LAG)
        absorb(first)
        absorb(first + 1)
        return 0

    lax.fori_loop(LAG, 8, turn, 0)
    for k in range(5):
        coef_rim[k, 0:CLAT, :] = coef[k, :, 0, :]
        coef_rim[k, CLAT : 2 * CLAT, :] = coef[k, :, CLON - 1, :]

    for copy in lon_near:
        copy.wait_recv()
    for n, copy in lat_near:
        @pl.when(jnp.logical_not(first_band if n == 0 else last_band))
        def _():
            copy.wait_recv()

    def inflow(wind):
        return jnp.concatenate([jnp.maximum(wind, 0.0) + diffusion] * TRACERS, axis=1)

    ring_coef[0:CLAT, :] = inflow(near_winds_col[0])
    ring_coef[CLAT : 2 * CLAT, :] = inflow(-near_winds_col[1])
    ring_coef[2 * CLAT : 2 * CLAT + CLON, :] = inflow(near_winds_row[0][:, LEV : 2 * LEV])
    ring_coef[2 * CLAT + CLON : RIM, :] = inflow(-near_winds_row[1][:, LEV : 2 * LEV])
    ring_basis = jnp.concatenate([near_basis_col[0], near_basis_col[1], near_basis_row[0], near_basis_row[1]], axis=0)
    high, low = split(ring_basis)
    ring_hi[...] = by_owner(high)
    ring_lo[...] = by_owner(low)

    absorb(0)
    last = 2 * pair_of(6)

    def last_turns(g, _):
        absorb(jnp.where(g == 2, 1, last + g))
        return 0

    lax.fori_loop(0, 3, last_turns, 0)

    def halo(buf, e):
        north = copy_to(buf.at[CLAT, 8:56, :], row_in.at[e, 0], hs_sem.at[e, 0], hr_sem.at[e, 0], (a + 1) % SIDE, b)
        south = copy_to(buf.at[1, 8:56, :], row_in.at[e, 1], hs_sem.at[e, 1], hr_sem.at[e, 1], (a + SIDE - 1) % SIDE, b)
        east = copy_to(col_out.at[e, 0], col_in.at[e, 0], hs_sem.at[e, 2], hr_sem.at[e, 2], a, (b + 1) % SIDE)
        west = copy_to(col_out.at[e, 1], col_in.at[e, 1], hs_sem.at[e, 3], hr_sem.at[e, 3], a, (b + SIDE - 1) % SIDE)

        @pl.when(a < SIDE - 1)
        def _():
            north.start()

        @pl.when(a > 0)
        def _():
            south.start()

        east.start()
        west.start()
        return north, south, east, west

    def arrive(copies):
        north, south, east, west = copies

        @pl.when(a > 0)
        def _():
            north.wait_recv()

        @pl.when(a < SIDE - 1)
        def _():
            south.wait_recv()

        east.wait_recv()
        west.wait_recv()

    def finish(copies):
        north, south, east, west = copies

        @pl.when(a < SIDE - 1)
        def _():
            north.wait_send()

        @pl.when(a > 0)
        def _():
            south.wait_send()

        east.wait_send()
        west.wait_send()

    def blend(weights, values):
        m = weights[0] * values[0]
        for k in range(1, 5):
            m = m + weights[k] * values[k]
        return m

    def mixed(high, low, to, start=0):
        return dot(high, mat_hi[:, start:to]) + dot(low, mat_hi[:, start:to]) + dot(high, mat_lo[:, start:to])

    def inner(buf, c, width):
        for k in range(ROWS):
            r = 1 + c * ROWS + k
            m = blend(
                [coef[n, r] for n in range(5)],
                [buf[r + 1, 8:56, 0:CHAN], buf[r + 1, 9:57, 0:CHAN], buf[r + 1, 7:55, 0:CHAN],
                 buf[r + 2, 8:56, 0:CHAN], buf[r, 8:56, 0:CHAN]],
            )
            mh[k * CLON : (k + 1) * CLON, :], ml[k * CLON : (k + 1) * CLON, :] = split(m)
        return mixed(mh[...], ml[...], width)

    def rim_inside(buf):
        for n, x in enumerate((8, 55)):
            span = slice(n * CLAT, (n + 1) * CLAT)
            rim[span, :] = blend(
                [coef_rim[k, span, :] for k in range(5)],
                [buf[1 : CLAT + 1, x, 0:CHAN], buf[1 : CLAT + 1, x + 1, 0:CHAN], buf[1 : CLAT + 1, x - 1, 0:CHAN],
                 buf[2 : CLAT + 2, x, 0:CHAN], buf[0:CLAT, x, 0:CHAN]],
            )
        for n, r in enumerate((0, CLAT - 1)):
            rim[2 * CLAT + n * CLON : 2 * CLAT + (n + 1) * CLON, :] = blend(
                [coef[k, r] for k in range(5)],
                [buf[r + 1, 8:56, 0:CHAN], buf[r + 1, 9:57, 0:CHAN], buf[r + 1, 7:55, 0:CHAN],
                 buf[r + 2, 8:56, 0:CHAN], buf[r, 8:56, 0:CHAN]],
            )

        for r, k, edge in ((0, 4, first_band), (CLAT - 1, 3, last_band)):
            @pl.when(edge)
            def _():
                n = min(r, 1)
                rim[2 * CLAT + n * CLON : 2 * CLAT + (n + 1) * CLON, :] += coef[k, r] * buf[r + 1, 8:56, 0:CHAN]
                for i, x in ((r, 8), (CLAT + r, 55)):
                    rim[i : i + 1, :] += coef_rim[k, i : i + 1, :] * buf[r + 1, x : x + 1, 0:CHAN]

    def rim_beyond(e, width):
        rim[0:CLAT, :] += coef_rim[2, 0:CLAT, :] * col_in[e, 0, :, 0:CHAN]
        rim[CLAT : 2 * CLAT, :] += coef_rim[1, CLAT : 2 * CLAT, :] * col_in[e, 1, :, 0:CHAN]
        for n, r, k in ((0, 0, 4), (1, CLAT - 1, 3)):
            rim[2 * CLAT + n * CLON : 2 * CLAT + (n + 1) * CLON, :] += coef[k, r] * row_in[e, n, :, 0:CHAN]
            for i, x in ((r, 0), (CLAT + r, CLON - 1)):
                rim[i : i + 1, :] += coef_rim[k, i : i + 1, :] * row_in[e, n, x : x + 1, 0:CHAN]
        return mixed(*split(rim[...]), width)

    col_out[0, 0, :, 0:CHAN] = cur[1 : CLAT + 1, 55, 0:CHAN]
    col_out[0, 1, :, 0:CHAN] = cur[1 : CLAT + 1, 8, 0:CHAN]
    one = halo(cur, 0)

    def inner_one(c, _):
        res = inner(cur, c, CHAN).reshape(ROWS, CLON, CHAN)
        nxt[pl.ds(c * ROWS + 2, ROWS), 8:56, 0:CHAN] = res
        return 0

    lax.fori_loop(0, 2, inner_one, 0)
    rim_inside(cur)
    arrive(one)
    res = rim_beyond(0, CHAN)
    nxt[1, 8:56, 0:CHAN] = res[2 * CLAT : 2 * CLAT + CLON]
    nxt[CLAT, 8:56, 0:CHAN] = res[2 * CLAT + CLON : RIM]
    nxt[1 : CLAT + 1, 8, 0:CHAN] = res[0:CLAT]
    nxt[1 : CLAT + 1, 55, 0:CHAN] = res[CLAT : 2 * CLAT]
    col_out[1, 0, :, 0:CHAN] = res[CLAT : 2 * CLAT]
    col_out[1, 1, :, 0:CHAN] = res[0:CLAT]
    two = halo(nxt, 1)

    def inner_two(c, _):
        res = inner(nxt, c, WIDE)
        out_v[pl.ds(c * ROWS + 1, ROWS)] = res[:, 0:CHAN].reshape(ROWS, CLON, CHAN)
        sens[pl.ds(c * ROWS + 1, ROWS)] = res[:, 256:WIDE].reshape(ROWS, CLON, 128)
        return 0

    lax.fori_loop(0, 2, inner_two, 0)
    rim_inside(nxt)
    ring[0:CLAT, :] = ring_coef[0:CLAT, :] * nxt[1 : CLAT + 1, 8, 0:CHAN]
    ring[CLAT : 2 * CLAT, :] = ring_coef[CLAT : 2 * CLAT, :] * nxt[1 : CLAT + 1, 55, 0:CHAN]
    ring[2 * CLAT : 2 * CLAT + CLON, :] = ring_coef[2 * CLAT : 2 * CLAT + CLON, :] * nxt[1, 8:56, 0:CHAN]
    ring[2 * CLAT + CLON : RIM, :] = ring_coef[2 * CLAT + CLON : RIM, :] * nxt[CLAT, 8:56, 0:CHAN]
    ends = mixed(*split(rim[2 * CLAT : RIM, :]), WIDE, 256)
    sens[0] = ends[0:CLON]
    sens[CLAT - 1] = ends[CLON : 2 * CLON]
    beyond_hi, beyond_lo = split(mixed(*split(ring[...]), WIDE, 256))

    sens_hi, sens_lo = split(sens[...].reshape(CELLS, 128))
    part = dot(base_hi[...], sens_hi) + dot(base_lo[...], sens_hi) + dot(base_hi[...], sens_lo)
    part = part + (dot(ring_hi[...], beyond_hi) + dot(ring_lo[...], beyond_hi) + dot(ring_hi[...], beyond_lo))
    rows = iota((DEVICES, 128), 0)
    lanes = iota((DEVICES, 128), 1)
    part = jnp.where((lanes // TRACERS == rows % SIDE + 8) & (lanes >= 32), part, 0.0)
    gsend[:, 0, :] = jnp.sum(part.reshape(SIDE, SIDE, 128), axis=1)

    def give_lat(i, _):
        ta = (a + i) % SIDE
        copy_to(gsend.at[ta], gin.at[i], gs_sem.at[0], gr_sem.at[0], ta, b).start()
        return 0

    lax.fori_loop(1, SIDE, give_lat, 0)
    arrive(two)
    res = rim_beyond(1, CHAN)
    out_v[0] = res[2 * CLAT : 2 * CLAT + CLON]
    out_v[CLAT - 1] = res[2 * CLAT + CLON : RIM]
    out_v[:, 0, :] = res[0:CLAT]
    out_v[:, CLON - 1, :] = res[CLAT : 2 * CLAT]
    leave = pltpu.make_async_copy(out_v, out, out_sem.at[0])
    leave.start()
    got = gsend[a]
    lat_in = gin.at[pl.ds(1, SIDE - 1)]
    pltpu.make_async_copy(lat_in, lat_in, gr_sem.at[0]).wait()
    for i in range(1, SIDE):
        got = got + gin[i]
    grow[...] = got

    def give_lon(i, _):
        copy_to(grow, gfin.at[i], gs_sem.at[1], gr_sem.at[1], a, (b + i) % SIDE).start()
        return 0

    lax.fori_loop(1, SIDE, give_lon, 0)
    lon_in = gfin.at[pl.ds(1, SIDE - 1)]
    pltpu.make_async_copy(lon_in, lon_in, gr_sem.at[1]).wait()
    for i in range(1, SIDE):
        got = got + gfin[i]
    lanes = iota((1, 128), 1)
    owned = jnp.zeros((1, TRACERS), F32)
    for t in range(TRACERS):
        value = jnp.sum(jnp.where(lanes == 32 + TRACERS * b + t, got, 0.0), axis=1, keepdims=True)
        owned = jnp.where(iota((1, TRACERS), 1) == t, value, owned)
    owned = owned * (1.0 / jnp.sqrt(jnp.full((1, TRACERS), CELLS * DEVICES, F32)))
    grad[...] = owned.reshape(1, 1, TRACERS)

    finish(one)
    finish(two)
    for copy in lon_near:
        copy.wait_send()
    for n, copy in lat_near:
        @pl.when(jnp.logical_not(last_band if n == 0 else first_band))
        def _():
            copy.wait_send()

    leave.wait()
    for piece, sem in ((landed, ks_sem.at[0]), (coming, ks_sem.at[1]), (lat_in, gs_sem.at[0]), (lon_in, gs_sem.at[1])):
        pltpu.make_async_copy(piece, piece, sem).wait()
    for n, buf in enumerate((recv, recr)):
        piece = buf.at[pl.ds(1, DEVICES - 1)]
        pltpu.make_async_copy(piece, piece, ssem.at[n]).wait()


def deliver_kernel(state, grad, state_out, grad_out, held, small, sems):
    parts = 4
    rows = CLAT // parts
    reads = [pltpu.make_async_copy(grad, small, sems.at[0, parts])]
    writes = [pltpu.make_async_copy(small, grad_out, sems.at[1, parts])]
    for i in range(parts):
        span = pl.ds(i * rows, rows)
        reads.append(pltpu.make_async_copy(state.at[span], held.at[span], sems.at[0, i]))
        writes.append(pltpu.make_async_copy(held.at[span], state_out.at[span], sems.at[1, i]))
    for read in reads:
        read.start()
    for read, write in zip(reads, writes):
        read.wait()
        write.start()
    for write in writes:
        write.wait()


def body(
    adjoint_in, winds, vert_mix, level_weights, snd_weights, snd_columns, snd_counts, basis, owner
):
    anywhere = pl.BlockSpec(memory_space=pl.ANY)
    vmem = pl.BlockSpec(memory_space=pltpu.VMEM)
    state, grad = pl.pallas_call(
        window_kernel,
        out_shape=(
            jax.ShapeDtypeStruct((CLAT, CLON, CHAN), F32),
            jax.ShapeDtypeStruct((1, 1, TRACERS), F32),
        ),
        in_specs=[anywhere, anywhere, vmem, vmem, anywhere, vmem, vmem, anywhere, vmem],
        out_specs=(anywhere, vmem),
        scratch_shapes=[
            pltpu.VMEM((2, SLOTS, CHAN, 128), BF16),
            pltpu.VMEM((128 * SLOTS, 128), F32),
            pltpu.VMEM((128 * SLOTS, 128), F32),
            pltpu.VMEM((128 * 4, 128), F32),
            pltpu.VMEM((DEVICES, SLOTS, 256), BF16),
            pltpu.VMEM((DEVICES, 4, 128), BF16),
            pltpu.VMEM((DEVICES, 128), jnp.int32),
            pltpu.VMEM((SIDE, SIDE, 128), jnp.int32),
            pltpu.VMEM((SIDE, 1, 256), jnp.int32),
            pltpu.VMEM((DEVICES, SLOTS, 256), BF16),
            pltpu.VMEM((DEVICES, 4, 128), BF16),
            pltpu.VMEM((SIDE, 1, 256), jnp.int32),
            pltpu.VMEM((64, 128), F32),
            pltpu.VMEM((256, WIDE), BF16),
            pltpu.VMEM((CLAT, CLON, CHAN), F32),
            pltpu.VMEM((CLAT, CLON, 2 * LEV), F32),
            pltpu.VMEM((5, CLAT, CLON, CHAN), F32),
            pltpu.VMEM((5, 2 * CLAT, CHAN), F32),
            pltpu.VMEM((CLAT, CLON, DEVICES), F32),
            pltpu.VMEM((DEVICES, CELLS), BF16),
            pltpu.VMEM((DEVICES, CELLS), BF16),
            pltpu.VMEM((CHAN, WIDE), F32),
            pltpu.VMEM((CHAN, WIDE), BF16),
            pltpu.VMEM((CHAN, WIDE), BF16),
            pltpu.VMEM((CLAT + 2, 64, WIDE), F32),
            pltpu.VMEM((CLAT + 2, 64, WIDE), F32),
            pltpu.VMEM((2, 2, CLAT, WIDE), F32),
            pltpu.VMEM((2, 2, CLAT, WIDE), F32),
            pltpu.VMEM((2, 2, CLON, WIDE), F32),
            pltpu.VMEM((ROWS * CLON, CHAN), BF16),
            pltpu.VMEM((ROWS * CLON, CHAN), BF16),
            pltpu.VMEM((RIM, CHAN), F32),
            pltpu.VMEM((RIM, CHAN), F32),
            pltpu.VMEM((RIM, CHAN), F32),
            pltpu.VMEM((DEVICES, RIM), BF16),
            pltpu.VMEM((DEVICES, RIM), BF16),
            pltpu.VMEM((CLAT, CLON, CHAN), F32),
            pltpu.VMEM((CLAT, CLON, 128), F32),
            pltpu.VMEM((SIDE, 1, 128), F32),
            pltpu.VMEM((SIDE, 1, 128), F32),
            pltpu.VMEM((1, 128), F32),
            pltpu.VMEM((SIDE, 1, 128), F32),
            pltpu.VMEM((2, CLAT, LEV), F32),
            pltpu.VMEM((2, CLAT, DEVICES), F32),
            pltpu.VMEM((2, CLAT, LEV), F32),
            pltpu.VMEM((2, CLAT, DEVICES), F32),
            pltpu.VMEM((2, CLON, 2 * LEV), F32),
            pltpu.VMEM((2, CLON, DEVICES), F32),
            pltpu.SemaphoreType.REGULAR,
            pltpu.SemaphoreType.DMA((2, 4)),
            pltpu.SemaphoreType.DMA((2, 4)),
            pltpu.SemaphoreType.DMA((2,)),
            pltpu.SemaphoreType.DMA((2, SIDE)),
            pltpu.SemaphoreType.DMA((7,)),
            pltpu.SemaphoreType.DMA((2,)),
            pltpu.SemaphoreType.DMA((2,)),
            pltpu.SemaphoreType.DMA((2, 4)),
            pltpu.SemaphoreType.DMA((2, 4)),
            pltpu.SemaphoreType.DMA((2,)),
            pltpu.SemaphoreType.DMA((2,)),
            pltpu.SemaphoreType.DMA((1,)),
        ],
        compiler_params=pltpu.CompilerParams(
            collective_id=0, has_side_effects=True, vmem_limit_bytes=56 << 20
        ),
        name="window",
    )(
        adjoint_in,
        winds,
        vert_mix,
        level_weights,
        jnp.transpose(snd_weights[0, 0], (1, 2, 0)),
        jnp.transpose(snd_columns[0, 0], (1, 0)),
        snd_counts[0],
        basis,
        owner.reshape(1, DEVICES),
    )
    return pl.pallas_call(
        deliver_kernel,
        out_shape=(
            jax.ShapeDtypeStruct((CLAT, CLON, CHAN), F32),
            jax.ShapeDtypeStruct((1, 1, TRACERS), F32),
        ),
        in_specs=[anywhere, anywhere],
        out_specs=(anywhere, anywhere),
        scratch_shapes=[
            pltpu.VMEM((CLAT, CLON, CHAN), F32),
            pltpu.VMEM((1, 1, TRACERS), F32),
            pltpu.SemaphoreType.DMA((2, 5)),
        ],
        compiler_params=pltpu.CompilerParams(vmem_limit_bytes=56 << 20),
        name="deliver",
    )(state, grad)


def solution(mesh):
    return jax.shard_map(
        body,
        mesh=mesh,
        in_specs=(
            P("lat", "lon", None),
            P("lat", "lon", None),
            P(),
            P(),
            P("lat", "lon", None, None, None),
            P("lat", "lon", None, None),
            P("lat", "lon", None),
            P("lat", "lon", None),
            P(),
        ),
        out_specs=(P("lat", "lon", None), P(("lat", "lon"), None, None)),
        check_vma=False,
    )
```

```python
import jax
import jax.numpy as jnp
from jax import lax
from jax.experimental import pallas as pl
from jax.experimental.pallas import tpu as pltpu
from jax.sharding import PartitionSpec as P

diffusion = 0.05
MESH = pl.DeviceIdType.MESH
BF16 = jnp.bfloat16
F32 = jnp.float32
DEVICES = 256
SIDE = 16
SLOTS = 16
CLAT, CLON = 24, 48
CELLS = CLAT * CLON
CHAN = 288
WIDE = 384
LEV = 72
TRACERS = 4
BAND = 8
LAG = 2
ROWS = 11
RIM = 2 * CLAT + 2 * CLON


def flip(index, by):
    return sum(((index // k) % 2 + (by // k) % 2) % 2 * k for k in (8, 4, 2, 1))


def along(b, lon_off):
    p, f, e = lon_off // 4, (lon_off // 2) % 2, lon_off % 2
    dz = jnp.where(p == 0, 4 * f, jnp.where(e == 0, p, 8 - p))
    f = jnp.where(p == 0, e, f)
    return (b // 8 + f) % 2 * 8 + (b % 8 + dz) % 8


def iota(shape, dim):
    return lax.broadcasted_iota(jnp.int32, shape, dim)


def split(value):
    high = value.astype(BF16)
    return high, (value - high.astype(F32)).astype(BF16)


def dot(x, y):
    return jnp.dot(x, y, preferred_element_type=F32)


def window_kernel(
    adj, winds, mix, lweights, w, columns, counts, basis, owner,
    out, grad,
    w_v, f0, f1, fr, wbuf, rbuf, kbuf, kin, kmid, recv, recr, reck, stage, rhs,
    adj_v, winds_v, coef, coef_rim, basis_v, base_hi, base_lo, mat, mat_hi, mat_lo, mat_end,
    cur, nxt, col_out, col_in, row_in, mh, ml, rim, ring_coef, ring_hi, ring_lo, out_v, sens, gsend, gin, grow, gfin,
    winds_col, basis_col, near_winds_col, near_basis_col, near_winds_row, near_basis_row,
    pair_sem, ns_sem, nr_sem, ssem, rsem, lsem, ks_sem, kr_sem, hs_sem, hr_sem, gs_sem, gr_sem, out_sem,
):
    a = lax.axis_index("lat")
    b = lax.axis_index("lon")
    me = a * SIDE + b
    bar = pltpu.get_barrier_semaphore()

    def greet(i, _):
        pl.semaphore_signal(bar, inc=1, device_id=((a + i) % SIDE, b), device_id_type=MESH)
        pl.semaphore_signal(bar, inc=1, device_id=(a, (b + i) % SIDE), device_id_type=MESH)
        return 0

    halves = [a // 8, 1 - a // 8]
    loads = []
    for n, h in enumerate(halves):
        lanes = pl.ds(pl.multiple_of(128 * h, 128), 128)
        for q in range(2):
            eight = pl.ds(8 * q, 8)
            loads.append(pltpu.make_async_copy(w.at[eight, :, lanes], w_v.at[n, eight], lsem.at[2 * n + q]))
    for load in loads:
        load.start()
    lax.fori_loop(1, SIDE, greet, 0)
    loads.append(pltpu.make_async_copy(adj, adj_v, lsem.at[4]))
    loads.append(pltpu.make_async_copy(winds, winds_v, lsem.at[5]))
    loads.append(pltpu.make_async_copy(basis, basis_v, lsem.at[6]))
    for load in loads[4:]:
        load.start()

    def copy_to(src, dst, send_sem, recv_sem, ta, tb):
        return pltpu.make_async_remote_copy(
            src_ref=src, dst_ref=dst, send_sem=send_sem, recv_sem=recv_sem, device_id=(ta, tb), device_id_type=MESH
        )

    slot = iota((SLOTS, DEVICES), 0)
    where = jnp.where(slot < counts[...], columns[...], -1)
    place = flip(a, iota((1, DEVICES), 1) // SIDE) % 8
    placed = jnp.where(iota((128, DEVICES), 0) // SLOTS == place, jnp.concatenate([where] * 8, axis=0), 0)
    for h in range(2):
        kbuf[128 * h : 128 * h + 128, :] = placed[:, 128 * h : 128 * h + 128].T

    def prepare(n):
        h = halves[n]
        for q in range(2):
            loads[2 * n + q].wait()
            for s in range(8 * q, 8 * q + 8):
                for c, dst in ((0, f0), (1, f1)):
                    block = w_v[n, s, 128 * c : 128 * c + 128, :]
                    dst[pl.ds(s, 128, stride=SLOTS), :] = block.astype(F32).T
        for r in range(4):
            pieces = [w_v[n, 4 * g + r, 256:288, :] for g in range(4)]
            block = jnp.concatenate([p.astype(F32) for p in pieces], axis=0)
            fr[pl.ds(r, 128, stride=4), :] = block.T

        def pack(i, _):
            first = 128 * h + 8 * i
            rows = pl.ds(pl.multiple_of(128 * i, 128), 128)
            wbuf[pl.ds(first, 8), :, 0:128] = f0[rows, :].astype(BF16).reshape(8, SLOTS, 128)
            wbuf[pl.ds(first, 8), :, 128:256] = f1[rows, :].astype(BF16).reshape(8, SLOTS, 128)
            four = fr[pl.ds(pl.multiple_of(32 * i, 32), 32), :]
            rbuf[pl.ds(first, 8)] = four.reshape(8, 4, 128).astype(BF16)
            return 0

        lax.fori_loop(0, 16, pack, 0, unroll=4)

    def send(lat_off, lon_off):
        ta, tb = flip(a, lat_off), along(b, lon_off)
        d = ta * SIDE + tb
        i = lon_off * SIDE + lat_off
        for n, (src, dst) in enumerate(((wbuf, recv), (rbuf, recr))):
            copy_to(src.at[d], dst.at[i], ssem.at[n], rsem.at[n, lon_off], ta, tb).start()

    def send_lat(lat_off, _):
        send(lat_off, 0)
        return 0

    def send_lon(lon_off, _):
        send(0, lon_off)
        return 0

    prepare(0)
    pl.semaphore_wait(bar, 2 * (SIDE - 1))

    def ready(i, _):
        pl.semaphore_signal(pair_sem, inc=1, device_id=(a, (b + i) % SIDE), device_id_type=MESH)
        return 0

    lax.fori_loop(1, SIDE, ready, 0)

    def send_columns(lat_off, _):
        ta = flip(a, lat_off)
        src = kbuf.at[pl.ds(pl.multiple_of(ta * SIDE, SIDE), SIDE)]
        copy_to(src, kin.at[lat_off], ks_sem.at[0], kr_sem.at[0], ta, b).start()
        return 0

    lax.fori_loop(1, SIDE, send_columns, 0)
    lax.fori_loop(1, SIDE, send_lon, 0)
    lax.fori_loop(1, 8, send_lat, 0)
    prepare(1)
    lax.fori_loop(8, SIDE, send_lat, 0)
    own = [
        pltpu.make_async_copy(wbuf.at[me], recv.at[0], rsem.at[0, 0]),
        pltpu.make_async_copy(rbuf.at[me], recr.at[0], rsem.at[1, 0]),
    ]
    for copy in own:
        copy.start()

    def pair_of(t):
        near = 2 * (3 - (t - 1) // 2) + (t - 1) % 2
        return jnp.where(t == 0, 1, jnp.where(t == 7, 0, near))

    def send_pair(t):
        first = 2 * pair_of(t)

        def both(i, _):
            lat_off = SIDE - i

            @pl.when(first > 0)
            def _():
                send(lat_off, first)

            send(lat_off, first + 1)
            return 0

        lax.fori_loop(1, SIDE, both, 0)

    pl.semaphore_wait(pair_sem, SIDE - 1)
    send_pair(0)

    landed = kin.at[pl.ds(1, SIDE - 1)]
    pltpu.make_async_copy(landed, landed, kr_sem.at[0]).wait()
    low = kbuf[pl.ds(pl.multiple_of(a * SIDE, SIDE), SIDE), :]
    high = kin[8]
    for i in range(1, 8):
        low = low + kin[i]
        high = high + kin[8 + i]
    kmid[:, 0, 0:128] = low
    kmid[:, 0, 128:256] = high
    reck[0] = kmid[b]

    def send_rows(lon_off, _):
        tb = along(b, lon_off)
        copy_to(kmid.at[tb], reck.at[lon_off], ks_sem.at[1], kr_sem.at[1], a, tb).start()
        return 0

    lax.fori_loop(1, SIDE, send_rows, 0)
    send_pair(1)

    mat[...] = jnp.zeros_like(mat)
    for t in range(TRACERS):
        mat[LEV * t : LEV * t + LEV, LEV * t : LEV * t + LEV] = mix[...]
    gain = jnp.sum(mat[:, 0:CHAN] * lweights[...].reshape(1, CHAN), axis=1, keepdims=True)
    lane = iota((CHAN, WIDE - CHAN), 1)
    extra = (iota((CHAN, WIDE - CHAN), 0) // LEV == lane % TRACERS) & (lane < TRACERS * SIDE)
    mat[:, CHAN:WIDE] = jnp.where(extra, gain, 0.0)
    mat_hi[...], mat_lo[...] = split(mat[:, 0:256])
    mat_end[:, 0:128], mat_end[:, 128:256] = split(mat[:, 256:WIDE])

    loads[6].wait()
    pick = jnp.where(iota((DEVICES, DEVICES), 0) == owner[...], 1.0, 0.0).astype(BF16)

    def by_owner(piece):
        turned = lax.dot_general(pick, piece, (((1,), (1,)), ((), ())), preferred_element_type=F32)
        return turned.astype(BF16)

    for c in range(CLAT // BAND):
        high, low = split(basis_v[BAND * c : BAND * c + BAND].reshape(BAND * CLON, DEVICES))
        base_hi[:, BAND * CLON * c : BAND * CLON * (c + 1)] = by_owner(high)
        base_lo[:, BAND * CLON * c : BAND * CLON * (c + 1)] = by_owner(low)

    loads[4].wait()
    loads[5].wait()

    for n, x in enumerate((CLON - 1, 0)):
        winds_col[n] = winds_v[:, x, 0:LEV]
        basis_col[n] = basis_v[:, x, :]
    lon_near = []
    lat_near = []
    for n, (r, tb, ta) in enumerate((
        (CLAT - 1, (b + 1) % SIDE, (a + 1) % SIDE),
        (0, (b + SIDE - 1) % SIDE, (a + SIDE - 1) % SIDE),
    )):
        for k, (col, row, col_in_, row_in_) in enumerate((
            (winds_col, winds_v, near_winds_col, near_winds_row),
            (basis_col, basis_v, near_basis_col, near_basis_row),
        )):
            lon_near.append(copy_to(col.at[n], col_in_.at[n], ns_sem.at[k, n], nr_sem.at[k, n], a, tb))
            lat_near.append((n, copy_to(row.at[r], row_in_.at[n], ns_sem.at[k, 2 + n], nr_sem.at[k, 2 + n], ta, b)))
    for copy in lon_near:
        copy.start()
    first_band, last_band = a == 0, a == SIDE - 1
    for n, copy in lat_near:
        @pl.when(jnp.logical_not(last_band if n == 0 else first_band))
        def _():
            copy.start()

    for n, none in ((0, first_band), (1, last_band)):
        @pl.when(none)
        def _():
            near_winds_row[n] = jnp.zeros((CLON, 2 * LEV), F32)
            near_basis_row[n] = jnp.zeros((CLON, DEVICES), F32)
            row_in[0, n] = jnp.zeros((CLON, WIDE), F32)
            row_in[1, n] = jnp.zeros((CLON, WIDE), F32)

    def clear(r, _):
        cur[r] = jnp.zeros((64, WIDE), F32)
        nxt[r] = jnp.zeros((64, WIDE), F32)
        return 0

    lax.fori_loop(0, CLAT + 2, clear, 0)

    def begin(r, _):
        cur[r + 1, 8:56, 0:CHAN] = adj_v[r]
        return 0

    lax.fori_loop(0, CLAT, begin, 0)

    def coefficients(r):
        both = winds_v[r]
        u = jnp.concatenate([both[:, 0:LEV]] * TRACERS, axis=1)
        v = jnp.concatenate([both[:, LEV : 2 * LEV]] * TRACERS, axis=1)
        east = jnp.maximum(u, 0.0) + diffusion
        west = jnp.maximum(-u, 0.0) + diffusion
        north = jnp.maximum(v, 0.0) + diffusion
        south = jnp.maximum(-v, 0.0) + diffusion
        coef[0, r] = 1.0 - ((east + west) + (north + south))
        coef[1, r] = east
        coef[2, r] = west
        coef[3, r] = north
        coef[4, r] = south

    rows = iota((DEVICES, 64), 0)
    lanes = iota((DEVICES, 64), 1)
    spread = jnp.where((rows // 16 == lanes // 4) & (rows % 4 == lanes % 4), 1.0, 0.0).astype(BF16)
    rows = iota((DEVICES, 128), 0)
    lanes = iota((DEVICES, 128), 1)
    keep = jnp.where((rows // 4) % 4 == lanes // 32, 1.0, 0.0)
    rows = iota((128, 128), 0)
    lanes = iota((128, 128), 1)
    fold = jnp.where(rows % 32 == lanes, 1.0, 0.0).astype(BF16)

    def absorb(g):
        first = g * SIDE
        for n, buf in enumerate((recv, recr)):
            piece = buf.at[pl.ds(first, SIDE)]
            pltpu.make_async_copy(piece, piece, rsem.at[n, g]).wait()
        rhs[:, 0:256] = recv[pl.ds(first, SIDE)].reshape(256, 256)
        for m in range(SIDE):
            stage[4 * m : 4 * m + 4, :] = recr[first + m].astype(F32)
        wide = (dot(spread, stage[...].astype(BF16)) * keep).astype(BF16)
        rhs[:, 256:384] = dot(wide, fold).astype(BF16)
        spot = reck[g]
        for c in range(CLAT // BAND):
            ids = iota((BAND * CLON, 256), 0) + c * BAND * CLON
            table = jnp.where(ids == spot, 1.0, 0.0).astype(BF16)
            cur[c * BAND + 1 : (c + 1) * BAND + 1, 8:56, :] += dot(table, rhs[...]).reshape(BAND, CLON, WIDE)

    coming = reck.at[pl.ds(1, SIDE - 1)]
    pltpu.make_async_copy(coming, coming, kr_sem.at[1]).wait()

    def turn(t, _):
        @pl.when(t < 8)
        def _():
            send_pair(t)

        @pl.when(t < 8)
        def _():
            for i in range(4):
                coefficients(4 * (t - 2) + i)

        first = 2 * pair_of(t - LAG)
        absorb(first)
        absorb(first + 1)
        return 0

    lax.fori_loop(LAG, 8, turn, 0)
    for k in range(5):
        coef_rim[k, 0:CLAT, :] = coef[k, :, 0, :]
        coef_rim[k, CLAT : 2 * CLAT, :] = coef[k, :, CLON - 1, :]

    for copy in lon_near:
        copy.wait_recv()
    for n, copy in lat_near:
        @pl.when(jnp.logical_not(first_band if n == 0 else last_band))
        def _():
            copy.wait_recv()

    def inflow(wind):
        return jnp.concatenate([jnp.maximum(wind, 0.0) + diffusion] * TRACERS, axis=1)

    ring_coef[0:CLAT, :] = inflow(near_winds_col[0])
    ring_coef[CLAT : 2 * CLAT, :] = inflow(-near_winds_col[1])
    ring_coef[2 * CLAT : 2 * CLAT + CLON, :] = inflow(near_winds_row[0][:, LEV : 2 * LEV])
    ring_coef[2 * CLAT + CLON : RIM, :] = inflow(-near_winds_row[1][:, LEV : 2 * LEV])
    ring_basis = jnp.concatenate([near_basis_col[0], near_basis_col[1], near_basis_row[0], near_basis_row[1]], axis=0)
    high, low = split(ring_basis)
    ring_hi[...] = by_owner(high)
    ring_lo[...] = by_owner(low)

    absorb(0)
    last = 2 * pair_of(6)

    def last_turns(g, _):
        absorb(jnp.where(g == 2, 1, last + g))
        return 0

    lax.fori_loop(0, 3, last_turns, 0)

    def halo(buf, e):
        north = copy_to(buf.at[CLAT, 8:56, :], row_in.at[e, 0], hs_sem.at[e, 0], hr_sem.at[e, 0], (a + 1) % SIDE, b)
        south = copy_to(buf.at[1, 8:56, :], row_in.at[e, 1], hs_sem.at[e, 1], hr_sem.at[e, 1], (a + SIDE - 1) % SIDE, b)
        east = copy_to(col_out.at[e, 0], col_in.at[e, 0], hs_sem.at[e, 2], hr_sem.at[e, 2], a, (b + 1) % SIDE)
        west = copy_to(col_out.at[e, 1], col_in.at[e, 1], hs_sem.at[e, 3], hr_sem.at[e, 3], a, (b + SIDE - 1) % SIDE)

        @pl.when(a < SIDE - 1)
        def _():
            north.start()

        @pl.when(a > 0)
        def _():
            south.start()

        east.start()
        west.start()
        return north, south, east, west

    def arrive(copies):
        north, south, east, west = copies

        @pl.when(a > 0)
        def _():
            north.wait_recv()

        @pl.when(a < SIDE - 1)
        def _():
            south.wait_recv()

        east.wait_recv()
        west.wait_recv()

    def finish(copies):
        north, south, east, west = copies

        @pl.when(a < SIDE - 1)
        def _():
            north.wait_send()

        @pl.when(a > 0)
        def _():
            south.wait_send()

        east.wait_send()
        west.wait_send()

    def blend(weights, values):
        m = weights[0] * values[0]
        for k in range(1, 5):
            m = m + weights[k] * values[k]
        return m

    def mixed(high, low):
        return dot(high, mat_hi[...]) + dot(low, mat_hi[...]) + dot(high, mat_lo[...])

    def mixed_end(high, low, start=0):
        both = dot(high[:, start:], mat_end[start:, :])
        return both[:, 0:128] + both[:, 128:256] + dot(low[:, start:], mat_end[start:, 0:128])

    def span_of(c):
        return pl.ds(pl.multiple_of(c * ROWS * CLON, 16), ROWS * CLON)

    def inner(buf, c):
        for k in range(ROWS):
            r = 1 + c * ROWS + k
            m = blend(
                [coef[n, r] for n in range(5)],
                [buf[r + 1, 8:56, 0:CHAN], buf[r + 1, 9:57, 0:CHAN], buf[r + 1, 7:55, 0:CHAN],
                 buf[r + 2, 8:56, 0:CHAN], buf[r, 8:56, 0:CHAN]],
            )
            rows = pl.ds(pl.multiple_of((c * ROWS + k) * CLON, 16), CLON)
            mh[rows, :], ml[rows, :] = split(m)
        return mh[span_of(c), :], ml[span_of(c), :]

    def rim_inside(buf):
        for n, x in enumerate((8, 55)):
            span = slice(n * CLAT, (n + 1) * CLAT)
            rim[span, :] = blend(
                [coef_rim[k, span, :] for k in range(5)],
                [buf[1 : CLAT + 1, x, 0:CHAN], buf[1 : CLAT + 1, x + 1, 0:CHAN], buf[1 : CLAT + 1, x - 1, 0:CHAN],
                 buf[2 : CLAT + 2, x, 0:CHAN], buf[0:CLAT, x, 0:CHAN]],
            )
        for n, r in enumerate((0, CLAT - 1)):
            rim[2 * CLAT + n * CLON : 2 * CLAT + (n + 1) * CLON, :] = blend(
                [coef[k, r] for k in range(5)],
                [buf[r + 1, 8:56, 0:CHAN], buf[r + 1, 9:57, 0:CHAN], buf[r + 1, 7:55, 0:CHAN],
                 buf[r + 2, 8:56, 0:CHAN], buf[r, 8:56, 0:CHAN]],
            )

        for r, k, edge in ((0, 4, first_band), (CLAT - 1, 3, last_band)):
            @pl.when(edge)
            def _():
                n = min(r, 1)
                rim[2 * CLAT + n * CLON : 2 * CLAT + (n + 1) * CLON, :] += coef[k, r] * buf[r + 1, 8:56, 0:CHAN]
                for i, x in ((r, 8), (CLAT + r, 55)):
                    rim[i : i + 1, :] += coef_rim[k, i : i + 1, :] * buf[r + 1, x : x + 1, 0:CHAN]

    def rim_beyond(e):
        rim[0:CLAT, :] += coef_rim[2, 0:CLAT, :] * col_in[e, 0, :, 0:CHAN]
        rim[CLAT : 2 * CLAT, :] += coef_rim[1, CLAT : 2 * CLAT, :] * col_in[e, 1, :, 0:CHAN]
        for n, r, k in ((0, 0, 4), (1, CLAT - 1, 3)):
            rim[2 * CLAT + n * CLON : 2 * CLAT + (n + 1) * CLON, :] += coef[k, r] * row_in[e, n, :, 0:CHAN]
            for i, x in ((r, 0), (CLAT + r, CLON - 1)):
                rim[i : i + 1, :] += coef_rim[k, i : i + 1, :] * row_in[e, n, x : x + 1, 0:CHAN]
        parts = split(rim[0:RIM, :])
        return (slice(0, 256), mixed(*parts)), (slice(256, CHAN), mixed_end(*parts, 128)[:, 0 : CHAN - 256])

    col_out[0, 0, :, 0:CHAN] = cur[1 : CLAT + 1, 55, 0:CHAN]
    col_out[0, 1, :, 0:CHAN] = cur[1 : CLAT + 1, 8, 0:CHAN]
    one = halo(cur, 0)

    def inner_one(c, _):
        high, low = inner(cur, c)
        rows = pl.ds(c * ROWS + 2, ROWS)
        nxt[rows, 8:56, 0:256] = mixed(high, low).reshape(ROWS, CLON, 256)
        end = mixed_end(high, low, 128)[:, 0 : CHAN - 256]
        nxt[rows, 8:56, 256:CHAN] = end.reshape(ROWS, CLON, CHAN - 256)
        return 0

    lax.fori_loop(0, 2, inner_one, 0)
    rim_inside(cur)
    arrive(one)
    for lanes, res in rim_beyond(0):
        nxt[1, 8:56, lanes] = res[2 * CLAT : 2 * CLAT + CLON]
        nxt[CLAT, 8:56, lanes] = res[2 * CLAT + CLON : RIM]
        nxt[1 : CLAT + 1, 8, lanes] = res[0:CLAT]
        nxt[1 : CLAT + 1, 55, lanes] = res[CLAT : 2 * CLAT]
        col_out[1, 0, :, lanes] = res[CLAT : 2 * CLAT]
        col_out[1, 1, :, lanes] = res[0:CLAT]
    two = halo(nxt, 1)

    def inner_sens(c, _):
        end = mixed_end(*inner(nxt, c)).reshape(ROWS, CLON, 128)
        sens[pl.ds(c * ROWS + 1, ROWS)] = end
        out_v[pl.ds(c * ROWS + 1, ROWS), :, 256:CHAN] = end[:, :, 0 : CHAN - 256]
        return 0

    lax.fori_loop(0, 2, inner_sens, 0)

    rim_inside(nxt)
    rim[RIM : RIM + CLAT, :] = ring_coef[0:CLAT, :] * nxt[1 : CLAT + 1, 8, 0:CHAN]
    rim[RIM + CLAT : RIM + 2 * CLAT, :] = ring_coef[CLAT : 2 * CLAT, :] * nxt[1 : CLAT + 1, 55, 0:CHAN]
    rim[RIM + 2 * CLAT : RIM + 2 * CLAT + CLON, :] = ring_coef[2 * CLAT : 2 * CLAT + CLON, :] * nxt[1, 8:56, 0:CHAN]
    rim[RIM + 2 * CLAT + CLON : 2 * RIM, :] = ring_coef[2 * CLAT + CLON : RIM, :] * nxt[CLAT, 8:56, 0:CHAN]
    ends = mixed_end(*split(rim[2 * CLAT : 2 * RIM, :]))
    sens[0] = ends[0:CLON]
    sens[CLAT - 1] = ends[CLON : 2 * CLON]
    beyond_hi, beyond_lo = split(ends[2 * CLON :])

    sens_hi, sens_lo = split(sens[...].reshape(CELLS, 128))
    both = dot(base_hi[...], jnp.concatenate([sens_hi, sens_lo], axis=1))
    both = both + dot(ring_hi[...], jnp.concatenate([beyond_hi, beyond_lo], axis=1))
    part = both[:, 0:128] + both[:, 128:256] + (dot(base_lo[...], sens_hi) + dot(ring_lo[...], beyond_hi))
    rows = iota((DEVICES, 128), 0)
    lanes = iota((DEVICES, 128), 1)
    part = jnp.where((lanes // TRACERS == rows % SIDE + 8) & (lanes >= 32), part, 0.0)
    gsend[:, 0, :] = jnp.sum(part.reshape(SIDE, SIDE, 128), axis=1)

    def give_lat(i, _):
        ta = (a + i) % SIDE
        copy_to(gsend.at[ta], gin.at[i], gs_sem.at[0], gr_sem.at[0], ta, b).start()
        return 0

    lax.fori_loop(1, SIDE, give_lat, 0)

    def inner_state(c, _):
        res = mixed(mh[span_of(c), :], ml[span_of(c), :])
        out_v[pl.ds(c * ROWS + 1, ROWS), :, 0:256] = res.reshape(ROWS, CLON, 256)
        return 0

    lax.fori_loop(0, 2, inner_state, 0)
    arrive(two)
    for lanes, res in rim_beyond(1):
        out_v[0, :, lanes] = res[2 * CLAT : 2 * CLAT + CLON]
        out_v[CLAT - 1, :, lanes] = res[2 * CLAT + CLON : RIM]
        out_v[:, 0, lanes] = res[0:CLAT]
        out_v[:, CLON - 1, lanes] = res[CLAT : 2 * CLAT]
    leave = pltpu.make_async_copy(out_v, out, out_sem.at[0])
    leave.start()
    got = gsend[a]
    lat_in = gin.at[pl.ds(1, SIDE - 1)]
    pltpu.make_async_copy(lat_in, lat_in, gr_sem.at[0]).wait()
    for i in range(1, SIDE):
        got = got + gin[i]
    grow[...] = got

    def give_lon(i, _):
        copy_to(grow, gfin.at[i], gs_sem.at[1], gr_sem.at[1], a, (b + i) % SIDE).start()
        return 0

    lax.fori_loop(1, SIDE, give_lon, 0)
    lon_in = gfin.at[pl.ds(1, SIDE - 1)]
    pltpu.make_async_copy(lon_in, lon_in, gr_sem.at[1]).wait()
    for i in range(1, SIDE):
        got = got + gfin[i]
    lanes = iota((1, 128), 1)
    owned = jnp.zeros((1, TRACERS), F32)
    for t in range(TRACERS):
        value = jnp.sum(jnp.where(lanes == 32 + TRACERS * b + t, got, 0.0), axis=1, keepdims=True)
        owned = jnp.where(iota((1, TRACERS), 1) == t, value, owned)
    owned = owned * (1.0 / jnp.sqrt(jnp.full((1, TRACERS), CELLS * DEVICES, F32)))
    grad[...] = owned.reshape(1, 1, TRACERS)

    finish(one)
    finish(two)
    for copy in lon_near:
        copy.wait_send()
    for n, copy in lat_near:
        @pl.when(jnp.logical_not(last_band if n == 0 else first_band))
        def _():
            copy.wait_send()

    leave.wait()
    for piece, sem in ((landed, ks_sem.at[0]), (coming, ks_sem.at[1]), (lat_in, gs_sem.at[0]), (lon_in, gs_sem.at[1])):
        pltpu.make_async_copy(piece, piece, sem).wait()
    for n, buf in enumerate((recv, recr)):
        piece = buf.at[pl.ds(1, DEVICES - 1)]
        pltpu.make_async_copy(piece, piece, ssem.at[n]).wait()


def deliver_kernel(state, grad, state_out, grad_out, held, small, sems):
    parts = 4
    rows = CLAT // parts
    reads = [pltpu.make_async_copy(grad, small, sems.at[0, parts])]
    writes = [pltpu.make_async_copy(small, grad_out, sems.at[1, parts])]
    for i in range(parts):
        span = pl.ds(i * rows, rows)
        reads.append(pltpu.make_async_copy(state.at[span], held.at[span], sems.at[0, i]))
        writes.append(pltpu.make_async_copy(held.at[span], state_out.at[span], sems.at[1, i]))
    for read in reads:
        read.start()
    for read, write in zip(reads, writes):
        read.wait()
        write.start()
    for write in writes:
        write.wait()


def body(
    adjoint_in, winds, vert_mix, level_weights, snd_weights, snd_columns, snd_counts, basis, owner
):
    anywhere = pl.BlockSpec(memory_space=pl.ANY)
    vmem = pl.BlockSpec(memory_space=pltpu.VMEM)
    state, grad = pl.pallas_call(
        window_kernel,
        out_shape=(
            jax.ShapeDtypeStruct((CLAT, CLON, CHAN), F32),
            jax.ShapeDtypeStruct((1, 1, TRACERS), F32),
        ),
        in_specs=[anywhere, anywhere, vmem, vmem, anywhere, vmem, vmem, anywhere, vmem],
        out_specs=(anywhere, vmem),
        scratch_shapes=[
            pltpu.VMEM((2, SLOTS, CHAN, 128), BF16),
            pltpu.VMEM((128 * SLOTS, 128), F32),
            pltpu.VMEM((128 * SLOTS, 128), F32),
            pltpu.VMEM((128 * 4, 128), F32),
            pltpu.VMEM((DEVICES, SLOTS, 256), BF16),
            pltpu.VMEM((DEVICES, 4, 128), BF16),
            pltpu.VMEM((DEVICES, 128), jnp.int32),
            pltpu.VMEM((SIDE, SIDE, 128), jnp.int32),
            pltpu.VMEM((SIDE, 1, 256), jnp.int32),
            pltpu.VMEM((DEVICES, SLOTS, 256), BF16),
            pltpu.VMEM((DEVICES, 4, 128), BF16),
            pltpu.VMEM((SIDE, 1, 256), jnp.int32),
            pltpu.VMEM((64, 128), F32),
            pltpu.VMEM((256, WIDE), BF16),
            pltpu.VMEM((CLAT, CLON, CHAN), F32),
            pltpu.VMEM((CLAT, CLON, 2 * LEV), F32),
            pltpu.VMEM((5, CLAT, CLON, CHAN), F32),
            pltpu.VMEM((5, 2 * CLAT, CHAN), F32),
            pltpu.VMEM((CLAT, CLON, DEVICES), F32),
            pltpu.VMEM((DEVICES, CELLS), BF16),
            pltpu.VMEM((DEVICES, CELLS), BF16),
            pltpu.VMEM((CHAN, WIDE), F32),
            pltpu.VMEM((CHAN, 256), BF16),
            pltpu.VMEM((CHAN, 256), BF16),
            pltpu.VMEM((CHAN, 256), BF16),
            pltpu.VMEM((CLAT + 2, 64, WIDE), F32),
            pltpu.VMEM((CLAT + 2, 64, WIDE), F32),
            pltpu.VMEM((2, 2, CLAT, WIDE), F32),
            pltpu.VMEM((2, 2, CLAT, WIDE), F32),
            pltpu.VMEM((2, 2, CLON, WIDE), F32),
            pltpu.VMEM((2 * ROWS * CLON, CHAN), BF16),
            pltpu.VMEM((2 * ROWS * CLON, CHAN), BF16),
            pltpu.VMEM((2 * RIM, CHAN), F32),
            pltpu.VMEM((RIM, CHAN), F32),
            pltpu.VMEM((DEVICES, RIM), BF16),
            pltpu.VMEM((DEVICES, RIM), BF16),
            pltpu.VMEM((CLAT, CLON, CHAN), F32),
            pltpu.VMEM((CLAT, CLON, 128), F32),
            pltpu.VMEM((SIDE, 1, 128), F32),
            pltpu.VMEM((SIDE, 1, 128), F32),
            pltpu.VMEM((1, 128), F32),
            pltpu.VMEM((SIDE, 1, 128), F32),
            pltpu.VMEM((2, CLAT, LEV), F32),
            pltpu.VMEM((2, CLAT, DEVICES), F32),
            pltpu.VMEM((2, CLAT, LEV), F32),
            pltpu.VMEM((2, CLAT, DEVICES), F32),
            pltpu.VMEM((2, CLON, 2 * LEV), F32),
            pltpu.VMEM((2, CLON, DEVICES), F32),
            pltpu.SemaphoreType.REGULAR,
            pltpu.SemaphoreType.DMA((2, 4)),
            pltpu.SemaphoreType.DMA((2, 4)),
            pltpu.SemaphoreType.DMA((2,)),
            pltpu.SemaphoreType.DMA((2, SIDE)),
            pltpu.SemaphoreType.DMA((7,)),
            pltpu.SemaphoreType.DMA((2,)),
            pltpu.SemaphoreType.DMA((2,)),
            pltpu.SemaphoreType.DMA((2, 4)),
            pltpu.SemaphoreType.DMA((2, 4)),
            pltpu.SemaphoreType.DMA((2,)),
            pltpu.SemaphoreType.DMA((2,)),
            pltpu.SemaphoreType.DMA((1,)),
        ],
        compiler_params=pltpu.CompilerParams(
            collective_id=0, has_side_effects=True, vmem_limit_bytes=56 << 20
        ),
        name="window",
    )(
        adjoint_in,
        winds,
        vert_mix,
        level_weights,
        jnp.transpose(snd_weights[0, 0], (1, 2, 0)),
        jnp.transpose(snd_columns[0, 0], (1, 0)),
        snd_counts[0],
        basis,
        owner.reshape(1, DEVICES),
    )
    return pl.pallas_call(
        deliver_kernel,
        out_shape=(
            jax.ShapeDtypeStruct((CLAT, CLON, CHAN), F32),
            jax.ShapeDtypeStruct((1, 1, TRACERS), F32),
        ),
        in_specs=[anywhere, anywhere],
        out_specs=(anywhere, anywhere),
        scratch_shapes=[
            pltpu.VMEM((CLAT, CLON, CHAN), F32),
            pltpu.VMEM((1, 1, TRACERS), F32),
            pltpu.SemaphoreType.DMA((2, 5)),
        ],
        compiler_params=pltpu.CompilerParams(vmem_limit_bytes=56 << 20),
        name="deliver",
    )(state, grad)


def solution(mesh):
    return jax.shard_map(
        body,
        mesh=mesh,
        in_specs=(
            P("lat", "lon", None),
            P("lat", "lon", None),
            P(),
            P(),
            P("lat", "lon", None, None, None),
            P("lat", "lon", None, None),
            P("lat", "lon", None),
            P("lat", "lon", None),
            P(),
        ),
        out_specs=(P("lat", "lon", None), P(("lat", "lon"), None, None)),
        check_vma=False,
    )
```

```python
import jax
import jax.numpy as jnp
from jax import lax
from jax.experimental import pallas as pl
from jax.experimental.pallas import tpu as pltpu
from jax.sharding import PartitionSpec as P

diffusion = 0.05
MESH = pl.DeviceIdType.MESH
BF16 = jnp.bfloat16
F32 = jnp.float32
DEVICES = 256
SIDE = 16
SLOTS = 16
CLAT, CLON = 24, 48
CELLS = CLAT * CLON
CHAN = 288
WIDE = 384
LEV = 72
TRACERS = 4
BAND = 8
LAG = 2
ROWS = 11
RIM = 2 * CLAT + 2 * CLON


FAR_LAT = (10, 6, 11, 9, 7, 5, 8, 14, 2, 13, 3, 12, 4, 15, 1)
FAR_LON = (4, 12, 3, 5, 11, 13, 2, 6, 10, 14, 1, 7, 9, 15, 8)


def flip(index, by):
    return sum(((index // k) % 2 + (by // k) % 2) % 2 * k for k in (8, 4, 2, 1))


def along(b, lon_off):
    p, f, e = lon_off // 4, (lon_off // 2) % 2, lon_off % 2
    dz = jnp.where(p == 0, 4 * f, jnp.where(e == 0, p, 8 - p))
    f = jnp.where(p == 0, e, f)
    return (b // 8 + f) % 2 * 8 + (b % 8 + dz) % 8


def iota(shape, dim):
    return lax.broadcasted_iota(jnp.int32, shape, dim)


def split(value):
    high = value.astype(BF16)
    return high, (value - high.astype(F32)).astype(BF16)


def dot(x, y):
    return jnp.dot(x, y, preferred_element_type=F32)


def window_kernel(
    adj, winds, mix, lweights, w, columns, counts, basis, owner,
    out, grad,
    w_v, f0, f1, fr, wbuf, rbuf, kbuf, kin, kmid, recv, recr, reck, stage, rhs,
    adj_v, winds_v, coef, coef_rim, basis_v, base_hi, base_lo, mat, mat_hi, mat_lo, mat_end,
    cur, nxt, col_out, col_in, row_in, mh, ml, rim, ring_coef, ring_hi, ring_lo, out_v, sens, gsend, gin, grow, gfin,
    winds_col, basis_col, near_winds_col, near_basis_col, near_winds_row, near_basis_row,
    pair_sem, ns_sem, nr_sem, ssem, rsem, lsem, ks_sem, kr_sem, hs_sem, hr_sem, gs_sem, gr_sem, out_sem,
):
    a = lax.axis_index("lat")
    b = lax.axis_index("lon")
    me = a * SIDE + b
    bar = pltpu.get_barrier_semaphore()

    halves = [a // 8, 1 - a // 8]
    loads = []
    for n, h in enumerate(halves):
        lanes = pl.ds(pl.multiple_of(128 * h, 128), 128)
        for q in range(2):
            eight = pl.ds(8 * q, 8)
            loads.append(pltpu.make_async_copy(w.at[eight, :, lanes], w_v.at[n, eight], lsem.at[2 * n + q]))
    for load in loads:
        load.start()
    for i, j in zip(FAR_LAT, FAR_LON):
        pl.semaphore_signal(bar, inc=1, device_id=(a, (b + j) % SIDE), device_id_type=MESH)
        pl.semaphore_signal(bar, inc=1, device_id=((a + i) % SIDE, b), device_id_type=MESH)
    loads.append(pltpu.make_async_copy(adj, adj_v, lsem.at[4]))
    loads.append(pltpu.make_async_copy(winds, winds_v, lsem.at[5]))
    loads.append(pltpu.make_async_copy(basis, basis_v, lsem.at[6]))
    for load in loads[4:]:
        load.start()

    def copy_to(src, dst, send_sem, recv_sem, ta, tb):
        return pltpu.make_async_remote_copy(
            src_ref=src, dst_ref=dst, send_sem=send_sem, recv_sem=recv_sem, device_id=(ta, tb), device_id_type=MESH
        )

    slot = iota((SLOTS, DEVICES), 0)
    where = jnp.where(slot < counts[...], columns[...], -1)
    place = flip(a, iota((1, DEVICES), 1) // SIDE) % 8
    placed = jnp.where(iota((128, DEVICES), 0) // SLOTS == place, jnp.concatenate([where] * 8, axis=0), 0)
    for h in range(2):
        kbuf[128 * h : 128 * h + 128, :] = placed[:, 128 * h : 128 * h + 128].T

    def prepare(n):
        h = halves[n]
        for q in range(2):
            loads[2 * n + q].wait()
            for s in range(8 * q, 8 * q + 8):
                for c, dst in ((0, f0), (1, f1)):
                    block = w_v[n, s, 128 * c : 128 * c + 128, :]
                    dst[pl.ds(s, 128, stride=SLOTS), :] = block.astype(F32).T
        for r in range(4):
            pieces = [w_v[n, 4 * g + r, 256:288, :] for g in range(4)]
            block = jnp.concatenate([p.astype(F32) for p in pieces], axis=0)
            fr[pl.ds(r, 128, stride=4), :] = block.T

        def pack(i, _):
            first = 128 * h + 8 * i
            rows = pl.ds(pl.multiple_of(128 * i, 128), 128)
            wbuf[pl.ds(first, 8), :, 0:128] = f0[rows, :].astype(BF16).reshape(8, SLOTS, 128)
            wbuf[pl.ds(first, 8), :, 128:256] = f1[rows, :].astype(BF16).reshape(8, SLOTS, 128)
            four = fr[pl.ds(pl.multiple_of(32 * i, 32), 32), :]
            rbuf[pl.ds(first, 8)] = four.reshape(8, 4, 128).astype(BF16)
            return 0

        lax.fori_loop(0, 16, pack, 0, unroll=4)

    def send(lat_off, lon_off):
        ta, tb = flip(a, lat_off), along(b, lon_off)
        d = ta * SIDE + tb
        i = lon_off * SIDE + lat_off
        for n, (src, dst) in enumerate(((wbuf, recv), (rbuf, recr))):
            copy_to(src.at[d], dst.at[i], ssem.at[n], rsem.at[n, lon_off], ta, tb).start()

    def send_lat(lat_off, _):
        send(lat_off, 0)
        return 0

    def send_lon(i, _):
        send(0, jnp.where(i <= 2, i + 1, jnp.where(i == SIDE - 1, 1, 18 - i)))
        return 0

    prepare(0)
    pl.semaphore_wait(bar, 2 * (SIDE - 1))

    for j in FAR_LON:
        pl.semaphore_signal(pair_sem, inc=1, device_id=(a, (b + j) % SIDE), device_id_type=MESH)

    def send_columns(lat_off, _):
        ta = flip(a, lat_off)
        src = kbuf.at[pl.ds(pl.multiple_of(ta * SIDE, SIDE), SIDE)]
        copy_to(src, kin.at[lat_off], ks_sem.at[0], kr_sem.at[0], ta, b).start()
        return 0

    lax.fori_loop(1, SIDE, send_lon, 0)
    lax.fori_loop(1, SIDE, send_columns, 0)
    lax.fori_loop(1, 8, send_lat, 0)
    prepare(1)
    lax.fori_loop(8, SIDE, send_lat, 0)
    own = [
        pltpu.make_async_copy(wbuf.at[me], recv.at[0], rsem.at[0, 0]),
        pltpu.make_async_copy(rbuf.at[me], recr.at[0], rsem.at[1, 0]),
    ]
    for copy in own:
        copy.start()

    def pair_of(t):
        near = 2 * (3 - (t - 1) // 2) + (t - 1) % 2
        return jnp.where(t == 0, 1, jnp.where(t == 7, 0, near))

    def send_pair(t):
        first = 2 * pair_of(t)

        def both(i, _):
            lat_off = SIDE - i

            @pl.when(first > 0)
            def _():
                send(lat_off, first)

            send(lat_off, first + 1)
            return 0

        lax.fori_loop(1, SIDE, both, 0)

    pl.semaphore_wait(pair_sem, SIDE - 1)
    send_pair(0)

    landed = kin.at[pl.ds(1, SIDE - 1)]
    pltpu.make_async_copy(landed, landed, kr_sem.at[0]).wait()
    low = kbuf[pl.ds(pl.multiple_of(a * SIDE, SIDE), SIDE), :]
    high = kin[8]
    for i in range(1, 8):
        low = low + kin[i]
        high = high + kin[8 + i]
    kmid[:, 0, 0:128] = low
    kmid[:, 0, 128:256] = high
    reck[0] = kmid[b]

    def send_rows(lon_off, _):
        tb = along(b, lon_off)
        copy_to(kmid.at[tb], reck.at[lon_off], ks_sem.at[1], kr_sem.at[1], a, tb).start()
        return 0

    lax.fori_loop(1, SIDE, send_rows, 0)
    send_pair(1)

    mat[...] = jnp.zeros_like(mat)
    for t in range(TRACERS):
        mat[LEV * t : LEV * t + LEV, LEV * t : LEV * t + LEV] = mix[...]
    gain = jnp.sum(mat[:, 0:CHAN] * lweights[...].reshape(1, CHAN), axis=1, keepdims=True)
    lane = iota((CHAN, WIDE - CHAN), 1)
    extra = (iota((CHAN, WIDE - CHAN), 0) // LEV == lane % TRACERS) & (lane < TRACERS * SIDE)
    mat[:, CHAN:WIDE] = jnp.where(extra, gain, 0.0)
    mat_hi[...], mat_lo[...] = split(mat[:, 0:256])
    mat_end[:, 0:128], mat_end[:, 128:256] = split(mat[:, 256:WIDE])

    loads[6].wait()
    pick = jnp.where(iota((DEVICES, DEVICES), 0) == owner[...], 1.0, 0.0).astype(BF16)

    def by_owner(piece):
        turned = lax.dot_general(pick, piece, (((1,), (1,)), ((), ())), preferred_element_type=F32)
        return turned.astype(BF16)

    for c in range(CLAT // BAND):
        high, low = split(basis_v[BAND * c : BAND * c + BAND].reshape(BAND * CLON, DEVICES))
        base_hi[:, BAND * CLON * c : BAND * CLON * (c + 1)] = by_owner(high)
        base_lo[:, BAND * CLON * c : BAND * CLON * (c + 1)] = by_owner(low)

    loads[4].wait()
    loads[5].wait()

    for n, x in enumerate((CLON - 1, 0)):
        winds_col[n] = winds_v[:, x, 0:LEV]
        basis_col[n] = basis_v[:, x, :]
    lon_near = []
    lat_near = []
    for n, (r, tb, ta) in enumerate((
        (CLAT - 1, (b + 1) % SIDE, (a + 1) % SIDE),
        (0, (b + SIDE - 1) % SIDE, (a + SIDE - 1) % SIDE),
    )):
        for k, (col, row, col_in_, row_in_) in enumerate((
            (winds_col, winds_v, near_winds_col, near_winds_row),
            (basis_col, basis_v, near_basis_col, near_basis_row),
        )):
            lon_near.append(copy_to(col.at[n], col_in_.at[n], ns_sem.at[k, n], nr_sem.at[k, n], a, tb))
            lat_near.append((n, copy_to(row.at[r], row_in_.at[n], ns_sem.at[k, 2 + n], nr_sem.at[k, 2 + n], ta, b)))
    for copy in lon_near:
        copy.start()
    first_band, last_band = a == 0, a == SIDE - 1
    for n, copy in lat_near:
        @pl.when(jnp.logical_not(last_band if n == 0 else first_band))
        def _():
            copy.start()

    for n, none in ((0, first_band), (1, last_band)):
        @pl.when(none)
        def _():
            near_winds_row[n] = jnp.zeros((CLON, 2 * LEV), F32)
            near_basis_row[n] = jnp.zeros((CLON, DEVICES), F32)
            row_in[0, n] = jnp.zeros((CLON, WIDE), F32)
            row_in[1, n] = jnp.zeros((CLON, WIDE), F32)

    def clear(r, _):
        cur[r] = jnp.zeros((64, WIDE), F32)
        nxt[r] = jnp.zeros((64, WIDE), F32)
        return 0

    lax.fori_loop(0, CLAT + 2, clear, 0)

    def begin(r, _):
        cur[r + 1, 8:56, 0:CHAN] = adj_v[r]
        return 0

    lax.fori_loop(0, CLAT, begin, 0)

    def coefficients(r):
        both = winds_v[r]
        u = jnp.concatenate([both[:, 0:LEV]] * TRACERS, axis=1)
        v = jnp.concatenate([both[:, LEV : 2 * LEV]] * TRACERS, axis=1)
        east = jnp.maximum(u, 0.0) + diffusion
        west = jnp.maximum(-u, 0.0) + diffusion
        north = jnp.maximum(v, 0.0) + diffusion
        south = jnp.maximum(-v, 0.0) + diffusion
        coef[0, r] = 1.0 - ((east + west) + (north + south))
        coef[1, r] = east
        coef[2, r] = west
        coef[3, r] = north
        coef[4, r] = south

    rows = iota((DEVICES, 64), 0)
    lanes = iota((DEVICES, 64), 1)
    spread = jnp.where((rows // 16 == lanes // 4) & (rows % 4 == lanes % 4), 1.0, 0.0).astype(BF16)
    rows = iota((DEVICES, 128), 0)
    lanes = iota((DEVICES, 128), 1)
    keep = jnp.where((rows // 4) % 4 == lanes // 32, 1.0, 0.0)
    rows = iota((128, 128), 0)
    lanes = iota((128, 128), 1)
    fold = jnp.where(rows % 32 == lanes, 1.0, 0.0).astype(BF16)

    def absorb(g):
        first = g * SIDE
        for n, buf in enumerate((recv, recr)):
            piece = buf.at[pl.ds(first, SIDE)]
            pltpu.make_async_copy(piece, piece, rsem.at[n, g]).wait()
        rhs[:, 0:256] = recv[pl.ds(first, SIDE)].reshape(256, 256)
        for m in range(SIDE):
            stage[4 * m : 4 * m + 4, :] = recr[first + m].astype(F32)
        wide = (dot(spread, stage[...].astype(BF16)) * keep).astype(BF16)
        rhs[:, 256:384] = dot(wide, fold).astype(BF16)
        spot = reck[g]
        for c in range(CLAT // BAND):
            ids = iota((BAND * CLON, 256), 0) + c * BAND * CLON
            table = jnp.where(ids == spot, 1.0, 0.0).astype(BF16)
            cur[c * BAND + 1 : (c + 1) * BAND + 1, 8:56, :] += dot(table, rhs[...]).reshape(BAND, CLON, WIDE)

    coming = reck.at[pl.ds(1, SIDE - 1)]
    pltpu.make_async_copy(coming, coming, kr_sem.at[1]).wait()

    def turn(t, _):
        @pl.when(t < 8)
        def _():
            send_pair(t)

        @pl.when(t < 8)
        def _():
            for i in range(4):
                coefficients(4 * (t - 2) + i)

        first = 2 * pair_of(t - LAG)
        absorb(first)
        absorb(first + 1)
        return 0

    lax.fori_loop(LAG, 8, turn, 0)
    for k in range(5):
        coef_rim[k, 0:CLAT, :] = coef[k, :, 0, :]
        coef_rim[k, CLAT : 2 * CLAT, :] = coef[k, :, CLON - 1, :]

    for copy in lon_near:
        copy.wait_recv()
    for n, copy in lat_near:
        @pl.when(jnp.logical_not(first_band if n == 0 else last_band))
        def _():
            copy.wait_recv()

    def inflow(wind):
        return jnp.concatenate([jnp.maximum(wind, 0.0) + diffusion] * TRACERS, axis=1)

    ring_coef[0:CLAT, :] = inflow(near_winds_col[0])
    ring_coef[CLAT : 2 * CLAT, :] = inflow(-near_winds_col[1])
    ring_coef[2 * CLAT : 2 * CLAT + CLON, :] = inflow(near_winds_row[0][:, LEV : 2 * LEV])
    ring_coef[2 * CLAT + CLON : RIM, :] = inflow(-near_winds_row[1][:, LEV : 2 * LEV])
    ring_basis = jnp.concatenate([near_basis_col[0], near_basis_col[1], near_basis_row[0], near_basis_row[1]], axis=0)
    high, low = split(ring_basis)
    ring_hi[...] = by_owner(high)
    ring_lo[...] = by_owner(low)

    absorb(0)
    last = 2 * pair_of(6)

    def last_turns(g, _):
        absorb(jnp.where(g == 2, 1, last + g))
        return 0

    lax.fori_loop(0, 3, last_turns, 0)

    def halo(buf, e):
        north = copy_to(buf.at[CLAT, 8:56, :], row_in.at[e, 0], hs_sem.at[e, 0], hr_sem.at[e, 0], (a + 1) % SIDE, b)
        south = copy_to(buf.at[1, 8:56, :], row_in.at[e, 1], hs_sem.at[e, 1], hr_sem.at[e, 1], (a + SIDE - 1) % SIDE, b)
        east = copy_to(col_out.at[e, 0], col_in.at[e, 0], hs_sem.at[e, 2], hr_sem.at[e, 2], a, (b + 1) % SIDE)
        west = copy_to(col_out.at[e, 1], col_in.at[e, 1], hs_sem.at[e, 3], hr_sem.at[e, 3], a, (b + SIDE - 1) % SIDE)

        @pl.when(a < SIDE - 1)
        def _():
            north.start()

        @pl.when(a > 0)
        def _():
            south.start()

        east.start()
        west.start()
        return north, south, east, west

    def arrive(copies):
        north, south, east, west = copies

        @pl.when(a > 0)
        def _():
            north.wait_recv()

        @pl.when(a < SIDE - 1)
        def _():
            south.wait_recv()

        east.wait_recv()
        west.wait_recv()

    def finish(copies):
        north, south, east, west = copies

        @pl.when(a < SIDE - 1)
        def _():
            north.wait_send()

        @pl.when(a > 0)
        def _():
            south.wait_send()

        east.wait_send()
        west.wait_send()

    def blend(weights, values):
        m = weights[0] * values[0]
        for k in range(1, 5):
            m = m + weights[k] * values[k]
        return m

    def mixed(high, low):
        return dot(high, mat_hi[...]) + dot(low, mat_hi[...]) + dot(high, mat_lo[...])

    def mixed_end(high, low, start=0):
        both = dot(high[:, start:], mat_end[start:, :])
        return both[:, 0:128] + both[:, 128:256] + dot(low[:, start:], mat_end[start:, 0:128])

    def span_of(c):
        return pl.ds(pl.multiple_of(c * ROWS * CLON, 16), ROWS * CLON)

    def inner(buf, c):
        for k in range(ROWS):
            r = 1 + c * ROWS + k
            m = blend(
                [coef[n, r] for n in range(5)],
                [buf[r + 1, 8:56, 0:CHAN], buf[r + 1, 9:57, 0:CHAN], buf[r + 1, 7:55, 0:CHAN],
                 buf[r + 2, 8:56, 0:CHAN], buf[r, 8:56, 0:CHAN]],
            )
            rows = pl.ds(pl.multiple_of((c * ROWS + k) * CLON, 16), CLON)
            mh[rows, :], ml[rows, :] = split(m)
        return mh[span_of(c), :], ml[span_of(c), :]

    def rim_inside(buf):
        for n, x in enumerate((8, 55)):
            span = slice(n * CLAT, (n + 1) * CLAT)
            rim[span, :] = blend(
                [coef_rim[k, span, :] for k in range(5)],
                [buf[1 : CLAT + 1, x, 0:CHAN], buf[1 : CLAT + 1, x + 1, 0:CHAN], buf[1 : CLAT + 1, x - 1, 0:CHAN],
                 buf[2 : CLAT + 2, x, 0:CHAN], buf[0:CLAT, x, 0:CHAN]],
            )
        for n, r in enumerate((0, CLAT - 1)):
            rim[2 * CLAT + n * CLON : 2 * CLAT + (n + 1) * CLON, :] = blend(
                [coef[k, r] for k in range(5)],
                [buf[r + 1, 8:56, 0:CHAN], buf[r + 1, 9:57, 0:CHAN], buf[r + 1, 7:55, 0:CHAN],
                 buf[r + 2, 8:56, 0:CHAN], buf[r, 8:56, 0:CHAN]],
            )

        for r, k, edge in ((0, 4, first_band), (CLAT - 1, 3, last_band)):
            @pl.when(edge)
            def _():
                n = min(r, 1)
                rim[2 * CLAT + n * CLON : 2 * CLAT + (n + 1) * CLON, :] += coef[k, r] * buf[r + 1, 8:56, 0:CHAN]
                for i, x in ((r, 8), (CLAT + r, 55)):
                    rim[i : i + 1, :] += coef_rim[k, i : i + 1, :] * buf[r + 1, x : x + 1, 0:CHAN]

    def rim_beyond(e):
        rim[0:CLAT, :] += coef_rim[2, 0:CLAT, :] * col_in[e, 0, :, 0:CHAN]
        rim[CLAT : 2 * CLAT, :] += coef_rim[1, CLAT : 2 * CLAT, :] * col_in[e, 1, :, 0:CHAN]
        for n, r, k in ((0, 0, 4), (1, CLAT - 1, 3)):
            rim[2 * CLAT + n * CLON : 2 * CLAT + (n + 1) * CLON, :] += coef[k, r] * row_in[e, n, :, 0:CHAN]
            for i, x in ((r, 0), (CLAT + r, CLON - 1)):
                rim[i : i + 1, :] += coef_rim[k, i : i + 1, :] * row_in[e, n, x : x + 1, 0:CHAN]
        parts = split(rim[0:RIM, :])
        return (slice(0, 256), mixed(*parts)), (slice(256, CHAN), mixed_end(*parts, 128)[:, 0 : CHAN - 256])

    col_out[0, 0, :, 0:CHAN] = cur[1 : CLAT + 1, 55, 0:CHAN]
    col_out[0, 1, :, 0:CHAN] = cur[1 : CLAT + 1, 8, 0:CHAN]
    one = halo(cur, 0)

    def inner_one(c, _):
        high, low = inner(cur, c)
        rows = pl.ds(c * ROWS + 2, ROWS)
        nxt[rows, 8:56, 0:256] = mixed(high, low).reshape(ROWS, CLON, 256)
        end = mixed_end(high, low, 128)[:, 0 : CHAN - 256]
        nxt[rows, 8:56, 256:CHAN] = end.reshape(ROWS, CLON, CHAN - 256)
        return 0

    lax.fori_loop(0, 2, inner_one, 0)
    rim_inside(cur)
    arrive(one)
    for lanes, res in rim_beyond(0):
        nxt[1, 8:56, lanes] = res[2 * CLAT : 2 * CLAT + CLON]
        nxt[CLAT, 8:56, lanes] = res[2 * CLAT + CLON : RIM]
        nxt[1 : CLAT + 1, 8, lanes] = res[0:CLAT]
        nxt[1 : CLAT + 1, 55, lanes] = res[CLAT : 2 * CLAT]
        col_out[1, 0, :, lanes] = res[CLAT : 2 * CLAT]
        col_out[1, 1, :, lanes] = res[0:CLAT]
    two = halo(nxt, 1)

    def inner_sens(c, _):
        end = mixed_end(*inner(nxt, c)).reshape(ROWS, CLON, 128)
        sens[pl.ds(c * ROWS + 1, ROWS)] = end
        out_v[pl.ds(c * ROWS + 1, ROWS), :, 256:CHAN] = end[:, :, 0 : CHAN - 256]
        return 0

    lax.fori_loop(0, 2, inner_sens, 0)

    rim_inside(nxt)
    rim[RIM : RIM + CLAT, :] = ring_coef[0:CLAT, :] * nxt[1 : CLAT + 1, 8, 0:CHAN]
    rim[RIM + CLAT : RIM + 2 * CLAT, :] = ring_coef[CLAT : 2 * CLAT, :] * nxt[1 : CLAT + 1, 55, 0:CHAN]
    rim[RIM + 2 * CLAT : RIM + 2 * CLAT + CLON, :] = ring_coef[2 * CLAT : 2 * CLAT + CLON, :] * nxt[1, 8:56, 0:CHAN]
    rim[RIM + 2 * CLAT + CLON : 2 * RIM, :] = ring_coef[2 * CLAT + CLON : RIM, :] * nxt[CLAT, 8:56, 0:CHAN]
    ends = mixed_end(*split(rim[2 * CLAT : 2 * RIM, :]))
    sens[0] = ends[0:CLON]
    sens[CLAT - 1] = ends[CLON : 2 * CLON]
    beyond_hi, beyond_lo = split(ends[2 * CLON :])

    sens_hi, sens_lo = split(sens[...].reshape(CELLS, 128))
    both = dot(base_hi[...], jnp.concatenate([sens_hi, sens_lo], axis=1))
    both = both + dot(ring_hi[...], jnp.concatenate([beyond_hi, beyond_lo], axis=1))
    part = both[:, 0:128] + both[:, 128:256] + (dot(base_lo[...], sens_hi) + dot(ring_lo[...], beyond_hi))
    rows = iota((DEVICES, 128), 0)
    lanes = iota((DEVICES, 128), 1)
    part = jnp.where((lanes // TRACERS == rows % SIDE + 8) & (lanes >= 32), part, 0.0)
    gsend[:, 0, :] = jnp.sum(part.reshape(SIDE, SIDE, 128), axis=1)

    for i in FAR_LAT:
        ta = (a + i) % SIDE
        copy_to(gsend.at[ta], gin.at[i], gs_sem.at[0], gr_sem.at[0], ta, b).start()

    def inner_state(c, _):
        res = mixed(mh[span_of(c), :], ml[span_of(c), :])
        out_v[pl.ds(c * ROWS + 1, ROWS), :, 0:256] = res.reshape(ROWS, CLON, 256)
        return 0

    lax.fori_loop(0, 2, inner_state, 0)
    arrive(two)
    for lanes, res in rim_beyond(1):
        out_v[0, :, lanes] = res[2 * CLAT : 2 * CLAT + CLON]
        out_v[CLAT - 1, :, lanes] = res[2 * CLAT + CLON : RIM]
        out_v[:, 0, lanes] = res[0:CLAT]
        out_v[:, CLON - 1, lanes] = res[CLAT : 2 * CLAT]
    leave = pltpu.make_async_copy(out_v, out, out_sem.at[0])
    leave.start()
    got = gsend[a]
    lat_in = gin.at[pl.ds(1, SIDE - 1)]
    pltpu.make_async_copy(lat_in, lat_in, gr_sem.at[0]).wait()
    for i in range(1, SIDE):
        got = got + gin[i]
    grow[...] = got

    for j in FAR_LON:
        copy_to(grow, gfin.at[j], gs_sem.at[1], gr_sem.at[1], a, (b + j) % SIDE).start()
    lon_in = gfin.at[pl.ds(1, SIDE - 1)]
    pltpu.make_async_copy(lon_in, lon_in, gr_sem.at[1]).wait()
    for i in range(1, SIDE):
        got = got + gfin[i]
    lanes = iota((1, 128), 1)
    owned = jnp.zeros((1, TRACERS), F32)
    for t in range(TRACERS):
        value = jnp.sum(jnp.where(lanes == 32 + TRACERS * b + t, got, 0.0), axis=1, keepdims=True)
        owned = jnp.where(iota((1, TRACERS), 1) == t, value, owned)
    owned = owned * (1.0 / jnp.sqrt(jnp.full((1, TRACERS), CELLS * DEVICES, F32)))
    grad[...] = owned.reshape(1, 1, TRACERS)

    finish(one)
    finish(two)
    for copy in lon_near:
        copy.wait_send()
    for n, copy in lat_near:
        @pl.when(jnp.logical_not(last_band if n == 0 else first_band))
        def _():
            copy.wait_send()

    leave.wait()
    for piece, sem in ((landed, ks_sem.at[0]), (coming, ks_sem.at[1]), (lat_in, gs_sem.at[0]), (lon_in, gs_sem.at[1])):
        pltpu.make_async_copy(piece, piece, sem).wait()
    for n, buf in enumerate((recv, recr)):
        piece = buf.at[pl.ds(1, DEVICES - 1)]
        pltpu.make_async_copy(piece, piece, ssem.at[n]).wait()


def deliver_kernel(state, grad, state_out, grad_out, held, small, sems):
    parts = 4
    rows = CLAT // parts
    reads = [pltpu.make_async_copy(grad, small, sems.at[0, parts])]
    writes = [pltpu.make_async_copy(small, grad_out, sems.at[1, parts])]
    for i in range(parts):
        span = pl.ds(i * rows, rows)
        reads.append(pltpu.make_async_copy(state.at[span], held.at[span], sems.at[0, i]))
        writes.append(pltpu.make_async_copy(held.at[span], state_out.at[span], sems.at[1, i]))
    for read in reads:
        read.start()
    for read, write in zip(reads, writes):
        read.wait()
        write.start()
    for write in writes:
        write.wait()


def body(
    adjoint_in, winds, vert_mix, level_weights, snd_weights, snd_columns, snd_counts, basis, owner
):
    anywhere = pl.BlockSpec(memory_space=pl.ANY)
    vmem = pl.BlockSpec(memory_space=pltpu.VMEM)
    state, grad = pl.pallas_call(
        window_kernel,
        out_shape=(
            jax.ShapeDtypeStruct((CLAT, CLON, CHAN), F32),
            jax.ShapeDtypeStruct((1, 1, TRACERS), F32),
        ),
        in_specs=[anywhere, anywhere, vmem, vmem, anywhere, vmem, vmem, anywhere, vmem],
        out_specs=(anywhere, vmem),
        scratch_shapes=[
            pltpu.VMEM((2, SLOTS, CHAN, 128), BF16),
            pltpu.VMEM((128 * SLOTS, 128), F32),
            pltpu.VMEM((128 * SLOTS, 128), F32),
            pltpu.VMEM((128 * 4, 128), F32),
            pltpu.VMEM((DEVICES, SLOTS, 256), BF16),
            pltpu.VMEM((DEVICES, 4, 128), BF16),
            pltpu.VMEM((DEVICES, 128), jnp.int32),
            pltpu.VMEM((SIDE, SIDE, 128), jnp.int32),
            pltpu.VMEM((SIDE, 1, 256), jnp.int32),
            pltpu.VMEM((DEVICES, SLOTS, 256), BF16),
            pltpu.VMEM((DEVICES, 4, 128), BF16),
            pltpu.VMEM((SIDE, 1, 256), jnp.int32),
            pltpu.VMEM((64, 128), F32),
            pltpu.VMEM((256, WIDE), BF16),
            pltpu.VMEM((CLAT, CLON, CHAN), F32),
            pltpu.VMEM((CLAT, CLON, 2 * LEV), F32),
            pltpu.VMEM((5, CLAT, CLON, CHAN), F32),
            pltpu.VMEM((5, 2 * CLAT, CHAN), F32),
            pltpu.VMEM((CLAT, CLON, DEVICES), F32),
            pltpu.VMEM((DEVICES, CELLS), BF16),
            pltpu.VMEM((DEVICES, CELLS), BF16),
            pltpu.VMEM((CHAN, WIDE), F32),
            pltpu.VMEM((CHAN, 256), BF16),
            pltpu.VMEM((CHAN, 256), BF16),
            pltpu.VMEM((CHAN, 256), BF16),
            pltpu.VMEM((CLAT + 2, 64, WIDE), F32),
            pltpu.VMEM((CLAT + 2, 64, WIDE), F32),
            pltpu.VMEM((2, 2, CLAT, WIDE), F32),
            pltpu.VMEM((2, 2, CLAT, WIDE), F32),
            pltpu.VMEM((2, 2, CLON, WIDE), F32),
            pltpu.VMEM((2 * ROWS * CLON, CHAN), BF16),
            pltpu.VMEM((2 * ROWS * CLON, CHAN), BF16),
            pltpu.VMEM((2 * RIM, CHAN), F32),
            pltpu.VMEM((RIM, CHAN), F32),
            pltpu.VMEM((DEVICES, RIM), BF16),
            pltpu.VMEM((DEVICES, RIM), BF16),
            pltpu.VMEM((CLAT, CLON, CHAN), F32),
            pltpu.VMEM((CLAT, CLON, 128), F32),
            pltpu.VMEM((SIDE, 1, 128), F32),
            pltpu.VMEM((SIDE, 1, 128), F32),
            pltpu.VMEM((1, 128), F32),
            pltpu.VMEM((SIDE, 1, 128), F32),
            pltpu.VMEM((2, CLAT, LEV), F32),
            pltpu.VMEM((2, CLAT, DEVICES), F32),
            pltpu.VMEM((2, CLAT, LEV), F32),
            pltpu.VMEM((2, CLAT, DEVICES), F32),
            pltpu.VMEM((2, CLON, 2 * LEV), F32),
            pltpu.VMEM((2, CLON, DEVICES), F32),
            pltpu.SemaphoreType.REGULAR,
            pltpu.SemaphoreType.DMA((2, 4)),
            pltpu.SemaphoreType.DMA((2, 4)),
            pltpu.SemaphoreType.DMA((2,)),
            pltpu.SemaphoreType.DMA((2, SIDE)),
            pltpu.SemaphoreType.DMA((7,)),
            pltpu.SemaphoreType.DMA((2,)),
            pltpu.SemaphoreType.DMA((2,)),
            pltpu.SemaphoreType.DMA((2, 4)),
            pltpu.SemaphoreType.DMA((2, 4)),
            pltpu.SemaphoreType.DMA((2,)),
            pltpu.SemaphoreType.DMA((2,)),
            pltpu.SemaphoreType.DMA((1,)),
        ],
        compiler_params=pltpu.CompilerParams(
            collective_id=0, has_side_effects=True, vmem_limit_bytes=56 << 20
        ),
        name="window",
    )(
        adjoint_in,
        winds,
        vert_mix,
        level_weights,
        jnp.transpose(snd_weights[0, 0], (1, 2, 0)),
        jnp.transpose(snd_columns[0, 0], (1, 0)),
        snd_counts[0],
        basis,
        owner.reshape(1, DEVICES),
    )
    return pl.pallas_call(
        deliver_kernel,
        out_shape=(
            jax.ShapeDtypeStruct((CLAT, CLON, CHAN), F32),
            jax.ShapeDtypeStruct((1, 1, TRACERS), F32),
        ),
        in_specs=[anywhere, anywhere],
        out_specs=(anywhere, anywhere),
        scratch_shapes=[
            pltpu.VMEM((CLAT, CLON, CHAN), F32),
            pltpu.VMEM((1, 1, TRACERS), F32),
            pltpu.SemaphoreType.DMA((2, 5)),
        ],
        compiler_params=pltpu.CompilerParams(vmem_limit_bytes=56 << 20),
        name="deliver",
    )(state, grad)


def solution(mesh):
    return jax.shard_map(
        body,
        mesh=mesh,
        in_specs=(
            P("lat", "lon", None),
            P("lat", "lon", None),
            P(),
            P(),
            P("lat", "lon", None, None, None),
            P("lat", "lon", None, None),
            P("lat", "lon", None),
            P("lat", "lon", None),
            P(),
        ),
        out_specs=(P("lat", "lon", None), P(("lat", "lon"), None, None)),
        check_vma=False,
    )
```

```python
import jax
import jax.numpy as jnp
from jax import lax
from jax.experimental import pallas as pl
from jax.experimental.pallas import tpu as pltpu
from jax.sharding import PartitionSpec as P

diffusion = 0.05
MESH = pl.DeviceIdType.MESH
BF16 = jnp.bfloat16
F32 = jnp.float32
DEVICES = 256
SIDE = 16
SLOTS = 16
CLAT, CLON = 24, 48
CELLS = CLAT * CLON
CHAN = 288
WIDE = 384
LEV = 72
TRACERS = 4
BAND = 8
LAG = 2
ROWS = 11
RIM = 2 * CLAT + 2 * CLON


FAR_LAT = (10, 6, 11, 9, 7, 5, 8, 14, 2, 13, 3, 12, 4, 15, 1)
FAR_LON = (4, 12, 3, 5, 11, 13, 2, 6, 10, 14, 1, 7, 9, 15, 8)


def flip(index, by):
    return sum(((index // k) % 2 + (by // k) % 2) % 2 * k for k in (8, 4, 2, 1))


def along(b, lon_off):
    p, f, e = lon_off // 4, (lon_off // 2) % 2, lon_off % 2
    dz = jnp.where(p == 0, 4 * f, jnp.where(e == 0, p, 8 - p))
    f = jnp.where(p == 0, e, f)
    return (b // 8 + f) % 2 * 8 + (b % 8 + dz) % 8


def iota(shape, dim):
    return lax.broadcasted_iota(jnp.int32, shape, dim)


def split(value):
    high = value.astype(BF16)
    return high, (value - high.astype(F32)).astype(BF16)


def dot(x, y):
    return jnp.dot(x, y, preferred_element_type=F32)


def window_kernel(
    adj, winds, mix, lweights, w, columns, counts, basis, owner,
    out, grad,
    w_v, f0, f1, fr, wbuf, rbuf, kbuf, kin, kmid, recv, recr, reck, stage, rhs,
    adj_v, winds_v, coef, coef_rim, basis_v, base_hi, base_lo, mat, mat_hi, mat_lo, mat_end,
    cur, nxt, col_out, col_in, row_in, mh, ml, rim, ring_coef, ring_hi, ring_lo, out_v, sens, gsend, gin, grow, gfin,
    winds_col, basis_col, near_winds_col, near_basis_col, near_winds_row, near_basis_row,
    pair_sem, ns_sem, nr_sem, ssem, rsem, lsem, ks_sem, kr_sem, hs_sem, hr_sem, gs_sem, gr_sem, out_sem,
):
    a = lax.axis_index("lat")
    b = lax.axis_index("lon")
    me = a * SIDE + b
    bar = pltpu.get_barrier_semaphore()

    halves = [a // 8, 1 - a // 8]
    loads = []
    for n, h in enumerate(halves):
        lanes = pl.ds(pl.multiple_of(128 * h, 128), 128)
        for q in range(2):
            eight = pl.ds(8 * q, 8)
            loads.append(pltpu.make_async_copy(w.at[eight, :, lanes], w_v.at[n, eight], lsem.at[2 * n + q]))
    for load in loads:
        load.start()
    for i, j in zip(FAR_LAT, FAR_LON):
        pl.semaphore_signal(bar, inc=1, device_id=(a, (b + j) % SIDE), device_id_type=MESH)
        pl.semaphore_signal(bar, inc=1, device_id=((a + i) % SIDE, b), device_id_type=MESH)
    loads.append(pltpu.make_async_copy(adj, adj_v, lsem.at[4]))
    loads.append(pltpu.make_async_copy(winds, winds_v.at[pl.ds(0, CLAT)], lsem.at[5]))
    loads.append(pltpu.make_async_copy(basis, basis_v.at[pl.ds(0, CLAT)], lsem.at[6]))
    for load in loads[4:]:
        load.start()

    def copy_to(src, dst, send_sem, recv_sem, ta, tb):
        return pltpu.make_async_remote_copy(
            src_ref=src, dst_ref=dst, send_sem=send_sem, recv_sem=recv_sem, device_id=(ta, tb), device_id_type=MESH
        )

    slot = iota((SLOTS, DEVICES), 0)
    where = jnp.where(slot < counts[...], columns[...], -1)
    place = flip(a, iota((1, DEVICES), 1) // SIDE) % 8
    placed = jnp.where(iota((128, DEVICES), 0) // SLOTS == place, jnp.concatenate([where] * 8, axis=0), 0)
    for h in range(2):
        kbuf[128 * h : 128 * h + 128, :] = placed[:, 128 * h : 128 * h + 128].T

    def prepare(n):
        h = halves[n]
        for q in range(2):
            loads[2 * n + q].wait()
            for s in range(8 * q, 8 * q + 8):
                for c, dst in ((0, f0), (1, f1)):
                    block = w_v[n, s, 128 * c : 128 * c + 128, :]
                    dst[pl.ds(s, 128, stride=SLOTS), :] = block.astype(F32).T
        for r in range(4):
            pieces = [w_v[n, 4 * g + r, 256:288, :] for g in range(4)]
            block = jnp.concatenate([p.astype(F32) for p in pieces], axis=0)
            fr[pl.ds(r, 128, stride=4), :] = block.T

        def pack(i, _):
            first = 128 * h + 8 * i
            rows = pl.ds(pl.multiple_of(128 * i, 128), 128)
            wbuf[pl.ds(first, 8), :, 0:128] = f0[rows, :].astype(BF16).reshape(8, SLOTS, 128)
            wbuf[pl.ds(first, 8), :, 128:256] = f1[rows, :].astype(BF16).reshape(8, SLOTS, 128)
            four = fr[pl.ds(pl.multiple_of(32 * i, 32), 32), :]
            rbuf[pl.ds(first, 8)] = four.reshape(8, 4, 128).astype(BF16)
            return 0

        lax.fori_loop(0, 16, pack, 0, unroll=4)

    def send(lat_off, lon_off):
        ta, tb = flip(a, lat_off), along(b, lon_off)
        d = ta * SIDE + tb
        i = lon_off * SIDE + lat_off
        for n, (src, dst) in enumerate(((wbuf, recv), (rbuf, recr))):
            copy_to(src.at[d], dst.at[i], ssem.at[n], rsem.at[n, lon_off], ta, tb).start()

    def send_lat(lat_off, _):
        send(lat_off, 0)
        return 0

    def send_lon(i, _):
        send(0, jnp.where(i <= 2, i + 1, jnp.where(i == SIDE - 1, 1, 18 - i)))
        return 0

    prepare(0)
    pl.semaphore_wait(bar, 2 * (SIDE - 1))

    for j in FAR_LON:
        pl.semaphore_signal(pair_sem, inc=1, device_id=(a, (b + j) % SIDE), device_id_type=MESH)

    def send_columns(lat_off, _):
        ta = flip(a, lat_off)
        src = kbuf.at[pl.ds(pl.multiple_of(ta * SIDE, SIDE), SIDE)]
        copy_to(src, kin.at[lat_off], ks_sem.at[0], kr_sem.at[0], ta, b).start()
        return 0

    lax.fori_loop(1, SIDE, send_lon, 0)
    lax.fori_loop(1, SIDE, send_columns, 0)
    lax.fori_loop(1, 8, send_lat, 0)
    prepare(1)
    lax.fori_loop(8, SIDE, send_lat, 0)
    own = [
        pltpu.make_async_copy(wbuf.at[me], recv.at[0], rsem.at[0, 0]),
        pltpu.make_async_copy(rbuf.at[me], recr.at[0], rsem.at[1, 0]),
    ]
    for copy in own:
        copy.start()

    def pair_of(t):
        near = 2 * (3 - (t - 1) // 2) + (t - 1) % 2
        return jnp.where(t == 0, 1, jnp.where(t == 7, 0, near))

    def send_pair(t):
        first = 2 * pair_of(t)

        def both(i, _):
            lat_off = SIDE - i

            @pl.when(first > 0)
            def _():
                send(lat_off, first)

            send(lat_off, first + 1)
            return 0

        lax.fori_loop(1, SIDE, both, 0)

    pl.semaphore_wait(pair_sem, SIDE - 1)
    send_pair(0)

    landed = kin.at[pl.ds(1, SIDE - 1)]
    pltpu.make_async_copy(landed, landed, kr_sem.at[0]).wait()
    low = kbuf[pl.ds(pl.multiple_of(a * SIDE, SIDE), SIDE), :]
    high = kin[8]
    for i in range(1, 8):
        low = low + kin[i]
        high = high + kin[8 + i]
    kmid[:, 0, 0:128] = low
    kmid[:, 0, 128:256] = high
    reck[0] = kmid[b]

    def send_rows(lon_off, _):
        tb = along(b, lon_off)
        copy_to(kmid.at[tb], reck.at[lon_off], ks_sem.at[1], kr_sem.at[1], a, tb).start()
        return 0

    lax.fori_loop(1, SIDE, send_rows, 0)
    send_pair(1)

    mat[...] = jnp.zeros_like(mat)
    for t in range(TRACERS):
        mat[LEV * t : LEV * t + LEV, LEV * t : LEV * t + LEV] = mix[...]
    gain = jnp.sum(mat[:, 0:CHAN] * lweights[...].reshape(1, CHAN), axis=1, keepdims=True)
    lane = iota((CHAN, WIDE - CHAN), 1)
    extra = (iota((CHAN, WIDE - CHAN), 0) // LEV == lane % TRACERS) & (lane < TRACERS * SIDE)
    mat[:, CHAN:WIDE] = jnp.where(extra, gain, 0.0)
    mat_hi[...], mat_lo[...] = split(mat[:, 0:256])
    mat_end[:, 0:128], mat_end[:, 128:256] = split(mat[:, 256:WIDE])

    loads[6].wait()
    pick = jnp.where(iota((DEVICES, DEVICES), 0) == owner[...], 1.0, 0.0).astype(BF16)

    def by_owner(piece):
        turned = lax.dot_general(pick, piece, (((1,), (1,)), ((), ())), preferred_element_type=F32)
        return turned.astype(BF16)

    for c in range(CLAT // BAND):
        high, low = split(basis_v[BAND * c : BAND * c + BAND].reshape(BAND * CLON, DEVICES))
        base_hi[:, BAND * CLON * c : BAND * CLON * (c + 1)] = by_owner(high)
        base_lo[:, BAND * CLON * c : BAND * CLON * (c + 1)] = by_owner(low)

    loads[4].wait()
    loads[5].wait()

    for n, x in enumerate((CLON - 1, 0)):
        winds_col[n] = winds_v[0:CLAT, x, 0:LEV]
        basis_col[n] = basis_v[0:CLAT, x, :]
    lon_near = []
    lat_near = []
    for n, (r, tb, ta) in enumerate((
        (CLAT - 1, (b + 1) % SIDE, (a + 1) % SIDE),
        (0, (b + SIDE - 1) % SIDE, (a + SIDE - 1) % SIDE),
    )):
        for k, (col, row, col_in_, row_in_) in enumerate((
            (winds_col, winds_v, near_winds_col, near_winds_row),
            (basis_col, basis_v, near_basis_col, near_basis_row),
        )):
            lon_near.append(copy_to(col.at[n], col_in_.at[n], ns_sem.at[k, n], nr_sem.at[k, n], a, tb))
            lat_near.append((n, copy_to(row.at[r], row_in_.at[n], ns_sem.at[k, 2 + n], nr_sem.at[k, 2 + n], ta, b)))
    for copy in lon_near:
        copy.start()
    first_band, last_band = a == 0, a == SIDE - 1
    for n, copy in lat_near:
        @pl.when(jnp.logical_not(last_band if n == 0 else first_band))
        def _():
            copy.start()

    for n, none in ((0, first_band), (1, last_band)):
        @pl.when(none)
        def _():
            near_winds_row[n] = jnp.zeros((CLON, 2 * LEV), F32)
            near_basis_row[n] = jnp.zeros((CLON, DEVICES), F32)
            row_in[0, n] = jnp.zeros((CLON, WIDE), F32)
            row_in[1, n] = jnp.zeros((CLON, WIDE), F32)

    def clear(r, _):
        cur[r] = jnp.zeros((64, WIDE), F32)
        nxt[r] = jnp.zeros((64, WIDE), F32)
        return 0

    lax.fori_loop(0, CLAT + 2, clear, 0)

    def begin(r, _):
        cur[r + 1, 8:56, 0:CHAN] = adj_v[r]
        return 0

    lax.fori_loop(0, CLAT, begin, 0)

    def coefficients(r):
        both = winds_v[r]
        u = jnp.concatenate([both[:, 0:LEV]] * TRACERS, axis=1)
        v = jnp.concatenate([both[:, LEV : 2 * LEV]] * TRACERS, axis=1)
        east = jnp.maximum(u, 0.0) + diffusion
        west = jnp.maximum(-u, 0.0) + diffusion
        north = jnp.maximum(v, 0.0) + diffusion
        south = jnp.maximum(-v, 0.0) + diffusion
        coef[0, r] = 1.0 - ((east + west) + (north + south))
        coef[1, r] = east
        coef[2, r] = west
        coef[3, r] = north
        coef[4, r] = south

    rows = iota((DEVICES, 64), 0)
    lanes = iota((DEVICES, 64), 1)
    spread = jnp.where((rows // 16 == lanes // 4) & (rows % 4 == lanes % 4), 1.0, 0.0).astype(BF16)
    rows = iota((DEVICES, 128), 0)
    lanes = iota((DEVICES, 128), 1)
    keep = jnp.where((rows // 4) % 4 == lanes // 32, 1.0, 0.0)
    rows = iota((128, 128), 0)
    lanes = iota((128, 128), 1)
    fold = jnp.where(rows % 32 == lanes, 1.0, 0.0).astype(BF16)

    def absorb(g):
        first = g * SIDE
        for n, buf in enumerate((recv, recr)):
            piece = buf.at[pl.ds(first, SIDE)]
            pltpu.make_async_copy(piece, piece, rsem.at[n, g]).wait()
        rhs[:, 0:256] = recv[pl.ds(first, SIDE)].reshape(256, 256)
        for m in range(SIDE):
            stage[4 * m : 4 * m + 4, :] = recr[first + m].astype(F32)
        wide = (dot(spread, stage[0:64, :].astype(BF16)) * keep).astype(BF16)
        rhs[:, 256:384] = dot(wide, fold).astype(BF16)
        spot = reck[g]
        for c in range(CLAT // BAND):
            ids = iota((BAND * CLON, 256), 0) + c * BAND * CLON
            table = jnp.where(ids == spot, 1.0, 0.0).astype(BF16)
            cur[c * BAND + 1 : (c + 1) * BAND + 1, 8:56, :] += dot(table, rhs[...]).reshape(BAND, CLON, WIDE)

    coming = reck.at[pl.ds(1, SIDE - 1)]
    pltpu.make_async_copy(coming, coming, kr_sem.at[1]).wait()

    def turn(t, _):
        @pl.when(t < 8)
        def _():
            send_pair(t)

        @pl.when(t < 8)
        def _():
            for i in range(4):
                coefficients(4 * (t - 2) + i)

        first = 2 * pair_of(t - LAG)
        absorb(first)
        absorb(first + 1)
        return 0

    lax.fori_loop(LAG, 8, turn, 0)
    for k in range(5):
        coef_rim[k, 0:CLAT, :] = coef[k, 0:CLAT, 0, :]
        coef_rim[k, CLAT : 2 * CLAT, :] = coef[k, 0:CLAT, CLON - 1, :]

    for copy in lon_near:
        copy.wait_recv()
    for n, copy in lat_near:
        @pl.when(jnp.logical_not(first_band if n == 0 else last_band))
        def _():
            copy.wait_recv()

    def inflow(wind):
        return jnp.concatenate([jnp.maximum(wind, 0.0) + diffusion] * TRACERS, axis=1)

    ring_coef[0:CLAT, :] = inflow(near_winds_col[0])
    ring_coef[CLAT : 2 * CLAT, :] = inflow(-near_winds_col[1])
    ring_coef[2 * CLAT : 2 * CLAT + CLON, :] = inflow(near_winds_row[0][:, LEV : 2 * LEV])
    ring_coef[2 * CLAT + CLON : RIM, :] = inflow(-near_winds_row[1][:, LEV : 2 * LEV])
    ring_basis = jnp.concatenate([near_basis_col[0], near_basis_col[1], near_basis_row[0], near_basis_row[1]], axis=0)
    high, low = split(ring_basis)
    ring_hi[...] = by_owner(high)
    ring_lo[...] = by_owner(low)

    absorb(0)
    last = 2 * pair_of(6)

    def last_turns(g, _):
        absorb(jnp.where(g == 2, 1, last + g))
        return 0

    lax.fori_loop(0, 3, last_turns, 0)

    def halo(buf, e):
        north = copy_to(buf.at[CLAT, 8:56, :], row_in.at[e, 0], hs_sem.at[e, 0], hr_sem.at[e, 0], (a + 1) % SIDE, b)
        south = copy_to(buf.at[1, 8:56, :], row_in.at[e, 1], hs_sem.at[e, 1], hr_sem.at[e, 1], (a + SIDE - 1) % SIDE, b)
        east = copy_to(col_out.at[e, 0], col_in.at[e, 0], hs_sem.at[e, 2], hr_sem.at[e, 2], a, (b + 1) % SIDE)
        west = copy_to(col_out.at[e, 1], col_in.at[e, 1], hs_sem.at[e, 3], hr_sem.at[e, 3], a, (b + SIDE - 1) % SIDE)

        @pl.when(a < SIDE - 1)
        def _():
            north.start()

        @pl.when(a > 0)
        def _():
            south.start()

        east.start()
        west.start()
        return north, south, east, west

    def arrive(copies):
        north, south, east, west = copies

        @pl.when(a > 0)
        def _():
            north.wait_recv()

        @pl.when(a < SIDE - 1)
        def _():
            south.wait_recv()

        east.wait_recv()
        west.wait_recv()

    def finish(copies):
        north, south, east, west = copies

        @pl.when(a < SIDE - 1)
        def _():
            north.wait_send()

        @pl.when(a > 0)
        def _():
            south.wait_send()

        east.wait_send()
        west.wait_send()

    def blend(weights, values):
        m = weights[0] * values[0]
        for k in range(1, 5):
            m = m + weights[k] * values[k]
        return m

    def mixed(high, low):
        return dot(high, mat_hi[...]) + dot(low, mat_hi[...]) + dot(high, mat_lo[...])

    def mixed_end(high, low, start=0):
        both = dot(high[:, start:], mat_end[start:, :])
        return both[:, 0:128] + both[:, 128:256] + dot(low[:, start:], mat_end[start:, 0:128])

    def span_of(c):
        return pl.ds(pl.multiple_of(c * ROWS * CLON, 16), ROWS * CLON)

    def inner(buf, c):
        for k in range(ROWS):
            r = 1 + c * ROWS + k
            m = blend(
                [coef[n, r] for n in range(5)],
                [buf[r + 1, 8:56, 0:CHAN], buf[r + 1, 9:57, 0:CHAN], buf[r + 1, 7:55, 0:CHAN],
                 buf[r + 2, 8:56, 0:CHAN], buf[r, 8:56, 0:CHAN]],
            )
            rows = pl.ds(pl.multiple_of((c * ROWS + k) * CLON, 16), CLON)
            mh[rows, :], ml[rows, :] = split(m)
        return mh[span_of(c), :], ml[span_of(c), :]

    def rim_inside(buf):
        for n, x in enumerate((8, 55)):
            span = slice(n * CLAT, (n + 1) * CLAT)
            rim[span, :] = blend(
                [coef_rim[k, span, :] for k in range(5)],
                [buf[1 : CLAT + 1, x, 0:CHAN], buf[1 : CLAT + 1, x + 1, 0:CHAN], buf[1 : CLAT + 1, x - 1, 0:CHAN],
                 buf[2 : CLAT + 2, x, 0:CHAN], buf[0:CLAT, x, 0:CHAN]],
            )
        for n, r in enumerate((0, CLAT - 1)):
            rim[2 * CLAT + n * CLON : 2 * CLAT + (n + 1) * CLON, :] = blend(
                [coef[k, r] for k in range(5)],
                [buf[r + 1, 8:56, 0:CHAN], buf[r + 1, 9:57, 0:CHAN], buf[r + 1, 7:55, 0:CHAN],
                 buf[r + 2, 8:56, 0:CHAN], buf[r, 8:56, 0:CHAN]],
            )

        for r, k, edge in ((0, 4, first_band), (CLAT - 1, 3, last_band)):
            @pl.when(edge)
            def _():
                n = min(r, 1)
                rim[2 * CLAT + n * CLON : 2 * CLAT + (n + 1) * CLON, :] += coef[k, r] * buf[r + 1, 8:56, 0:CHAN]
                for i, x in ((r, 8), (CLAT + r, 55)):
                    rim[i : i + 1, :] += coef_rim[k, i : i + 1, :] * buf[r + 1, x : x + 1, 0:CHAN]

    def rim_beyond(e):
        rim[0:CLAT, :] += coef_rim[2, 0:CLAT, :] * col_in[e, 0, :, 0:CHAN]
        rim[CLAT : 2 * CLAT, :] += coef_rim[1, CLAT : 2 * CLAT, :] * col_in[e, 1, :, 0:CHAN]
        for n, r, k in ((0, 0, 4), (1, CLAT - 1, 3)):
            rim[2 * CLAT + n * CLON : 2 * CLAT + (n + 1) * CLON, :] += coef[k, r] * row_in[e, n, :, 0:CHAN]
            for i, x in ((r, 0), (CLAT + r, CLON - 1)):
                rim[i : i + 1, :] += coef_rim[k, i : i + 1, :] * row_in[e, n, x : x + 1, 0:CHAN]
        parts = split(rim[0:RIM, :])
        return (slice(0, 256), mixed(*parts)), (slice(256, CHAN), mixed_end(*parts, 128)[:, 0 : CHAN - 256])

    col_out[0, 0, :, 0:CHAN] = cur[1 : CLAT + 1, 55, 0:CHAN]
    col_out[0, 1, :, 0:CHAN] = cur[1 : CLAT + 1, 8, 0:CHAN]
    one = halo(cur, 0)

    def inner_one(c, _):
        high, low = inner(cur, c)
        rows = pl.ds(c * ROWS + 2, ROWS)
        nxt[rows, 8:56, 0:256] = mixed(high, low).reshape(ROWS, CLON, 256)
        end = mixed_end(high, low, 128)[:, 0 : CHAN - 256]
        nxt[rows, 8:56, 256:CHAN] = end.reshape(ROWS, CLON, CHAN - 256)
        return 0

    lax.fori_loop(0, 2, inner_one, 0)
    rim_inside(cur)
    arrive(one)
    for lanes, res in rim_beyond(0):
        nxt[1, 8:56, lanes] = res[2 * CLAT : 2 * CLAT + CLON]
        nxt[CLAT, 8:56, lanes] = res[2 * CLAT + CLON : RIM]
        nxt[1 : CLAT + 1, 8, lanes] = res[0:CLAT]
        nxt[1 : CLAT + 1, 55, lanes] = res[CLAT : 2 * CLAT]
        col_out[1, 0, :, lanes] = res[CLAT : 2 * CLAT]
        col_out[1, 1, :, lanes] = res[0:CLAT]
    two = halo(nxt, 1)

    def inner_sens(c, _):
        end = mixed_end(*inner(nxt, c)).reshape(ROWS, CLON, 128)
        sens[pl.ds(c * ROWS + 1, ROWS)] = end
        out_v[pl.ds(c * ROWS + 1, ROWS), :, 256:CHAN] = end[:, :, 0 : CHAN - 256]
        return 0

    lax.fori_loop(0, 2, inner_sens, 0)

    rim_inside(nxt)
    rim[RIM : RIM + CLAT, :] = ring_coef[0:CLAT, :] * nxt[1 : CLAT + 1, 8, 0:CHAN]
    rim[RIM + CLAT : RIM + 2 * CLAT, :] = ring_coef[CLAT : 2 * CLAT, :] * nxt[1 : CLAT + 1, 55, 0:CHAN]
    rim[RIM + 2 * CLAT : RIM + 2 * CLAT + CLON, :] = ring_coef[2 * CLAT : 2 * CLAT + CLON, :] * nxt[1, 8:56, 0:CHAN]
    rim[RIM + 2 * CLAT + CLON : 2 * RIM, :] = ring_coef[2 * CLAT + CLON : RIM, :] * nxt[CLAT, 8:56, 0:CHAN]
    ends = mixed_end(*split(rim[2 * CLAT : 2 * RIM, :]))
    sens[0] = ends[0:CLON]
    sens[CLAT - 1] = ends[CLON : 2 * CLON]
    beyond_hi, beyond_lo = split(ends[2 * CLON :])

    sens_hi, sens_lo = split(sens[0:CLAT].reshape(CELLS, 128))
    both = dot(base_hi[...], jnp.concatenate([sens_hi, sens_lo], axis=1))
    both = both + dot(ring_hi[...], jnp.concatenate([beyond_hi, beyond_lo], axis=1))
    part = both[:, 0:128] + both[:, 128:256] + (dot(base_lo[...], sens_hi) + dot(ring_lo[...], beyond_hi))
    rows = iota((DEVICES, 128), 0)
    lanes = iota((DEVICES, 128), 1)
    part = jnp.where((lanes // TRACERS == rows % SIDE + 8) & (lanes >= 32), part, 0.0)
    gsend[:, 0, :] = jnp.sum(part.reshape(SIDE, SIDE, 128), axis=1)

    for i in FAR_LAT:
        ta = (a + i) % SIDE
        copy_to(gsend.at[ta], gin.at[i], gs_sem.at[0], gr_sem.at[0], ta, b).start()

    def inner_state(c, _):
        res = mixed(mh[span_of(c), :], ml[span_of(c), :])
        out_v[pl.ds(c * ROWS + 1, ROWS), :, 0:256] = res.reshape(ROWS, CLON, 256)
        return 0

    lax.fori_loop(0, 2, inner_state, 0)
    arrive(two)
    for lanes, res in rim_beyond(1):
        out_v[0, :, lanes] = res[2 * CLAT : 2 * CLAT + CLON]
        out_v[CLAT - 1, :, lanes] = res[2 * CLAT + CLON : RIM]
        out_v[0:CLAT, 0, lanes] = res[0:CLAT]
        out_v[0:CLAT, CLON - 1, lanes] = res[CLAT : 2 * CLAT]
    leave = pltpu.make_async_copy(out_v.at[pl.ds(0, CLAT)], out, out_sem.at[0])
    leave.start()
    got = gsend[a]
    lat_in = gin.at[pl.ds(1, SIDE - 1)]
    pltpu.make_async_copy(lat_in, lat_in, gr_sem.at[0]).wait()
    for i in range(1, SIDE):
        got = got + gin[i]
    grow[...] = got

    for j in FAR_LON:
        copy_to(grow, gfin.at[j], gs_sem.at[1], gr_sem.at[1], a, (b + j) % SIDE).start()
    lon_in = gfin.at[pl.ds(1, SIDE - 1)]
    pltpu.make_async_copy(lon_in, lon_in, gr_sem.at[1]).wait()
    for i in range(1, SIDE):
        got = got + gfin[i]
    lanes = iota((1, 128), 1)
    owned = jnp.zeros((1, TRACERS), F32)
    for t in range(TRACERS):
        value = jnp.sum(jnp.where(lanes == 32 + TRACERS * b + t, got, 0.0), axis=1, keepdims=True)
        owned = jnp.where(iota((1, TRACERS), 1) == t, value, owned)
    owned = owned * (1.0 / jnp.sqrt(jnp.full((1, TRACERS), CELLS * DEVICES, F32)))
    grad[...] = owned.reshape(1, 1, TRACERS)

    finish(one)
    finish(two)
    for copy in lon_near:
        copy.wait_send()
    for n, copy in lat_near:
        @pl.when(jnp.logical_not(last_band if n == 0 else first_band))
        def _():
            copy.wait_send()

    leave.wait()
    for piece, sem in ((landed, ks_sem.at[0]), (coming, ks_sem.at[1]), (lat_in, gs_sem.at[0]), (lon_in, gs_sem.at[1])):
        pltpu.make_async_copy(piece, piece, sem).wait()
    for n, buf in enumerate((recv, recr)):
        piece = buf.at[pl.ds(1, DEVICES - 1)]
        pltpu.make_async_copy(piece, piece, ssem.at[n]).wait()


def deliver_kernel(state, grad, state_out, grad_out, held, small, sems):
    parts = 4
    rows = CLAT // parts
    reads = [pltpu.make_async_copy(grad, small, sems.at[0, parts])]
    writes = [pltpu.make_async_copy(small, grad_out, sems.at[1, parts])]
    for i in range(parts):
        span = pl.ds(i * rows, rows)
        reads.append(pltpu.make_async_copy(state.at[span], held.at[span], sems.at[0, i]))
        writes.append(pltpu.make_async_copy(held.at[span], state_out.at[span], sems.at[1, i]))
    for read in reads:
        read.start()
    for read, write in zip(reads, writes):
        read.wait()
        write.start()
    for write in writes:
        write.wait()


def body(
    adjoint_in, winds, vert_mix, level_weights, snd_weights, snd_columns, snd_counts, basis, owner
):
    anywhere = pl.BlockSpec(memory_space=pl.ANY)
    vmem = pl.BlockSpec(memory_space=pltpu.VMEM)
    state, grad = pl.pallas_call(
        window_kernel,
        out_shape=(
            jax.ShapeDtypeStruct((CLAT, CLON, CHAN), F32),
            jax.ShapeDtypeStruct((1, 1, TRACERS), F32),
        ),
        in_specs=[anywhere, anywhere, vmem, vmem, anywhere, vmem, vmem, anywhere, vmem],
        out_specs=(anywhere, vmem),
        scratch_shapes=[
            pltpu.VMEM((2, SLOTS, CHAN, 128), BF16),
            pltpu.VMEM((129 * SLOTS, 128), F32),
            pltpu.VMEM((129 * SLOTS, 128), F32),
            pltpu.VMEM((130 * 4, 128), F32),
            pltpu.VMEM((DEVICES, SLOTS, 256), BF16),
            pltpu.VMEM((DEVICES, 4, 128), BF16),
            pltpu.VMEM((DEVICES, 128), jnp.int32),
            pltpu.VMEM((SIDE, SIDE, 128), jnp.int32),
            pltpu.VMEM((SIDE, 1, 256), jnp.int32),
            pltpu.VMEM((DEVICES, SLOTS, 256), BF16),
            pltpu.VMEM((DEVICES, 4, 128), BF16),
            pltpu.VMEM((SIDE, 1, 256), jnp.int32),
            pltpu.VMEM((72, 128), F32),
            pltpu.VMEM((256, WIDE), BF16),
            pltpu.VMEM((CLAT, CLON, CHAN), F32),
            pltpu.VMEM((CLAT + 1, CLON, 2 * LEV), F32),
            pltpu.VMEM((5, CLAT + 1, CLON, CHAN), F32),
            pltpu.VMEM((5, 2 * CLAT, CHAN), F32),
            pltpu.VMEM((CLAT + 1, CLON, DEVICES), F32),
            pltpu.VMEM((DEVICES, CELLS), BF16),
            pltpu.VMEM((DEVICES, CELLS), BF16),
            pltpu.VMEM((CHAN, WIDE), F32),
            pltpu.VMEM((CHAN, 256), BF16),
            pltpu.VMEM((CHAN, 256), BF16),
            pltpu.VMEM((CHAN, 256), BF16),
            pltpu.VMEM((CLAT + 2, 64, WIDE), F32),
            pltpu.VMEM((CLAT + 2, 64, WIDE), F32),
            pltpu.VMEM((2, 2, CLAT, WIDE), F32),
            pltpu.VMEM((2, 2, CLAT, WIDE), F32),
            pltpu.VMEM((3, 2, CLON, WIDE), F32),
            pltpu.VMEM((2 * ROWS * CLON, CHAN), BF16),
            pltpu.VMEM((2 * ROWS * CLON, CHAN), BF16),
            pltpu.VMEM((2 * RIM, CHAN), F32),
            pltpu.VMEM((RIM, CHAN), F32),
            pltpu.VMEM((DEVICES, RIM), BF16),
            pltpu.VMEM((DEVICES, RIM), BF16),
            pltpu.VMEM((CLAT + 1, CLON, CHAN), F32),
            pltpu.VMEM((CLAT + 1, CLON, 128), F32),
            pltpu.VMEM((SIDE, 1, 128), F32),
            pltpu.VMEM((SIDE, 1, 128), F32),
            pltpu.VMEM((1, 128), F32),
            pltpu.VMEM((SIDE, 1, 128), F32),
            pltpu.VMEM((2, CLAT, LEV), F32),
            pltpu.VMEM((2, CLAT, DEVICES), F32),
            pltpu.VMEM((2, CLAT, LEV), F32),
            pltpu.VMEM((2, CLAT, DEVICES), F32),
            pltpu.VMEM((2, CLON, 2 * LEV), F32),
            pltpu.VMEM((2, CLON, DEVICES), F32),
            pltpu.SemaphoreType.REGULAR,
            pltpu.SemaphoreType.DMA((2, 4)),
            pltpu.SemaphoreType.DMA((2, 4)),
            pltpu.SemaphoreType.DMA((2,)),
            pltpu.SemaphoreType.DMA((2, SIDE)),
            pltpu.SemaphoreType.DMA((7,)),
            pltpu.SemaphoreType.DMA((2,)),
            pltpu.SemaphoreType.DMA((2,)),
            pltpu.SemaphoreType.DMA((2, 4)),
            pltpu.SemaphoreType.DMA((2, 4)),
            pltpu.SemaphoreType.DMA((2,)),
            pltpu.SemaphoreType.DMA((2,)),
            pltpu.SemaphoreType.DMA((1,)),
        ],
        compiler_params=pltpu.CompilerParams(
            collective_id=0, has_side_effects=True, vmem_limit_bytes=56 << 20
        ),
        name="window",
    )(
        adjoint_in,
        winds,
        vert_mix,
        level_weights,
        jnp.transpose(snd_weights[0, 0], (1, 2, 0)),
        jnp.transpose(snd_columns[0, 0], (1, 0)),
        snd_counts[0],
        basis,
        owner.reshape(1, DEVICES),
    )
    return pl.pallas_call(
        deliver_kernel,
        out_shape=(
            jax.ShapeDtypeStruct((CLAT, CLON, CHAN), F32),
            jax.ShapeDtypeStruct((1, 1, TRACERS), F32),
        ),
        in_specs=[anywhere, anywhere],
        out_specs=(anywhere, anywhere),
        scratch_shapes=[
            pltpu.VMEM((CLAT, CLON, CHAN), F32),
            pltpu.VMEM((1, 1, TRACERS), F32),
            pltpu.SemaphoreType.DMA((2, 5)),
        ],
        compiler_params=pltpu.CompilerParams(vmem_limit_bytes=56 << 20),
        name="deliver",
    )(state, grad)


def solution(mesh):
    return jax.shard_map(
        body,
        mesh=mesh,
        in_specs=(
            P("lat", "lon", None),
            P("lat", "lon", None),
            P(),
            P(),
            P("lat", "lon", None, None, None),
            P("lat", "lon", None, None),
            P("lat", "lon", None),
            P("lat", "lon", None),
            P(),
        ),
        out_specs=(P("lat", "lon", None), P(("lat", "lon"), None, None)),
        check_vma=False,
    )
```

```python
import jax
import jax.numpy as jnp
from jax import lax
from jax.experimental import pallas as pl
from jax.experimental.pallas import tpu as pltpu
from jax.sharding import PartitionSpec as P

diffusion = 0.05
MESH = pl.DeviceIdType.MESH
BF16 = jnp.bfloat16
F32 = jnp.float32
DEVICES = 256
SIDE = 16
SLOTS = 16
CLAT, CLON = 24, 48
CELLS = CLAT * CLON
CHAN = 288
WIDE = 384
LEV = 72
TRACERS = 4
BAND = 8
LAG = 2
ROWS = 11
RIM = 2 * CLAT + 2 * CLON


FAR_LAT = (10, 6, 11, 9, 7, 5, 8, 14, 2, 13, 3, 12, 4, 15, 1)
FAR_LON = (4, 12, 3, 5, 11, 13, 2, 6, 10, 14, 1, 7, 9, 15, 8)


def flip(index, by):
    return sum(((index // k) % 2 + (by // k) % 2) % 2 * k for k in (8, 4, 2, 1))


def along(b, lon_off):
    p, f, e = lon_off // 4, (lon_off // 2) % 2, lon_off % 2
    dz = jnp.where(p == 0, 4 * f, jnp.where(e == 0, p, 8 - p))
    f = jnp.where(p == 0, e, f)
    return (b // 8 + f) % 2 * 8 + (b % 8 + dz) % 8


def iota(shape, dim):
    return lax.broadcasted_iota(jnp.int32, shape, dim)


def split(value):
    high = value.astype(BF16)
    return high, (value - high.astype(F32)).astype(BF16)


def dot(x, y):
    return jnp.dot(x, y, preferred_element_type=F32)


def window_kernel(
    adj, winds, mix, lweights, w, columns, counts, basis, owner,
    out, grad,
    w_v, f0, f1, fr, wbuf, rbuf, kbuf, kin, kmid, recv, recr, reck, stage, rhs,
    adj_v, winds_v, coef, coef_rim, basis_v, base_hi, base_lo, mat, mat_hi, mat_lo, mat_end,
    cur, nxt, col_out, col_in, row_in, mh, ml, rim, ring_coef, ring_hi, ring_lo, out_v, sens, gsend, gin, grow, gfin,
    winds_col, basis_col, near_winds_col, near_basis_col, near_winds_row, near_basis_row,
    pair_sem, ns_sem, nr_sem, ssem, rsem, lsem, ks_sem, kr_sem, hs_sem, hr_sem, gs_sem, gr_sem, out_sem,
):
    a = lax.axis_index("lat")
    b = lax.axis_index("lon")
    me = a * SIDE + b
    bar = pltpu.get_barrier_semaphore()

    halves = [a // 8, 1 - a // 8]
    loads = []
    for n, h in enumerate(halves):
        lanes = pl.ds(pl.multiple_of(128 * h, 128), 128)
        for q in range(2):
            eight = pl.ds(8 * q, 8)
            loads.append(pltpu.make_async_copy(w.at[eight, :, lanes], w_v.at[n, eight], lsem.at[2 * n + q]))
    for load in loads:
        load.start()
    for i, j in zip(FAR_LAT, FAR_LON):
        pl.semaphore_signal(bar, inc=1, device_id=(a, (b + j) % SIDE), device_id_type=MESH)
        pl.semaphore_signal(bar, inc=1, device_id=((a + i) % SIDE, b), device_id_type=MESH)
    loads.append(pltpu.make_async_copy(adj, adj_v, lsem.at[4]))
    loads.append(pltpu.make_async_copy(winds, winds_v.at[pl.ds(0, CLAT)], lsem.at[5]))
    loads.append(pltpu.make_async_copy(basis, basis_v.at[pl.ds(0, CLAT)], lsem.at[6]))
    for load in loads[4:]:
        load.start()

    def copy_to(src, dst, send_sem, recv_sem, ta, tb):
        return pltpu.make_async_remote_copy(
            src_ref=src, dst_ref=dst, send_sem=send_sem, recv_sem=recv_sem, device_id=(ta, tb), device_id_type=MESH
        )

    slot = iota((SLOTS, DEVICES), 0)
    where = jnp.where(slot < counts[...], columns[...], -1)
    place = flip(a, iota((1, DEVICES), 1) // SIDE) % 8
    placed = jnp.where(iota((128, DEVICES), 0) // SLOTS == place, jnp.concatenate([where] * 8, axis=0), 0)
    for h in range(2):
        kbuf[128 * h : 128 * h + 128, :] = placed[:, 128 * h : 128 * h + 128].T

    def prepare(n):
        h = halves[n]
        for q in range(2):
            loads[2 * n + q].wait()
            for s in range(8 * q, 8 * q + 8):
                for c, dst in ((0, f0), (1, f1)):
                    block = w_v[n, s, 128 * c : 128 * c + 128, :]
                    dst[pl.ds(s, 128, stride=SLOTS), :] = block.astype(F32).T
        for r in range(4):
            pieces = [w_v[n, 4 * g + r, 256:288, :] for g in range(4)]
            block = jnp.concatenate([p.astype(F32) for p in pieces], axis=0)
            fr[pl.ds(r, 128, stride=4), :] = block.T

        def pack(i, _):
            first = 128 * h + 8 * i
            rows = pl.ds(pl.multiple_of(128 * i, 128), 128)
            wbuf[pl.ds(first, 8), :, 0:128] = f0[rows, :].astype(BF16).reshape(8, SLOTS, 128)
            wbuf[pl.ds(first, 8), :, 128:256] = f1[rows, :].astype(BF16).reshape(8, SLOTS, 128)
            four = fr[pl.ds(pl.multiple_of(32 * i, 32), 32), :]
            rbuf[pl.ds(first, 8)] = four.reshape(8, 4, 128).astype(BF16)
            return 0

        lax.fori_loop(0, 16, pack, 0, unroll=4)

    def send(lat_off, lon_off):
        ta, tb = flip(a, lat_off), along(b, lon_off)
        d = ta * SIDE + tb
        i = lon_off * SIDE + lat_off
        for n, (src, dst) in enumerate(((wbuf, recv), (rbuf, recr))):
            copy_to(src.at[d], dst.at[i], ssem.at[n], rsem.at[n, lon_off], ta, tb).start()

    def send_lat(lat_off, _):
        send(lat_off, 0)
        return 0

    def send_lon(i, _):
        send(0, jnp.where(i <= 2, i + 1, jnp.where(i == SIDE - 1, 1, 18 - i)))
        return 0

    prepare(0)
    pl.semaphore_wait(bar, 2 * (SIDE - 1))

    for j in FAR_LON:
        pl.semaphore_signal(pair_sem, inc=1, device_id=(a, (b + j) % SIDE), device_id_type=MESH)

    def send_columns(lat_off, _):
        ta = flip(a, lat_off)
        src = kbuf.at[pl.ds(pl.multiple_of(ta * SIDE, SIDE), SIDE)]
        copy_to(src, kin.at[lat_off], ks_sem.at[0], kr_sem.at[0], ta, b).start()
        return 0

    lax.fori_loop(1, SIDE, send_lon, 0)
    lax.fori_loop(1, SIDE, send_columns, 0)
    lax.fori_loop(1, 8, send_lat, 0)
    prepare(1)
    lax.fori_loop(8, SIDE, send_lat, 0)
    own = [
        pltpu.make_async_copy(wbuf.at[me], recv.at[0], rsem.at[0, 0]),
        pltpu.make_async_copy(rbuf.at[me], recr.at[0], rsem.at[1, 0]),
    ]
    for copy in own:
        copy.start()

    def pair_of(t):
        near = 2 * (3 - (t - 1) // 2) + (t - 1) % 2
        return jnp.where(t == 0, 1, jnp.where(t == 7, 0, near))

    def send_pair(t):
        first = 2 * pair_of(t)

        def both(i, _):
            lat_off = SIDE - i

            @pl.when(first > 0)
            def _():
                send(lat_off, first)

            send(lat_off, first + 1)
            return 0

        lax.fori_loop(1, SIDE, both, 0)

    pl.semaphore_wait(pair_sem, SIDE - 1)
    send_pair(0)

    landed = kin.at[pl.ds(1, SIDE - 1)]
    pltpu.make_async_copy(landed, landed, kr_sem.at[0]).wait()
    low = kbuf[pl.ds(pl.multiple_of(a * SIDE, SIDE), SIDE), :]
    high = kin[8]
    for i in range(1, 8):
        low = low + kin[i]
        high = high + kin[8 + i]
    kmid[:, 0, 0:128] = low
    kmid[:, 0, 128:256] = high
    reck[0] = kmid[b]

    def send_rows(lon_off, _):
        tb = along(b, lon_off)
        copy_to(kmid.at[tb], reck.at[lon_off], ks_sem.at[1], kr_sem.at[1], a, tb).start()
        return 0

    lax.fori_loop(1, SIDE, send_rows, 0)
    send_pair(1)

    mat[...] = jnp.zeros_like(mat)
    for t in range(TRACERS):
        mat[LEV * t : LEV * t + LEV, LEV * t : LEV * t + LEV] = mix[...]
    gain = jnp.sum(mat[:, 0:CHAN] * lweights[...].reshape(1, CHAN), axis=1, keepdims=True)
    lane = iota((CHAN, WIDE - CHAN), 1)
    extra = (iota((CHAN, WIDE - CHAN), 0) // LEV == lane % TRACERS) & (lane < TRACERS * SIDE)
    mat[:, CHAN:WIDE] = jnp.where(extra, gain, 0.0)
    mat_hi[...], mat_lo[...] = split(mat[:, 0:256])
    mat_end[:, 0:128], mat_end[:, 128:256] = split(mat[:, 256:WIDE])

    loads[6].wait()
    pick = jnp.where(iota((DEVICES, DEVICES), 0) == owner[...], 1.0, 0.0).astype(BF16)

    def by_owner(piece):
        turned = lax.dot_general(pick, piece, (((1,), (1,)), ((), ())), preferred_element_type=F32)
        return turned.astype(BF16)

    for c in range(CLAT // BAND):
        high, low = split(basis_v[BAND * c : BAND * c + BAND].reshape(BAND * CLON, DEVICES))
        base_hi[:, BAND * CLON * c : BAND * CLON * (c + 1)] = by_owner(high)
        base_lo[:, BAND * CLON * c : BAND * CLON * (c + 1)] = by_owner(low)

    loads[4].wait()
    loads[5].wait()

    for n, x in enumerate((CLON - 1, 0)):
        winds_col[n] = winds_v[0:CLAT, x, 0:LEV]
        basis_col[n] = basis_v[0:CLAT, x, :]
    lon_near = []
    lat_near = []
    for n, (r, tb, ta) in enumerate((
        (CLAT - 1, (b + 1) % SIDE, (a + 1) % SIDE),
        (0, (b + SIDE - 1) % SIDE, (a + SIDE - 1) % SIDE),
    )):
        for k, (col, row, col_in_, row_in_) in enumerate((
            (winds_col, winds_v, near_winds_col, near_winds_row),
            (basis_col, basis_v, near_basis_col, near_basis_row),
        )):
            lon_near.append(copy_to(col.at[n], col_in_.at[n], ns_sem.at[k, n], nr_sem.at[k, n], a, tb))
            lat_near.append((n, copy_to(row.at[r], row_in_.at[n], ns_sem.at[k, 2 + n], nr_sem.at[k, 2 + n], ta, b)))
    for copy in lon_near:
        copy.start()
    first_band, last_band = a == 0, a == SIDE - 1
    for n, copy in lat_near:
        @pl.when(jnp.logical_not(last_band if n == 0 else first_band))
        def _():
            copy.start()

    for n, none in ((0, first_band), (1, last_band)):
        @pl.when(none)
        def _():
            near_winds_row[n] = jnp.zeros((CLON, 2 * LEV), F32)
            near_basis_row[n] = jnp.zeros((CLON, DEVICES), F32)
            row_in[0, n] = jnp.zeros((CLON, WIDE), F32)
            row_in[1, n] = jnp.zeros((CLON, WIDE), F32)

    def clear(r, _):
        cur[r] = jnp.zeros((64, WIDE), F32)
        nxt[r] = jnp.zeros((64, WIDE), F32)
        return 0

    lax.fori_loop(0, CLAT + 2, clear, 0)

    def begin(r, _):
        cur[r + 1, 8:56, 0:CHAN] = adj_v[r]
        return 0

    lax.fori_loop(0, CLAT, begin, 0)

    def coefficients(r):
        both = winds_v[r]
        u = jnp.concatenate([both[:, 0:LEV]] * TRACERS, axis=1)
        v = jnp.concatenate([both[:, LEV : 2 * LEV]] * TRACERS, axis=1)
        east = jnp.maximum(u, 0.0) + diffusion
        west = jnp.maximum(-u, 0.0) + diffusion
        north = jnp.maximum(v, 0.0) + diffusion
        south = jnp.maximum(-v, 0.0) + diffusion
        coef[0, r] = 1.0 - ((east + west) + (north + south))
        coef[1, r] = east
        coef[2, r] = west
        coef[3, r] = north
        coef[4, r] = south

    rows = iota((DEVICES, 64), 0)
    lanes = iota((DEVICES, 64), 1)
    spread = jnp.where((rows // 16 == lanes // 4) & (rows % 4 == lanes % 4), 1.0, 0.0).astype(BF16)
    rows = iota((DEVICES, 128), 0)
    lanes = iota((DEVICES, 128), 1)
    keep = jnp.where((rows // 4) % 4 == lanes // 32, 1.0, 0.0)
    rows = iota((128, 128), 0)
    lanes = iota((128, 128), 1)
    fold = jnp.where(rows % 32 == lanes, 1.0, 0.0).astype(BF16)

    def absorb(g):
        first = g * SIDE
        for n, buf in enumerate((recv, recr)):
            piece = buf.at[pl.ds(first, SIDE)]
            pltpu.make_async_copy(piece, piece, rsem.at[n, g]).wait()
        rhs[:, 0:256] = recv[pl.ds(first, SIDE)].reshape(256, 256)
        for m in range(SIDE):
            stage[4 * m : 4 * m + 4, :] = recr[first + m].astype(F32)
        wide = (dot(spread, stage[0:64, :].astype(BF16)) * keep).astype(BF16)
        rhs[:, 256:384] = dot(wide, fold).astype(BF16)
        spot = reck[g]
        for c in range(CLAT // BAND):
            ids = iota((BAND * CLON, 256), 0) + c * BAND * CLON
            table = jnp.where(ids == spot, 1.0, 0.0).astype(BF16)
            cur[c * BAND + 1 : (c + 1) * BAND + 1, 8:56, :] += dot(table, rhs[...]).reshape(BAND, CLON, WIDE)

    coming = reck.at[pl.ds(1, SIDE - 1)]
    pltpu.make_async_copy(coming, coming, kr_sem.at[1]).wait()

    def turn(t, _):
        @pl.when(t < 8)
        def _():
            send_pair(t)

        @pl.when(t < 8)
        def _():
            for i in range(4):
                coefficients(4 * (t - 2) + i)

        first = 2 * pair_of(t - LAG)
        absorb(first)
        absorb(first + 1)
        return 0

    lax.fori_loop(LAG, 8, turn, 0)
    for k in range(5):
        coef_rim[k, 0:CLAT, :] = coef[k, 0:CLAT, 0, :]
        coef_rim[k, CLAT : 2 * CLAT, :] = coef[k, 0:CLAT, CLON - 1, :]

    for copy in lon_near:
        copy.wait_recv()
    for n, copy in lat_near:
        @pl.when(jnp.logical_not(first_band if n == 0 else last_band))
        def _():
            copy.wait_recv()

    def inflow(wind):
        return jnp.concatenate([jnp.maximum(wind, 0.0) + diffusion] * TRACERS, axis=1)

    ring_coef[0:CLAT, :] = inflow(near_winds_col[0])
    ring_coef[CLAT : 2 * CLAT, :] = inflow(-near_winds_col[1])
    ring_coef[2 * CLAT : 2 * CLAT + CLON, :] = inflow(near_winds_row[0][:, LEV : 2 * LEV])
    ring_coef[2 * CLAT + CLON : RIM, :] = inflow(-near_winds_row[1][:, LEV : 2 * LEV])
    ring_basis = jnp.concatenate([near_basis_col[0], near_basis_col[1], near_basis_row[0], near_basis_row[1]], axis=0)
    high, low = split(ring_basis)
    ring_hi[...] = by_owner(high)
    ring_lo[...] = by_owner(low)

    absorb(0)
    last = 2 * pair_of(6)

    def last_turns(g, _):
        absorb(jnp.where(g == 2, 1, last + g))
        return 0

    lax.fori_loop(0, 3, last_turns, 0)

    def halo(buf, e, columns):
        north = copy_to(buf.at[CLAT, 8:56, :], row_in.at[e, 0], hs_sem.at[e, 0], hr_sem.at[e, 0], (a + 1) % SIDE, b)
        south = copy_to(buf.at[1, 8:56, :], row_in.at[e, 1], hs_sem.at[e, 1], hr_sem.at[e, 1], (a + SIDE - 1) % SIDE, b)
        east = copy_to(col_out.at[e, 0], col_in.at[e, 0], hs_sem.at[e, 2], hr_sem.at[e, 2], a, (b + 1) % SIDE)
        west = copy_to(col_out.at[e, 1], col_in.at[e, 1], hs_sem.at[e, 3], hr_sem.at[e, 3], a, (b + SIDE - 1) % SIDE)

        @pl.when(a < SIDE - 1)
        def _():
            north.start()

        @pl.when(a > 0)
        def _():
            south.start()

        columns()
        east.start()
        west.start()
        return north, south, east, west

    def arrive(copies):
        north, south, east, west = copies

        @pl.when(a > 0)
        def _():
            north.wait_recv()

        @pl.when(a < SIDE - 1)
        def _():
            south.wait_recv()

        east.wait_recv()
        west.wait_recv()

    def finish(copies):
        north, south, east, west = copies

        @pl.when(a < SIDE - 1)
        def _():
            north.wait_send()

        @pl.when(a > 0)
        def _():
            south.wait_send()

        east.wait_send()
        west.wait_send()

    def blend(weights, values):
        m = weights[0] * values[0]
        for k in range(1, 5):
            m = m + weights[k] * values[k]
        return m

    def mixed(high, low):
        return dot(high, mat_hi[...]) + dot(low, mat_hi[...]) + dot(high, mat_lo[...])

    def mixed_end(high, low, start=0):
        both = dot(high[:, start:], mat_end[start:, :])
        return both[:, 0:128] + both[:, 128:256] + dot(low[:, start:], mat_end[start:, 0:128])

    def span_of(c):
        return pl.ds(pl.multiple_of(c * ROWS * CLON, 16), ROWS * CLON)

    def inner(buf, c):
        for k in range(ROWS):
            r = 1 + c * ROWS + k
            m = blend(
                [coef[n, r] for n in range(5)],
                [buf[r + 1, 8:56, 0:CHAN], buf[r + 1, 9:57, 0:CHAN], buf[r + 1, 7:55, 0:CHAN],
                 buf[r + 2, 8:56, 0:CHAN], buf[r, 8:56, 0:CHAN]],
            )
            rows = pl.ds(pl.multiple_of((c * ROWS + k) * CLON, 16), CLON)
            mh[rows, :], ml[rows, :] = split(m)
        return mh[span_of(c), :], ml[span_of(c), :]

    def rim_inside(buf):
        for n, x in enumerate((8, 55)):
            span = slice(n * CLAT, (n + 1) * CLAT)
            rim[span, :] = blend(
                [coef_rim[k, span, :] for k in range(5)],
                [buf[1 : CLAT + 1, x, 0:CHAN], buf[1 : CLAT + 1, x + 1, 0:CHAN], buf[1 : CLAT + 1, x - 1, 0:CHAN],
                 buf[2 : CLAT + 2, x, 0:CHAN], buf[0:CLAT, x, 0:CHAN]],
            )
        for n, r in enumerate((0, CLAT - 1)):
            rim[2 * CLAT + n * CLON : 2 * CLAT + (n + 1) * CLON, :] = blend(
                [coef[k, r] for k in range(5)],
                [buf[r + 1, 8:56, 0:CHAN], buf[r + 1, 9:57, 0:CHAN], buf[r + 1, 7:55, 0:CHAN],
                 buf[r + 2, 8:56, 0:CHAN], buf[r, 8:56, 0:CHAN]],
            )

        for r, k, edge in ((0, 4, first_band), (CLAT - 1, 3, last_band)):
            @pl.when(edge)
            def _():
                n = min(r, 1)
                rim[2 * CLAT + n * CLON : 2 * CLAT + (n + 1) * CLON, :] += coef[k, r] * buf[r + 1, 8:56, 0:CHAN]
                for i, x in ((r, 8), (CLAT + r, 55)):
                    rim[i : i + 1, :] += coef_rim[k, i : i + 1, :] * buf[r + 1, x : x + 1, 0:CHAN]

    def rim_beyond(e):
        rim[0:CLAT, :] += coef_rim[2, 0:CLAT, :] * col_in[e, 0, :, 0:CHAN]
        rim[CLAT : 2 * CLAT, :] += coef_rim[1, CLAT : 2 * CLAT, :] * col_in[e, 1, :, 0:CHAN]
        for n, r, k in ((0, 0, 4), (1, CLAT - 1, 3)):
            rim[2 * CLAT + n * CLON : 2 * CLAT + (n + 1) * CLON, :] += coef[k, r] * row_in[e, n, :, 0:CHAN]
            for i, x in ((r, 0), (CLAT + r, CLON - 1)):
                rim[i : i + 1, :] += coef_rim[k, i : i + 1, :] * row_in[e, n, x : x + 1, 0:CHAN]
        parts = split(rim[0:RIM, :])
        return (slice(0, 256), mixed(*parts)), (slice(256, CHAN), mixed_end(*parts, 128)[:, 0 : CHAN - 256])

    def first_columns():
        col_out[0, 0, :, 0:CHAN] = cur[1 : CLAT + 1, 55, 0:CHAN]
        col_out[0, 1, :, 0:CHAN] = cur[1 : CLAT + 1, 8, 0:CHAN]

    one = halo(cur, 0, first_columns)

    def inner_one(c, _):
        high, low = inner(cur, c)
        rows = pl.ds(c * ROWS + 2, ROWS)
        nxt[rows, 8:56, 0:256] = mixed(high, low).reshape(ROWS, CLON, 256)
        end = mixed_end(high, low, 128)[:, 0 : CHAN - 256]
        nxt[rows, 8:56, 256:CHAN] = end.reshape(ROWS, CLON, CHAN - 256)
        return 0

    lax.fori_loop(0, 2, inner_one, 0)
    rim_inside(cur)
    arrive(one)
    for lanes, res in rim_beyond(0):
        nxt[1, 8:56, lanes] = res[2 * CLAT : 2 * CLAT + CLON]
        nxt[CLAT, 8:56, lanes] = res[2 * CLAT + CLON : RIM]
        nxt[1 : CLAT + 1, 8, lanes] = res[0:CLAT]
        nxt[1 : CLAT + 1, 55, lanes] = res[CLAT : 2 * CLAT]
        col_out[1, 0, :, lanes] = res[CLAT : 2 * CLAT]
        col_out[1, 1, :, lanes] = res[0:CLAT]
    two = halo(nxt, 1, lambda: None)

    def inner_sens(c, _):
        end = mixed_end(*inner(nxt, c)).reshape(ROWS, CLON, 128)
        sens[pl.ds(c * ROWS + 1, ROWS)] = end
        out_v[pl.ds(c * ROWS + 1, ROWS), :, 256:CHAN] = end[:, :, 0 : CHAN - 256]
        return 0

    lax.fori_loop(0, 2, inner_sens, 0)

    rim_inside(nxt)
    rim[RIM : RIM + CLAT, :] = ring_coef[0:CLAT, :] * nxt[1 : CLAT + 1, 8, 0:CHAN]
    rim[RIM + CLAT : RIM + 2 * CLAT, :] = ring_coef[CLAT : 2 * CLAT, :] * nxt[1 : CLAT + 1, 55, 0:CHAN]
    rim[RIM + 2 * CLAT : RIM + 2 * CLAT + CLON, :] = ring_coef[2 * CLAT : 2 * CLAT + CLON, :] * nxt[1, 8:56, 0:CHAN]
    rim[RIM + 2 * CLAT + CLON : 2 * RIM, :] = ring_coef[2 * CLAT + CLON : RIM, :] * nxt[CLAT, 8:56, 0:CHAN]
    ends = mixed_end(*split(rim[2 * CLAT : 2 * RIM, :]))
    sens[0] = ends[0:CLON]
    sens[CLAT - 1] = ends[CLON : 2 * CLON]
    beyond_hi, beyond_lo = split(ends[2 * CLON :])

    sens_hi, sens_lo = split(sens[0:CLAT].reshape(CELLS, 128))
    both = dot(base_hi[...], jnp.concatenate([sens_hi, sens_lo], axis=1))
    both = both + dot(ring_hi[...], jnp.concatenate([beyond_hi, beyond_lo], axis=1))
    part = both[:, 0:128] + both[:, 128:256] + (dot(base_lo[...], sens_hi) + dot(ring_lo[...], beyond_hi))
    rows = iota((DEVICES, 128), 0)
    lanes = iota((DEVICES, 128), 1)
    part = jnp.where((lanes // TRACERS == rows % SIDE + 8) & (lanes >= 32), part, 0.0)
    gsend[:, 0, :] = jnp.sum(part.reshape(SIDE, SIDE, 128), axis=1)

    for i in FAR_LAT:
        ta = (a + i) % SIDE
        copy_to(gsend.at[ta], gin.at[i], gs_sem.at[0], gr_sem.at[0], ta, b).start()

    def inner_state(c, _):
        res = mixed(mh[span_of(c), :], ml[span_of(c), :])
        out_v[pl.ds(c * ROWS + 1, ROWS), :, 0:256] = res.reshape(ROWS, CLON, 256)
        return 0

    lax.fori_loop(0, 2, inner_state, 0)
    arrive(two)
    for lanes, res in rim_beyond(1):
        out_v[0, :, lanes] = res[2 * CLAT : 2 * CLAT + CLON]
        out_v[CLAT - 1, :, lanes] = res[2 * CLAT + CLON : RIM]
        out_v[0:CLAT, 0, lanes] = res[0:CLAT]
        out_v[0:CLAT, CLON - 1, lanes] = res[CLAT : 2 * CLAT]
    leave = pltpu.make_async_copy(out_v.at[pl.ds(0, CLAT)], out, out_sem.at[0])
    leave.start()
    got = gsend[a]
    lat_in = gin.at[pl.ds(1, SIDE - 1)]
    pltpu.make_async_copy(lat_in, lat_in, gr_sem.at[0]).wait()
    for i in range(1, SIDE):
        got = got + gin[i]
    grow[...] = got

    for j in FAR_LON:
        copy_to(grow, gfin.at[j], gs_sem.at[1], gr_sem.at[1], a, (b + j) % SIDE).start()
    lon_in = gfin.at[pl.ds(1, SIDE - 1)]
    pltpu.make_async_copy(lon_in, lon_in, gr_sem.at[1]).wait()
    for i in range(1, SIDE):
        got = got + gfin[i]
    lanes = iota((1, 128), 1)
    owned = jnp.zeros((1, TRACERS), F32)
    for t in range(TRACERS):
        value = jnp.sum(jnp.where(lanes == 32 + TRACERS * b + t, got, 0.0), axis=1, keepdims=True)
        owned = jnp.where(iota((1, TRACERS), 1) == t, value, owned)
    owned = owned * (1.0 / jnp.sqrt(jnp.full((1, TRACERS), CELLS * DEVICES, F32)))
    grad[...] = owned.reshape(1, 1, TRACERS)

    finish(one)
    finish(two)
    for copy in lon_near:
        copy.wait_send()
    for n, copy in lat_near:
        @pl.when(jnp.logical_not(last_band if n == 0 else first_band))
        def _():
            copy.wait_send()

    leave.wait()
    for piece, sem in ((landed, ks_sem.at[0]), (coming, ks_sem.at[1]), (lat_in, gs_sem.at[0]), (lon_in, gs_sem.at[1])):
        pltpu.make_async_copy(piece, piece, sem).wait()
    for n, buf in enumerate((recv, recr)):
        piece = buf.at[pl.ds(1, DEVICES - 1)]
        pltpu.make_async_copy(piece, piece, ssem.at[n]).wait()


def deliver_kernel(state, grad, state_out, grad_out, held, small, sems):
    parts = 4
    rows = CLAT // parts
    reads = [pltpu.make_async_copy(grad, small, sems.at[0, parts])]
    writes = [pltpu.make_async_copy(small, grad_out, sems.at[1, parts])]
    for i in range(parts):
        span = pl.ds(i * rows, rows)
        reads.append(pltpu.make_async_copy(state.at[span], held.at[span], sems.at[0, i]))
        writes.append(pltpu.make_async_copy(held.at[span], state_out.at[span], sems.at[1, i]))
    for read in reads:
        read.start()
    for read, write in zip(reads, writes):
        read.wait()
        write.start()
    for write in writes:
        write.wait()


def body(
    adjoint_in, winds, vert_mix, level_weights, snd_weights, snd_columns, snd_counts, basis, owner
):
    anywhere = pl.BlockSpec(memory_space=pl.ANY)
    vmem = pl.BlockSpec(memory_space=pltpu.VMEM)
    state, grad = pl.pallas_call(
        window_kernel,
        out_shape=(
            jax.ShapeDtypeStruct((CLAT, CLON, CHAN), F32),
            jax.ShapeDtypeStruct((1, 1, TRACERS), F32),
        ),
        in_specs=[anywhere, anywhere, vmem, vmem, anywhere, vmem, vmem, anywhere, vmem],
        out_specs=(anywhere, vmem),
        scratch_shapes=[
            pltpu.VMEM((2, SLOTS, CHAN, 128), BF16),
            pltpu.VMEM((129 * SLOTS, 128), F32),
            pltpu.VMEM((129 * SLOTS, 128), F32),
            pltpu.VMEM((130 * 4, 128), F32),
            pltpu.VMEM((DEVICES, SLOTS, 256), BF16),
            pltpu.VMEM((DEVICES, 4, 128), BF16),
            pltpu.VMEM((DEVICES, 128), jnp.int32),
            pltpu.VMEM((SIDE, SIDE, 128), jnp.int32),
            pltpu.VMEM((SIDE, 1, 256), jnp.int32),
            pltpu.VMEM((DEVICES, SLOTS, 256), BF16),
            pltpu.VMEM((DEVICES, 4, 128), BF16),
            pltpu.VMEM((SIDE, 1, 256), jnp.int32),
            pltpu.VMEM((72, 128), F32),
            pltpu.VMEM((256, WIDE), BF16),
            pltpu.VMEM((CLAT, CLON, CHAN), F32),
            pltpu.VMEM((CLAT + 1, CLON, 2 * LEV), F32),
            pltpu.VMEM((5, CLAT + 1, CLON, CHAN), F32),
            pltpu.VMEM((5, 2 * CLAT, CHAN), F32),
            pltpu.VMEM((CLAT + 1, CLON, DEVICES), F32),
            pltpu.VMEM((DEVICES, CELLS), BF16),
            pltpu.VMEM((DEVICES, CELLS), BF16),
            pltpu.VMEM((CHAN, WIDE), F32),
            pltpu.VMEM((CHAN, 256), BF16),
            pltpu.VMEM((CHAN, 256), BF16),
            pltpu.VMEM((CHAN, 256), BF16),
            pltpu.VMEM((CLAT + 2, 64, WIDE), F32),
            pltpu.VMEM((CLAT + 2, 64, WIDE), F32),
            pltpu.VMEM((2, 2, CLAT, WIDE), F32),
            pltpu.VMEM((2, 2, CLAT, WIDE), F32),
            pltpu.VMEM((3, 2, CLON, WIDE), F32),
            pltpu.VMEM((2 * ROWS * CLON, CHAN), BF16),
            pltpu.VMEM((2 * ROWS * CLON, CHAN), BF16),
            pltpu.VMEM((2 * RIM, CHAN), F32),
            pltpu.VMEM((RIM, CHAN), F32),
            pltpu.VMEM((DEVICES, RIM), BF16),
            pltpu.VMEM((DEVICES, RIM), BF16),
            pltpu.VMEM((CLAT + 1, CLON, CHAN), F32),
            pltpu.VMEM((CLAT + 1, CLON, 128), F32),
            pltpu.VMEM((SIDE, 1, 128), F32),
            pltpu.VMEM((SIDE, 1, 128), F32),
            pltpu.VMEM((1, 128), F32),
            pltpu.VMEM((SIDE, 1, 128), F32),
            pltpu.VMEM((2, CLAT, LEV), F32),
            pltpu.VMEM((2, CLAT, DEVICES), F32),
            pltpu.VMEM((2, CLAT, LEV), F32),
            pltpu.VMEM((2, CLAT, DEVICES), F32),
            pltpu.VMEM((2, CLON, 2 * LEV), F32),
            pltpu.VMEM((2, CLON, DEVICES), F32),
            pltpu.SemaphoreType.REGULAR,
            pltpu.SemaphoreType.DMA((2, 4)),
            pltpu.SemaphoreType.DMA((2, 4)),
            pltpu.SemaphoreType.DMA((2,)),
            pltpu.SemaphoreType.DMA((2, SIDE)),
            pltpu.SemaphoreType.DMA((7,)),
            pltpu.SemaphoreType.DMA((2,)),
            pltpu.SemaphoreType.DMA((2,)),
            pltpu.SemaphoreType.DMA((2, 4)),
            pltpu.SemaphoreType.DMA((2, 4)),
            pltpu.SemaphoreType.DMA((2,)),
            pltpu.SemaphoreType.DMA((2,)),
            pltpu.SemaphoreType.DMA((1,)),
        ],
        compiler_params=pltpu.CompilerParams(
            collective_id=0, has_side_effects=True, vmem_limit_bytes=56 << 20
        ),
        name="window",
    )(
        adjoint_in,
        winds,
        vert_mix,
        level_weights,
        jnp.transpose(snd_weights[0, 0], (1, 2, 0)),
        jnp.transpose(snd_columns[0, 0], (1, 0)),
        snd_counts[0],
        basis,
        owner.reshape(1, DEVICES),
    )
    return pl.pallas_call(
        deliver_kernel,
        out_shape=(
            jax.ShapeDtypeStruct((CLAT, CLON, CHAN), F32),
            jax.ShapeDtypeStruct((1, 1, TRACERS), F32),
        ),
        in_specs=[anywhere, anywhere],
        out_specs=(anywhere, anywhere),
        scratch_shapes=[
            pltpu.VMEM((CLAT, CLON, CHAN), F32),
            pltpu.VMEM((1, 1, TRACERS), F32),
            pltpu.SemaphoreType.DMA((2, 5)),
        ],
        compiler_params=pltpu.CompilerParams(vmem_limit_bytes=56 << 20),
        name="deliver",
    )(state, grad)


def solution(mesh):
    return jax.shard_map(
        body,
        mesh=mesh,
        in_specs=(
            P("lat", "lon", None),
            P("lat", "lon", None),
            P(),
            P(),
            P("lat", "lon", None, None, None),
            P("lat", "lon", None, None),
            P("lat", "lon", None),
            P("lat", "lon", None),
            P(),
        ),
        out_specs=(P("lat", "lon", None), P(("lat", "lon"), None, None)),
        check_vma=False,
    )
```
